32 devices in a mesh: seq: 16 (over z, y, x), ch: 2 (over core).
Axes of the slice: x: 2, y: 2, z: 4, core: 2. Of those that a mesh axis runs over, the one named last changes fastest.
Arguments:
- signal: bfloat16 [256, 8192], P('ch', 'seq'), may hold values from -6 to 6
- in_gate: bfloat16 [256, 8192], P('ch', 'seq'), may hold values from -6 to 6
- out_gate: bfloat16 [256, 8192], P('ch', 'seq'), may hold values from -6 to 6
- short_taps: float32 [256, 128], P('ch'), may hold values from -0.5 to 0.5
- skip_gain: float32 [256], P('ch'), may hold values from 0.5 to 1.5
- decay_rate: float32 [256], P('ch'), may hold values from 0.00037475585 to 0.0018737793
- embed_weight: float32 [33, 64], replicated, may hold values from -1 to 1
- embed_bias: float32 [64], replicated, may hold values from -3.140625 to 3.140625
- sine_freq: float32 [64], replicated, may hold values from 1 to 10
- mid_weight: float32 [64, 64], replicated, may hold values from -0.75 to 0.75
- mid_bias: float32 [64], replicated, may hold values from -3.140625 to 3.140625
- out_weight: float32 [64, 256], P(None, 'ch'), may hold values from -0.75 to 0.75
Outputs:
- mixed: bfloat16 [256, 8192], P('ch', 'seq')
The draws below stay inside these ranges and needn't reach their ends.
All inputs are finite; a program needn't handle non-finite values.
Results may differ from the reference program's by a relative error of at most 0.001.
Values may be sent and summed in bfloat16 or wider, within the bound.
No kernel may reach another device: no remote copies, remote signals or barrier semaphores. Data moves between devices by JAX's collectives and lax.ppermute only.
A program may use at most 128 MiB of HBM per device.

```python
import math
import jax
import jax.numpy as jnp
from jax import lax

C = 256
F = 64
BANDS = 16
TAPS = 128
L = 8192
EMBED = 33


def block_scale(key, shape, cuts, least, high):
    def one(axis_at, blocks):
        draws = jax.random.uniform(jax.random.fold_in(jax.random.fold_in(key, 6), axis_at), (blocks,), jnp.float32, least / len(cuts), high / len(cuts))
        return jnp.repeat(jnp.exp(draws), shape[axis_at] // blocks).reshape((-1,) + (1,) * (len(shape) - axis_at - 1))

    level = one(*cuts[0])
    for cut in cuts[1:]:
        level = level * one(*cut)
    return level


def centred(stream_key, shape, width, limit, cuts=(), held_as=jnp.bfloat16):
    factor_of = block_scale(stream_key, shape, cuts, -0.22, 0.18) if cuts else 1.0
    array = jax.random.normal(stream_key, shape, jnp.float32) * width * factor_of
    return jnp.minimum(jnp.maximum(array, -limit), limit).astype(held_as)


def setup_inputs(seed: int = 0) -> dict:
    splits = jax.random.split(jax.random.key(seed), 13)
    return {
        "signal": centred(splits[0], (C, L), 1.0, 6.0, ((0, 2), (1, 16))),
        "in_gate": centred(splits[1], (C, L), 1.0, 6.0, ((0, 2), (1, 16))),
        "out_gate": centred(splits[2], (C, L), 1.0, 6.0, ((0, 2), (1, 16))),
        "short_taps": centred(splits[3], (C, TAPS), TAPS ** -0.5, 0.5, ((0, 2),), jnp.float32),
        "skip_gain": jnp.clip(0.5 + 1.0 * jax.random.uniform(splits[4], (C,), jnp.float32) ** block_scale(splits[4], (C,), ((0, 2),), -0.2, 0.2), 0.5, 1.5),
        "decay_rate": jnp.clip(jnp.exp(math.log(0.0018737793) - 1.609438 * jax.random.uniform(splits[5], (C,), jnp.float32) ** block_scale(splits[5], (C,), ((0, 2),), -0.2, 0.2)), 0.00037475585, 0.0018737793),
        "embed_weight": centred(splits[6], (EMBED, F), EMBED ** -0.5, 1.0, (), jnp.float32),
        "embed_bias": jnp.clip(jax.random.uniform(splits[7], (F,), jnp.float32, -3.140625, 3.140625), -3.140625, 3.140625),
        "sine_freq": jnp.clip(jnp.exp(jax.random.uniform(splits[8], (F,), jnp.float32, math.log(1.0), math.log(10.0))), 1.0, 10.0),
        "mid_weight": centred(splits[9], (F, F), F ** -0.5, 0.75, (), jnp.float32),
        "mid_bias": jnp.clip(jax.random.uniform(splits[10], (F,), jnp.float32, -3.140625, 3.140625), -3.140625, 3.140625),
        "out_weight": centred(splits[11], (F, C), F ** -0.5, 0.75, ((1, 2),), jnp.float32),
    }


def embed_rows(positions, full_len):
    phase = positions % full_len
    columns = [positions.astype(jnp.float32) / full_len]
    for band in range(BANDS):
        angle = phase.astype(jnp.float32) * (2.0 * math.pi / full_len)
        columns.append(jnp.cos(angle))
        columns.append(jnp.sin(angle))
        phase = 2 * phase % full_len
    return jnp.stack(columns, axis=1)

def filter_hidden(positions, full_len, embed_weight, embed_bias, sine_freq, mid_weight, mid_bias):
    embedding = embed_rows(positions, full_len)
    first = jnp.sin(sine_freq * (jnp.dot(embedding, embed_weight, precision=lax.Precision.HIGHEST, preferred_element_type=jnp.float32) + embed_bias))
    return jnp.sin(sine_freq * (jnp.dot(first, mid_weight, precision=lax.Precision.HIGHEST, preferred_element_type=jnp.float32) + mid_bias))

def shape_filter(second, positions, out_weight, decay_rate):
    raw_vals = jnp.dot(second, out_weight, precision=lax.Precision.HIGHEST, preferred_element_type=jnp.float32).T
    return raw_vals * (jnp.sqrt(2.0 * decay_rate)[:, None] * jnp.exp(-decay_rate[:, None] * positions.astype(jnp.float32)[None, :]))

def reference(signal, in_gate, out_gate, short_taps, skip_gain, decay_rate, embed_weight, embed_bias, sine_freq, mid_weight, mid_bias, out_weight):
    channels, full_len = signal.shape
    tap_count = short_taps.shape[1]
    values = signal.astype(jnp.float32)
    padded = jnp.pad(values, ((0, 0), (tap_count - 1, 0)))
    short_out = jnp.zeros_like(values)
    for lag in range(tap_count):
        begin = tap_count - 1 - lag
        short_out = short_out + short_taps[:, lag:lag + 1] * padded[:, begin:begin + full_len]
    gated_in = in_gate.astype(jnp.float32) * short_out
    positions = jnp.arange(full_len, dtype=jnp.int32)
    second = filter_hidden(positions, full_len, embed_weight, embed_bias, sine_freq, mid_weight, mid_bias)
    filter_vals = shape_filter(second, positions, out_weight, decay_rate)
    fft_len = 2 * full_len
    spectrum = jnp.fft.rfft(gated_in, n=fft_len, axis=1) * jnp.fft.rfft(filter_vals, n=fft_len, axis=1)
    conv = jnp.fft.irfft(spectrum, n=fft_len, axis=1)[:, :full_len]
    return (out_gate.astype(jnp.float32) * (conv + skip_gain[:, None] * gated_in)).astype(jnp.bfloat16)
```

```python
import functools
import math

import jax
import jax.numpy as jnp
import numpy as np
from jax import lax
from jax.experimental import pallas as pl
from jax.experimental.pallas import tpu as pltpu
from jax.sharding import PartitionSpec as P

BANDS = 16
LANES = 128
TILE = 1024
F32 = jnp.float32
BF16 = jnp.bfloat16


def round_up(count, step):
    return (count + step - 1) // step * step


def halves(table):
    high = table.astype(BF16)
    low = (table - high.astype(np.float64)).astype(BF16)
    return high, low


@functools.lru_cache(maxsize=None)
def embed_table(full_len):
    positions = np.arange(full_len, dtype=np.int64)
    rows = [positions / full_len]
    phase = positions
    for _ in range(BANDS):
        angle = phase * (2.0 * math.pi / full_len)
        rows += [np.cos(angle), np.sin(angle)]
        phase = 2 * phase % full_len
    table = np.zeros((round_up(len(rows), 8), full_len), np.float32)
    table[: len(rows)] = np.stack(rows)
    return table


@functools.lru_cache(maxsize=None)
def transform_tables(full_len):
    blocks = full_len // LANES
    a = np.arange(blocks)
    k1 = np.arange(blocks)
    b = np.arange(LANES)
    theta = 2.0 * math.pi / blocks * ((4 * k1 + 1)[:, None] * a[None, :] % (4 * blocks)) / 4.0
    phi = 2.0 * math.pi / full_len * ((4 * k1 + 1)[:, None] * b[None, :]) / 4.0
    psi = 2.0 * math.pi / LANES * (b[:, None] * b[None, :] % LANES)
    outer_high, outer_low = halves(np.concatenate([np.cos(theta), -np.sin(theta)], axis=0))
    outer = np.concatenate([outer_high, outer_high, outer_low], axis=1)
    back = np.concatenate([np.cos(theta).T, -np.sin(theta).T], axis=1) / full_len
    back_high, back_low = halves(back)
    outer_back = np.concatenate([back_high, back_high, back_low], axis=1)
    twiddle = np.stack([np.cos(phi), np.sin(phi)]).astype(np.float32)
    cos_in, sin_in = np.cos(psi), np.sin(psi)
    inner = np.stack(halves(np.block([[cos_in, -sin_in], [sin_in, cos_in]])))
    inner_back = np.stack(halves(np.block([[cos_in, sin_in], [-sin_in, cos_in]])))
    return outer, twiddle, inner, inner_back, outer_back


def sine_constants():
    nodes = np.cos((np.arange(400) + 0.5) * math.pi / 400) * (math.pi / 2)
    squares = nodes * nodes
    basis = np.stack([squares**p for p in range(6)], axis=1)
    fit = np.linalg.lstsq(basis, np.sin(nodes) / nodes, rcond=None)[0]
    first = np.floor(math.pi * 2.0**13) / 2.0**13
    second = np.floor((math.pi - first) * 2.0**28) / 2.0**28
    return [float(v) for v in fit], (float(first), float(second), math.pi - first - second)


SINE_FIT, PI_PARTS = sine_constants()


def sine(angle):
    turns = jnp.round(angle * (1.0 / math.pi))
    rest = angle
    for part in PI_PARTS:
        rest = rest - turns * part
    half = turns * 0.5
    odd = half - jnp.floor(half)
    square = rest * rest
    value = SINE_FIT[5]
    for term in SINE_FIT[4::-1]:
        value = value * square + term
    return value * (rest - rest * (4.0 * odd))


def split_two(vals):
    high = vals.astype(BF16)
    return high, (vals - high.astype(F32)).astype(BF16)


def split_three(vals):
    first = vals.astype(BF16).astype(F32)
    rest = vals - first
    second = rest.astype(BF16).astype(F32)
    return first, second, rest - second


def matmul(lhs, rhs):
    return jnp.dot(lhs, rhs, preferred_element_type=F32)


def six_left(vals):
    one, two, three = split_three(vals)
    return jnp.concatenate([one, one, two, one, three, two], axis=0)


def six_right(vals):
    one, two, three = split_three(vals)
    return jnp.concatenate([one, two, one, three, one, two], axis=0).astype(BF16)


def stack_three(vals):
    high, low = split_two(vals)
    return jnp.concatenate([high, low, high], axis=0)


def inner_product(vals, table_ref):
    high, low = split_two(vals)
    return (
        matmul(high, table_ref[0]) + matmul(low, table_ref[0]) + matmul(high, table_ref[1])
    )


def forward(columns, outer_ref, twiddle_ref, inner_ref):
    blocks = columns[0].shape[0]
    mixed = matmul(outer_ref[...], stack_three(jnp.concatenate(columns, axis=1)))
    cos_vals, sin_vals = twiddle_ref[0], twiddle_ref[1]
    rows = []
    for c in range(len(columns)):
        real = mixed[:blocks, c * LANES : (c + 1) * LANES]
        imag = mixed[blocks:, c * LANES : (c + 1) * LANES]
        rows.append(
            jnp.concatenate(
                [real * cos_vals + imag * sin_vals, imag * cos_vals - real * sin_vals], axis=1
            )
        )
    return inner_product(jnp.concatenate(rows, axis=0), inner_ref)


def backward(spectrum, channels, inner_back_ref, twiddle_ref, outer_back_ref):
    vals = inner_product(spectrum, inner_back_ref)
    blocks = vals.shape[0] // channels
    cos_vals, sin_vals = twiddle_ref[0], twiddle_ref[1]
    columns = []
    for c in range(channels):
        real = vals[c * blocks : (c + 1) * blocks, :LANES]
        imag = vals[c * blocks : (c + 1) * blocks, LANES:]
        columns.append(
            jnp.concatenate(
                [real * cos_vals - imag * sin_vals, imag * cos_vals + real * sin_vals], axis=0
            )
        )
    return matmul(outer_back_ref[...], stack_three(jnp.concatenate(columns, axis=1)))


def filter_kernel(
    own,
    embed_ref,
    embed_weight_ref,
    embed_bias_ref,
    sine_freq_ref,
    mid_weight_ref,
    mid_bias_ref,
    out_weight_ref,
    decay_ref,
    taps_ref,
    outer_ref,
    twiddle_ref,
    inner_ref,
    spectrum_ref,
    toeplitz_ref,
    pad_ref,
    vec_ref,
    out_rows_ref,
    filter_ref,
):
    full_len = embed_ref.shape[1]
    tap_count = taps_ref.shape[1]
    first_channel = pl.multiple_of(lax.axis_index("seq") * own, own)
    pad_ref[...] = jnp.zeros_like(pad_ref)
    pad_ref[: embed_weight_ref.shape[0], :] = embed_weight_ref[...]
    weight_one = six_left(pad_ref[...]).T.astype(BF16)
    weight_two = six_left(mid_weight_ref[...]).T.astype(BF16)
    high, low = split_two(out_weight_ref[...])
    high, low = high.astype(F32), low.astype(F32)
    out_rows_ref[...] = jnp.concatenate([high, high, low], axis=0).T
    weight_three = out_rows_ref[pl.ds(first_channel, own), :].astype(BF16)
    vec_ref[...] = jnp.zeros_like(vec_ref)
    vec_ref[0:1, : embed_bias_ref.shape[1]] = embed_bias_ref[...]
    vec_ref[1:2, : embed_bias_ref.shape[1]] = mid_bias_ref[...]
    vec_ref[2:3, : embed_bias_ref.shape[1]] = sine_freq_ref[...]
    vectors = vec_ref[...].T[: embed_bias_ref.shape[1]]
    bias_one, bias_two, freq = vectors[:, 0:1], vectors[:, 1:2], vectors[:, 2:3]
    decay = decay_ref[pl.ds(first_channel, own), :]
    scale = jnp.sqrt(2.0 * decay)

    def tile(index, carry):
        start = pl.multiple_of(index * TILE, TILE)
        first = sine(
            freq * (matmul(weight_one, six_right(embed_ref[:, pl.ds(start, TILE)])) + bias_one)
        )
        second = sine(freq * (matmul(weight_two, six_right(first)) + bias_two))
        raw = matmul(weight_three, stack_three(second))
        positions = (start + lax.broadcasted_iota(jnp.int32, (own, TILE), 1)).astype(F32)
        vals = raw * (scale * jnp.exp(-decay * positions))
        for j in range(TILE // LANES):
            row = pl.multiple_of(index * (TILE // LANES * own) + j * own, own)
            filter_ref[pl.ds(row, own), :] = vals[:, j * LANES : (j + 1) * LANES]
        return carry

    lax.fori_loop(0, full_len // TILE, tile, 0)
    blocks = full_len // LANES
    columns = [filter_ref[pl.ds(c, blocks, stride=own), :] for c in range(own)]
    spectrum_ref[...] = forward(columns, outer_ref, twiddle_ref, inner_ref)
    taps = taps_ref[pl.ds(first_channel, own), :]
    for c in range(own):
        line = jnp.concatenate(
            [taps[c : c + 1], jnp.zeros((1, tap_count), F32)], axis=1
        )
        table = pltpu.roll(
            jnp.broadcast_to(line, (2 * tap_count, 2 * tap_count)),
            tap_count,
            1,
            stride=1,
            stride_axis=0,
        )[:, :tap_count]
        high, low = split_two(table)
        toeplitz_ref[c] = jnp.concatenate([high, low], axis=1)


def mix_kernel(
    own,
    skip_ref,
    parts_ref,
    spectrum_ref,
    toeplitz_ref,
    outer_ref,
    twiddle_ref,
    inner_ref,
    inner_back_ref,
    outer_back_ref,
    out_ref,
    signal_ref,
    in_gate_ref,
    out_gate_ref,
    mixed_ref,
):
    seq_devs, _, part_rows, _ = parts_ref.shape
    blocks = seq_devs * part_rows // own
    first_channel = lax.axis_index("seq") * own
    signal_ref[:own, :] = jnp.zeros((own, LANES), F32)
    for p in range(seq_devs):
        at = p * part_rows
        signal_ref[own + at : own + at + part_rows, :] = parts_ref[p, 0].astype(F32)
        in_gate_ref[at : at + part_rows, :] = parts_ref[p, 1].astype(F32)
        out_gate_ref[at : at + part_rows, :] = parts_ref[p, 2].astype(F32)
    gated = []
    for c in range(own):
        window = jnp.concatenate(
            [
                signal_ref[pl.ds(c, blocks, stride=own), :],
                signal_ref[pl.ds(own + c, blocks, stride=own), :],
            ],
            axis=1,
        ).astype(BF16)
        both = matmul(window, toeplitz_ref[c])
        gated.append(
            in_gate_ref[pl.ds(c, blocks, stride=own), :] * (both[:, :LANES] + both[:, LANES:])
        )
    vals = forward(gated, outer_ref, twiddle_ref, inner_ref)
    real, imag = vals[:, :LANES], vals[:, LANES:]
    filt_real, filt_imag = spectrum_ref[:, :LANES], spectrum_ref[:, LANES:]
    product = jnp.concatenate(
        [real * filt_real - imag * filt_imag, real * filt_imag + imag * filt_real], axis=1
    )
    conv = backward(product, own, inner_back_ref, twiddle_ref, outer_back_ref)
    for c in range(own):
        mixed_ref[pl.ds(c, blocks, stride=own), :] = out_gate_ref[
            pl.ds(c, blocks, stride=own), :
        ] * (conv[:, c * LANES : (c + 1) * LANES] + skip_ref[first_channel + c] * gated[c])
    for q in range(part_rows // own):
        if own % 8 == 0:
            column = jnp.concatenate(
                [
                    mixed_ref[p * part_rows + q * own : p * part_rows + (q + 1) * own, :]
                    for p in range(seq_devs)
                ],
                axis=0,
            )
            out_ref[:, q * LANES : (q + 1) * LANES] = column.astype(BF16)
        else:
            for c in range(own):
                signal_ref[pl.ds(c, seq_devs, stride=own), :] = mixed_ref[
                    pl.ds(q * own + c, seq_devs, stride=part_rows), :
                ]
            out_ref[:, q * LANES : (q + 1) * LANES] = signal_ref[: seq_devs * own, :].astype(BF16)


def on_device(
    signal,
    in_gate,
    out_gate,
    short_taps,
    skip_gain,
    decay_rate,
    embed_weight,
    embed_bias,
    sine_freq,
    mid_weight,
    mid_bias,
    out_weight,
):
    channels, local_len = signal.shape
    tap_count = short_taps.shape[1]
    hidden = mid_weight.shape[0]
    seq_devs = lax.axis_size("seq")
    own = -(-channels // seq_devs)
    spare = own * seq_devs - channels
    full_len = seq_devs * local_len
    blocks = full_len // LANES
    local_blocks = local_len // LANES
    outer, twiddle, inner, inner_back, outer_back = transform_tables(full_len)
    embed = embed_table(full_len)

    parts = jnp.stack([signal, in_gate, out_gate])
    if spare:
        parts = jnp.pad(parts, ((0, 0), (0, spare), (0, 0)))
        short_taps = jnp.pad(short_taps, ((0, spare), (0, 0)))
        skip_gain = jnp.pad(skip_gain, (0, spare))
        decay_rate = jnp.pad(decay_rate, (0, spare), mode="edge")
        out_weight = jnp.pad(out_weight, ((0, 0), (0, spare)))
    parts = parts.reshape(3, seq_devs, own, local_blocks, LANES)
    parts = parts.transpose(1, 0, 3, 2, 4).reshape(seq_devs, 3, local_blocks * own, LANES)
    parts = lax.all_to_all(parts, "seq", split_axis=0, concat_axis=0, tiled=True)

    spectrum, toeplitz = pl.pallas_call(
        functools.partial(filter_kernel, own),
        out_shape=(
            jax.ShapeDtypeStruct((own * blocks, 2 * LANES), F32),
            jax.ShapeDtypeStruct((own, 2 * tap_count, 2 * tap_count), BF16),
        ),
        scratch_shapes=[
            pltpu.VMEM((embed.shape[0], hidden), F32),
            pltpu.VMEM((8, LANES), F32),
            pltpu.VMEM((channels + spare, 3 * hidden), F32),
            pltpu.VMEM((blocks * own, LANES), F32),
        ],
        compiler_params=pltpu.CompilerParams(vmem_limit_bytes=48 * 2**20),
    )(
        embed,
        embed_weight,
        embed_bias[None, :],
        sine_freq[None, :],
        mid_weight,
        mid_bias[None, :],
        out_weight,
        decay_rate[:, None],
        short_taps,
        outer,
        twiddle,
        inner,
    )
    vmem = pl.BlockSpec(memory_space=pltpu.VMEM)
    mixed = pl.pallas_call(
        functools.partial(mix_kernel, own),
        out_shape=jax.ShapeDtypeStruct((channels + spare, local_len), BF16),
        in_specs=[pl.BlockSpec(memory_space=pltpu.SMEM)] + [vmem] * 8,
        out_specs=vmem,
        scratch_shapes=[pltpu.VMEM(((blocks + 1) * own, LANES), F32)]
        + [pltpu.VMEM((blocks * own, LANES), F32)] * 3,
        compiler_params=pltpu.CompilerParams(vmem_limit_bytes=48 * 2**20),
    )(skip_gain, parts, spectrum, toeplitz, outer, twiddle, inner, inner_back, outer_back)
    return lax.all_to_all(mixed, "seq", split_axis=0, concat_axis=0, tiled=True)[:channels]


def solution(mesh):
    in_specs = (
        P("ch", "seq"),
        P("ch", "seq"),
        P("ch", "seq"),
        P("ch", None),
        P("ch"),
        P("ch"),
        P(),
        P(),
        P(),
        P(),
        P(),
        P(None, "ch"),
    )
    out_specs = P("ch", "seq")
    return jax.shard_map(
        on_device, mesh=mesh, in_specs=in_specs, out_specs=out_specs, check_vma=False
    )
```

```python
import functools
import math

import jax
import jax.numpy as jnp
import numpy as np
from jax import lax
from jax.experimental import pallas as pl
from jax.experimental.pallas import tpu as pltpu
from jax.sharding import PartitionSpec as P

BANDS = 16
LANES = 128
TILE = 1024
F32 = jnp.float32
BF16 = jnp.bfloat16
in_space = pltpu.with_memory_space_constraint


def round_up(count, step):
    return (count + step - 1) // step * step


def halves(table):
    high = table.astype(BF16)
    low = (table - high.astype(np.float64)).astype(BF16)
    return high, low


@functools.lru_cache(maxsize=None)
def embed_table(full_len):
    positions = np.arange(full_len, dtype=np.int64)
    rows = [positions / full_len]
    phase = positions
    for _ in range(BANDS):
        angle = phase * (2.0 * math.pi / full_len)
        rows += [np.cos(angle), np.sin(angle)]
        phase = 2 * phase % full_len
    table = np.zeros((round_up(len(rows), 8), full_len), np.float32)
    table[: len(rows)] = np.stack(rows)
    return table


@functools.lru_cache(maxsize=None)
def transform_tables(full_len):
    blocks = full_len // LANES
    a = np.arange(blocks)
    k1 = np.arange(blocks)
    b = np.arange(LANES)
    theta = 2.0 * math.pi / blocks * ((4 * k1 + 1)[:, None] * a[None, :] % (4 * blocks)) / 4.0
    phi = 2.0 * math.pi / full_len * ((4 * k1 + 1)[:, None] * b[None, :]) / 4.0
    psi = 2.0 * math.pi / LANES * (b[:, None] * b[None, :] % LANES)
    outer_high, outer_low = halves(np.concatenate([np.cos(theta), -np.sin(theta)], axis=0))
    outer = np.concatenate([outer_high, outer_high, outer_low], axis=1)
    back = np.concatenate([np.cos(theta).T, -np.sin(theta).T], axis=1) / full_len
    back_high, back_low = halves(back)
    outer_back = np.concatenate([back_high, back_high, back_low], axis=1)
    twiddle = np.stack([np.cos(phi), np.sin(phi)]).astype(np.float32)
    cos_in, sin_in = np.cos(psi), np.sin(psi)
    inner = np.stack(halves(np.block([[cos_in, -sin_in], [sin_in, cos_in]])))
    inner_back = np.stack(halves(np.block([[cos_in, sin_in], [-sin_in, cos_in]])))
    return outer, twiddle, inner, inner_back, outer_back


def sine_constants():
    nodes = np.cos((np.arange(400) + 0.5) * math.pi / 400) * (math.pi / 2)
    squares = nodes * nodes
    basis = np.stack([squares**p for p in range(6)], axis=1)
    fit = np.linalg.lstsq(basis, np.sin(nodes) / nodes, rcond=None)[0]
    first = np.floor(math.pi * 2.0**13) / 2.0**13
    second = np.floor((math.pi - first) * 2.0**28) / 2.0**28
    return [float(v) for v in fit], (float(first), float(second), math.pi - first - second)


SINE_FIT, PI_PARTS = sine_constants()


def sine(angle):
    turns = jnp.round(angle * (1.0 / math.pi))
    rest = angle
    for part in PI_PARTS:
        rest = rest - turns * part
    half = turns * 0.5
    odd = half - jnp.floor(half)
    square = rest * rest
    value = SINE_FIT[5]
    for term in SINE_FIT[4::-1]:
        value = value * square + term
    return value * (rest - rest * (4.0 * odd))


def split_two(vals):
    high = vals.astype(BF16)
    return high, (vals - high.astype(F32)).astype(BF16)


def split_three(vals):
    first = vals.astype(BF16).astype(F32)
    rest = vals - first
    second = rest.astype(BF16).astype(F32)
    return first, second, rest - second


def matmul(lhs, rhs):
    return jnp.dot(lhs, rhs, preferred_element_type=F32)


def six_left(vals):
    one, two, three = split_three(vals)
    return jnp.concatenate([one, one, two, one, three, two], axis=0)


def six_right(vals):
    one, two, three = split_three(vals)
    return jnp.concatenate([one, two, one, three, one, two], axis=0).astype(BF16)


def stack_three(vals):
    high, low = split_two(vals)
    return jnp.concatenate([high, low, high], axis=0)


def inner_product(vals, table_ref):
    high, low = split_two(vals)
    return (
        matmul(high, table_ref[0]) + matmul(low, table_ref[0]) + matmul(high, table_ref[1])
    )


def forward(columns, outer_ref, twiddle_ref, inner_ref):
    blocks = columns[0].shape[0]
    mixed = matmul(outer_ref[...], stack_three(jnp.concatenate(columns, axis=1)))
    cos_vals, sin_vals = twiddle_ref[0], twiddle_ref[1]
    rows = []
    for c in range(len(columns)):
        real = mixed[:blocks, c * LANES : (c + 1) * LANES]
        imag = mixed[blocks:, c * LANES : (c + 1) * LANES]
        rows.append(
            jnp.concatenate(
                [real * cos_vals + imag * sin_vals, imag * cos_vals - real * sin_vals], axis=1
            )
        )
    return inner_product(jnp.concatenate(rows, axis=0), inner_ref)


def backward(spectrum, channels, inner_back_ref, twiddle_ref, outer_back_ref):
    vals = inner_product(spectrum, inner_back_ref)
    blocks = vals.shape[0] // channels
    cos_vals, sin_vals = twiddle_ref[0], twiddle_ref[1]
    columns = []
    for c in range(channels):
        real = vals[c * blocks : (c + 1) * blocks, :LANES]
        imag = vals[c * blocks : (c + 1) * blocks, LANES:]
        columns.append(
            jnp.concatenate(
                [real * cos_vals - imag * sin_vals, imag * cos_vals + real * sin_vals], axis=0
            )
        )
    return matmul(outer_back_ref[...], stack_three(jnp.concatenate(columns, axis=1)))


def pack_kernel(signal_ref, in_gate_ref, out_gate_ref, parts_ref, sems):
    copies = [
        pltpu.make_async_copy(ref, parts_ref.at[:, i], sems.at[i])
        for i, ref in enumerate((signal_ref, in_gate_ref, out_gate_ref))
    ]
    for copy in copies:
        copy.start()
    for copy in copies:
        copy.wait()


def filter_kernel(
    own,
    embed_hbm,
    embed_weight_hbm,
    vectors_hbm,
    mid_weight_hbm,
    out_weight_hbm,
    channel_hbm,
    taps_hbm,
    outer_hbm,
    twiddle_hbm,
    inner_hbm,
    inner_back_hbm,
    outer_back_hbm,
    spectrum_ref,
    toeplitz_ref,
    skip_ref,
    outer_ref,
    twiddle_ref,
    inner_ref,
    inner_back_ref,
    outer_back_ref,
    embed_ref,
    embed_weight_ref,
    vectors_ref,
    mid_weight_ref,
    out_weight_ref,
    channel_ref,
    taps_ref,
    pad_ref,
    out_rows_ref,
    columns_ref,
    filter_ref,
    sems,
):
    pairs = [
        (embed_weight_hbm, embed_weight_ref),
        (vectors_hbm, vectors_ref),
        (mid_weight_hbm, mid_weight_ref),
        (out_weight_hbm, out_weight_ref),
        (channel_hbm, channel_ref),
        (embed_hbm, embed_ref),
        (taps_hbm, taps_ref),
        (outer_hbm, outer_ref),
        (twiddle_hbm, twiddle_ref),
        (inner_hbm, inner_ref),
        (inner_back_hbm, inner_back_ref),
        (outer_back_hbm, outer_back_ref),
    ]
    copies = [pltpu.make_async_copy(*pair, sems.at[i]) for i, pair in enumerate(pairs)]
    for copy in copies:
        copy.start()
    full_len = embed_ref.shape[1]
    hidden = mid_weight_ref.shape[0]
    tap_count = taps_ref.shape[1]
    first_channel = pl.multiple_of(lax.axis_index("seq") * own, own)
    pad_ref[...] = jnp.zeros_like(pad_ref)
    for copy in copies:
        copy.wait()
    pad_ref[: embed_weight_ref.shape[0], :] = embed_weight_ref[...]
    weight_one = six_left(pad_ref[...]).T.astype(BF16)
    weight_two = six_left(mid_weight_ref[...]).T.astype(BF16)
    high, low = split_two(out_weight_ref[...])
    high, low = high.astype(F32), low.astype(F32)
    out_rows_ref[...] = jnp.concatenate([high, high, low], axis=0).T
    weight_three = out_rows_ref[pl.ds(first_channel, own), :].astype(BF16)
    vectors = vectors_ref[...].T
    bias_one, bias_two, freq = vectors[:, 0:1], vectors[:, 1:2], vectors[:, 2:3]
    columns_ref[...] = channel_ref[...].T
    decay = columns_ref[pl.ds(first_channel, own), 0:1]
    skip_ref[...] = jnp.broadcast_to(columns_ref[pl.ds(first_channel, own), 1:2], skip_ref.shape)
    scale = jnp.sqrt(2.0 * decay)

    def tile(index, carry):
        start = pl.multiple_of(index * TILE, TILE)
        first = sine(
            freq * (matmul(weight_one, six_right(embed_ref[:, pl.ds(start, TILE)])) + bias_one)
        )
        second = sine(freq * (matmul(weight_two, six_right(first)) + bias_two))
        raw = matmul(weight_three, stack_three(second))
        positions = (start + lax.broadcasted_iota(jnp.int32, (own, TILE), 1)).astype(F32)
        vals = raw * (scale * jnp.exp(-decay * positions))
        for j in range(TILE // LANES):
            row = pl.multiple_of(index * (TILE // LANES * own) + j * own, own)
            filter_ref[pl.ds(row, own), :] = vals[:, j * LANES : (j + 1) * LANES]
        return carry

    lax.fori_loop(0, full_len // TILE, tile, 0)
    blocks = full_len // LANES
    columns = [filter_ref[pl.ds(c, blocks, stride=own), :] for c in range(own)]
    spectrum_ref[...] = forward(columns, outer_ref, twiddle_ref, inner_ref)
    taps = taps_ref[pl.ds(first_channel, own), :]
    for c in range(own):
        line = jnp.concatenate(
            [taps[c : c + 1], jnp.zeros((1, tap_count), F32)], axis=1
        )
        table = pltpu.roll(
            jnp.broadcast_to(line, (2 * tap_count, 2 * tap_count)),
            tap_count,
            1,
            stride=1,
            stride_axis=0,
        )[:, :tap_count]
        high, low = split_two(table)
        toeplitz_ref[c] = jnp.concatenate([high, low], axis=1)


def mix_kernel(
    own,
    parts_ref,
    spectrum_ref,
    toeplitz_ref,
    skip_ref,
    outer_ref,
    twiddle_ref,
    inner_ref,
    inner_back_ref,
    outer_back_ref,
    out_ref,
    signal_ref,
    in_gate_ref,
    out_gate_ref,
    mixed_ref,
):
    seq_devs, _, _, local_len = parts_ref.shape
    local_blocks = local_len // LANES
    part_rows = local_blocks * own
    blocks = seq_devs * local_blocks
    signal_ref[:own, :] = jnp.zeros((own, LANES), F32)
    for p in range(seq_devs):
        for q in range(local_blocks):
            at = p * part_rows + q * own
            lanes = slice(q * LANES, (q + 1) * LANES)
            signal_ref[own + at : 2 * own + at, :] = parts_ref[p, 0, :, lanes].astype(F32)
            in_gate_ref[at : at + own, :] = parts_ref[p, 1, :, lanes].astype(F32)
            out_gate_ref[at : at + own, :] = parts_ref[p, 2, :, lanes].astype(F32)
    gated = []
    for c in range(own):
        window = jnp.concatenate(
            [
                signal_ref[pl.ds(c, blocks, stride=own), :],
                signal_ref[pl.ds(own + c, blocks, stride=own), :],
            ],
            axis=1,
        ).astype(BF16)
        both = matmul(window, toeplitz_ref[c])
        gated.append(
            in_gate_ref[pl.ds(c, blocks, stride=own), :] * (both[:, :LANES] + both[:, LANES:])
        )
    vals = forward(gated, outer_ref, twiddle_ref, inner_ref)
    real, imag = vals[:, :LANES], vals[:, LANES:]
    filt_real, filt_imag = spectrum_ref[:, :LANES], spectrum_ref[:, LANES:]
    product = jnp.concatenate(
        [real * filt_real - imag * filt_imag, real * filt_imag + imag * filt_real], axis=1
    )
    conv = backward(product, own, inner_back_ref, twiddle_ref, outer_back_ref)
    for c in range(own):
        mixed_ref[pl.ds(c, blocks, stride=own), :] = out_gate_ref[
            pl.ds(c, blocks, stride=own), :
        ] * (conv[:, c * LANES : (c + 1) * LANES] + skip_ref[c : c + 1, :] * gated[c])
    for q in range(local_blocks):
        if own % 8 == 0:
            column = jnp.concatenate(
                [
                    mixed_ref[p * part_rows + q * own : p * part_rows + (q + 1) * own, :]
                    for p in range(seq_devs)
                ],
                axis=0,
            )
            out_ref[:, q * LANES : (q + 1) * LANES] = column.astype(BF16)
        else:
            for c in range(own):
                signal_ref[pl.ds(c, seq_devs, stride=own), :] = mixed_ref[
                    pl.ds(q * own + c, seq_devs, stride=part_rows), :
                ]
            out_ref[:, q * LANES : (q + 1) * LANES] = signal_ref[: seq_devs * own, :].astype(BF16)


def on_device(
    signal,
    in_gate,
    out_gate,
    short_taps,
    skip_gain,
    decay_rate,
    embed_weight,
    embed_bias,
    sine_freq,
    mid_weight,
    mid_bias,
    out_weight,
):
    channels, local_len = signal.shape
    tap_count = short_taps.shape[1]
    hidden = mid_weight.shape[0]
    seq_devs = lax.axis_size("seq")
    own = -(-channels // seq_devs)
    spare = own * seq_devs - channels
    full_len = seq_devs * local_len
    blocks = full_len // LANES
    local_blocks = local_len // LANES
    outer, twiddle, inner, inner_back, outer_back = transform_tables(full_len)
    embed = embed_table(full_len)

    parts = [signal, in_gate, out_gate]
    if spare:
        parts = [jnp.pad(part, ((0, spare), (0, 0))) for part in parts]
        short_taps = jnp.pad(short_taps, ((0, spare), (0, 0)))
        skip_gain = jnp.pad(skip_gain, (0, spare))
        decay_rate = jnp.pad(decay_rate, (0, spare), mode="edge")
        out_weight = jnp.pad(out_weight, ((0, 0), (0, spare)))
    hbm = pl.BlockSpec(memory_space=pltpu.HBM)
    vmem = pl.BlockSpec(memory_space=pltpu.VMEM)
    parts = pl.pallas_call(
        pack_kernel,
        out_shape=pltpu.VMEM((seq_devs, 3, own, local_len), BF16),
        in_specs=[hbm] * 3,
        out_specs=vmem,
        scratch_shapes=[pltpu.SemaphoreType.DMA((3,))],
    )(*[in_space(part.reshape(seq_devs, own, local_len), pltpu.HBM) for part in parts])
    parts = lax.all_to_all(parts, "seq", split_axis=0, concat_axis=0, tiled=True)

    params = (
        embed,
        embed_weight,
        jnp.stack([embed_bias, mid_bias, sine_freq]),
        mid_weight,
        out_weight,
        jnp.stack([decay_rate, skip_gain]),
        short_taps,
    )
    tables = (outer, twiddle, inner, inner_back, outer_back)
    shared = pl.pallas_call(
        functools.partial(filter_kernel, own),
        out_shape=(
            pltpu.VMEM((own * blocks, 2 * LANES), F32),
            pltpu.VMEM((own, 2 * tap_count, 2 * tap_count), BF16),
            pltpu.VMEM((own, LANES), F32),
        )
        + tuple(pltpu.VMEM(table.shape, table.dtype) for table in tables),
        in_specs=[hbm] * (len(params) + len(tables)),
        out_specs=(vmem,) * (3 + len(tables)),
        scratch_shapes=[pltpu.VMEM(param.shape, F32) for param in params]
        + [
            pltpu.VMEM((embed.shape[0], hidden), F32),
            pltpu.VMEM((channels + spare, 3 * hidden), F32),
            pltpu.VMEM((channels + spare, 2), F32),
            pltpu.VMEM((blocks * own, LANES), F32),
            pltpu.SemaphoreType.DMA((len(params) + len(tables),)),
        ],
        compiler_params=pltpu.CompilerParams(vmem_limit_bytes=48 * 2**20),
    )(*[in_space(jnp.asarray(vals), pltpu.HBM) for vals in params + tables])
    mixed = pl.pallas_call(
        functools.partial(mix_kernel, own),
        out_shape=jax.ShapeDtypeStruct((channels + spare, local_len), BF16),
        in_specs=[vmem] * (1 + len(shared)),
        out_specs=vmem,
        scratch_shapes=[pltpu.VMEM(((blocks + 1) * own, LANES), F32)]
        + [pltpu.VMEM((blocks * own, LANES), F32)] * 3,
        compiler_params=pltpu.CompilerParams(vmem_limit_bytes=48 * 2**20),
    )(parts, *[in_space(vals, pltpu.VMEM) for vals in shared])
    return lax.all_to_all(mixed, "seq", split_axis=0, concat_axis=0, tiled=True)[:channels]


def solution(mesh):
    in_specs = (
        P("ch", "seq"),
        P("ch", "seq"),
        P("ch", "seq"),
        P("ch", None),
        P("ch"),
        P("ch"),
        P(),
        P(),
        P(),
        P(),
        P(),
        P(None, "ch"),
    )
    out_specs = P("ch", "seq")
    return jax.shard_map(
        on_device, mesh=mesh, in_specs=in_specs, out_specs=out_specs, check_vma=False
    )
```

```python
import functools
import math

import jax
import jax.numpy as jnp
import numpy as np
from jax import lax
from jax.experimental import pallas as pl
from jax.experimental.pallas import tpu as pltpu
from jax.sharding import PartitionSpec as P

BANDS = 16
LANES = 128
TILES = 4
F32 = jnp.float32
BF16 = jnp.bfloat16
in_space = pltpu.with_memory_space_constraint


def round_up(count, step):
    return (count + step - 1) // step * step


def halves(table):
    high = table.astype(BF16)
    low = (table - high.astype(np.float64)).astype(BF16)
    return high, low


@functools.lru_cache(maxsize=None)
def embed_table(full_len):
    positions = np.arange(full_len, dtype=np.int64)
    rows = [positions / full_len]
    phase = positions
    for _ in range(BANDS):
        angle = phase * (2.0 * math.pi / full_len)
        rows += [np.cos(angle), np.sin(angle)]
        phase = 2 * phase % full_len
    rows.append(np.ones(full_len))
    table = np.zeros((round_up(len(rows), 8), full_len))
    table[: len(rows)] = np.stack(rows)
    first, rest = halves(table)
    second, third = halves(table - first.astype(np.float64))
    stacked = np.concatenate([first, second, third], axis=0)
    return np.pad(stacked, ((0, -len(stacked) % 16), (0, 0)))


@functools.lru_cache(maxsize=None)
def transform_tables(full_len):
    blocks = full_len // LANES
    a = np.arange(blocks)
    k1 = np.arange(blocks)
    b = np.arange(LANES)
    theta = 2.0 * math.pi / blocks * ((4 * k1 + 1)[:, None] * a[None, :] % (4 * blocks)) / 4.0
    phi = 2.0 * math.pi / full_len * ((4 * k1 + 1)[:, None] * b[None, :]) / 4.0
    psi = 2.0 * math.pi / LANES * (b[:, None] * b[None, :] % LANES)
    outer_high, outer_low = halves(np.concatenate([np.cos(theta), -np.sin(theta)], axis=0))
    outer = np.concatenate([outer_high, outer_high, outer_low], axis=1)
    back = np.concatenate([np.cos(theta).T, -np.sin(theta).T], axis=1) / full_len
    back_high, back_low = halves(back)
    outer_back = np.concatenate([back_high, back_high, back_low], axis=1)
    twiddle = np.stack([np.cos(phi), np.sin(phi)]).astype(np.float32)
    cos_in, sin_in = np.cos(psi), np.sin(psi)
    inner = np.stack(halves(np.block([[cos_in, -sin_in], [sin_in, cos_in]])))
    inner_back = np.stack(halves(np.block([[cos_in, sin_in], [-sin_in, cos_in]])))
    return outer, twiddle, inner, inner_back, outer_back


def sine_fit(terms):
    nodes = np.cos((np.arange(400) + 0.5) * math.pi / 400) * 0.5
    basis = np.stack([nodes ** (2 * p + 1) for p in range(terms)], axis=1)
    fit = np.linalg.lstsq(basis, np.sin(2.0 * math.pi * nodes), rcond=None)[0]
    return [float(v) for v in fit]


SINE_FIT = sine_fit(7)


def sine_of_turns(turns):
    part = turns - jnp.round(turns)
    square = part * part
    value = SINE_FIT[-1]
    for term in SINE_FIT[-2::-1]:
        value = value * square + term
    return value * part


def split_two(vals):
    high = vals.astype(BF16)
    return high, (vals - high.astype(F32)).astype(BF16)


def split_three(vals):
    first = vals.astype(BF16).astype(F32)
    rest = vals - first
    second = rest.astype(BF16).astype(F32)
    return first, second, rest - second


def matmul(lhs, rhs):
    return jnp.dot(lhs, rhs, preferred_element_type=F32)


def stack_three(vals):
    high, low = split_two(vals)
    return jnp.concatenate([high, low, high], axis=0)


def inner_product(vals, table_ref):
    high, low = split_two(vals)
    return (
        matmul(high, table_ref[0]) + matmul(low, table_ref[0]) + matmul(high, table_ref[1])
    )


def forward(columns, outer_ref, twiddle_ref, inner_ref):
    blocks = columns[0].shape[0]
    mixed = matmul(outer_ref[...], stack_three(jnp.concatenate(columns, axis=1)))
    cos_vals, sin_vals = twiddle_ref[0], twiddle_ref[1]
    rows = []
    for c in range(len(columns)):
        real = mixed[:blocks, c * LANES : (c + 1) * LANES]
        imag = mixed[blocks:, c * LANES : (c + 1) * LANES]
        rows.append(
            jnp.concatenate(
                [real * cos_vals + imag * sin_vals, imag * cos_vals - real * sin_vals], axis=1
            )
        )
    return inner_product(jnp.concatenate(rows, axis=0), inner_ref)


def backward(spectrum, channels, inner_back_ref, twiddle_ref, outer_back_ref):
    vals = inner_product(spectrum, inner_back_ref)
    blocks = vals.shape[0] // channels
    cos_vals, sin_vals = twiddle_ref[0], twiddle_ref[1]
    columns = []
    for c in range(channels):
        real = vals[c * blocks : (c + 1) * blocks, :LANES]
        imag = vals[c * blocks : (c + 1) * blocks, LANES:]
        columns.append(
            jnp.concatenate(
                [real * cos_vals - imag * sin_vals, imag * cos_vals + real * sin_vals], axis=0
            )
        )
    return matmul(outer_back_ref[...], stack_three(jnp.concatenate(columns, axis=1)))


def pack_kernel(signal_ref, in_gate_ref, out_gate_ref, parts_ref, sems):
    copies = [
        pltpu.make_async_copy(ref, parts_ref.at[:, i], sems.at[i])
        for i, ref in enumerate((signal_ref, in_gate_ref, out_gate_ref))
    ]
    for copy in copies:
        copy.start()
    for copy in copies:
        copy.wait()


def filter_kernel(
    own,
    embed_hbm,
    embed_weight_hbm,
    embed_bias_hbm,
    sine_freq_hbm,
    mid_weight_hbm,
    mid_bias_hbm,
    out_weight_hbm,
    decay_hbm,
    skip_hbm,
    taps_hbm,
    outer_hbm,
    twiddle_hbm,
    inner_hbm,
    inner_back_hbm,
    outer_back_hbm,
    spectrum_ref,
    toeplitz_ref,
    skip_ref,
    outer_ref,
    twiddle_ref,
    inner_ref,
    inner_back_ref,
    outer_back_ref,
    embed_ref,
    embed_weight_ref,
    embed_bias_ref,
    sine_freq_ref,
    mid_weight_ref,
    mid_bias_ref,
    out_weight_ref,
    decay_ref,
    skip_row_ref,
    taps_ref,
    pad_ref,
    vec_ref,
    row_ref,
    column_ref,
    out_rows_ref,
    filter_ref,
    sems,
    embed_sems,
):
    full_len = embed_ref.shape[1]
    tile_len = full_len // TILES
    hidden = mid_weight_ref.shape[0]
    pairs = [
        (embed_weight_hbm, embed_weight_ref),
        (embed_bias_hbm, embed_bias_ref),
        (sine_freq_hbm, sine_freq_ref),
        (mid_weight_hbm, mid_weight_ref),
        (mid_bias_hbm, mid_bias_ref),
        (out_weight_hbm, out_weight_ref),
        (decay_hbm, decay_ref),
        (skip_hbm, skip_row_ref),
        (taps_hbm, taps_ref),
        (outer_hbm, outer_ref),
        (twiddle_hbm, twiddle_ref),
        (inner_hbm, inner_ref),
        (inner_back_hbm, inner_back_ref),
        (outer_back_hbm, outer_back_ref),
    ]
    copies = [pltpu.make_async_copy(*pair, sems.at[i]) for i, pair in enumerate(pairs)]
    embed_copies = []
    for i in range(TILES):
        lanes = pl.ds(i * tile_len, tile_len)
        embed_copies.append(
            pltpu.make_async_copy(
                embed_hbm.at[:, lanes], embed_ref.at[:, lanes], embed_sems.at[i]
            )
        )
    for copy in copies[:8] + embed_copies + copies[8:]:
        copy.start()
    first_channel = pl.multiple_of(lax.axis_index("seq") * own, own)
    pad_ref[...] = jnp.zeros_like(pad_ref)
    vec_ref[...] = jnp.zeros_like(vec_ref)
    row_ref[...] = jnp.zeros_like(row_ref)
    for copy in copies[:8]:
        copy.wait()

    freq = sine_freq_ref[...] * (0.5 / math.pi)
    features = embed_weight_ref.shape[0]
    pad_ref[:features, :] = embed_weight_ref[...] * freq
    pad_ref[features : features + 1, :] = embed_bias_ref[...] * freq
    one, two, three = split_three(pad_ref[...])
    none = jnp.zeros_like(one)
    rest = jnp.zeros((embed_ref.shape[0] - 3 * one.shape[0], hidden), F32)
    weight_one = jnp.concatenate(
        [
            jnp.concatenate([one, one, one, rest], axis=0).T,
            jnp.concatenate([two, two, none, rest], axis=0).T,
            jnp.concatenate([three, none, none, rest], axis=0).T,
        ],
        axis=0,
    ).astype(BF16)
    one, two, _ = split_three(mid_weight_ref[...] * freq)
    weight_two = jnp.concatenate(
        [jnp.concatenate([one, one], axis=0).T, jnp.concatenate([two, two], axis=0).T], axis=0
    ).astype(BF16)
    vec_ref[0:1, :] = mid_bias_ref[...] * freq
    bias_two = vec_ref[...].T[:, 0:1]
    one, two, _ = split_three(out_weight_ref[...])
    out_rows_ref[0] = jnp.concatenate([one, one], axis=0).T
    out_rows_ref[1] = jnp.concatenate([two, two], axis=0).T
    own_rows = pl.ds(first_channel, own)
    weight_three = jnp.concatenate(
        [out_rows_ref[0, own_rows, :], out_rows_ref[1, own_rows, :]], axis=0
    ).astype(BF16)
    row_ref[0:1, :] = decay_ref[...]
    row_ref[1:2, :] = skip_row_ref[...]
    column_ref[...] = row_ref[...].T
    decay = column_ref[own_rows, 0:1]
    skip_ref[...] = jnp.broadcast_to(column_ref[own_rows, 1:2], skip_ref.shape)
    scale = jnp.sqrt(2.0 * decay)

    for i in range(TILES):
        start = i * tile_len
        embed_copies[i].wait()
        turns = matmul(weight_one, embed_ref[:, start : start + tile_len])
        first = sine_of_turns(
            turns[:hidden] + turns[hidden : 2 * hidden] + turns[2 * hidden :]
        )
        turns = matmul(weight_two, jnp.concatenate(split_two(first), axis=0))
        second = sine_of_turns(turns[:hidden] + turns[hidden:] + bias_two)
        raw = matmul(weight_three, jnp.concatenate(split_two(second), axis=0))
        positions = (start + lax.broadcasted_iota(jnp.int32, (own, tile_len), 1)).astype(F32)
        vals = (raw[:own] + raw[own:]) * (scale * jnp.exp(-decay * positions))
        for j in range(tile_len // LANES):
            row = (start // LANES + j) * own
            filter_ref[row : row + own, :] = vals[:, j * LANES : (j + 1) * LANES]

    for copy in copies[8:]:
        copy.wait()
    blocks = full_len // LANES
    columns = [filter_ref[pl.ds(c, blocks, stride=own), :] for c in range(own)]
    spectrum_ref[...] = forward(columns, outer_ref, twiddle_ref, inner_ref)
    taps = taps_ref[own_rows, :]
    tap_count = taps.shape[1]
    square = (tap_count, tap_count)
    upper = lax.broadcasted_iota(jnp.int32, square, 1) >= lax.broadcasted_iota(
        jnp.int32, square, 0
    )
    for c in range(own):
        lags = pltpu.roll(
            jnp.broadcast_to(taps[c : c + 1], square), 0, 1, stride=1, stride_axis=0
        )
        high, low = split_two(
            jnp.concatenate([jnp.where(upper, 0.0, lags), jnp.where(upper, lags, 0.0)], axis=0)
        )
        toeplitz_ref[c] = jnp.concatenate([high, low], axis=1)


def mix_kernel(
    own,
    parts_ref,
    spectrum_ref,
    toeplitz_ref,
    skip_ref,
    outer_ref,
    twiddle_ref,
    inner_ref,
    inner_back_ref,
    outer_back_ref,
    out_ref,
    signal_ref,
    in_gate_ref,
    out_gate_ref,
    mixed_ref,
):
    seq_devs, _, _, local_len = parts_ref.shape
    local_blocks = local_len // LANES
    part_rows = local_blocks * own
    blocks = seq_devs * local_blocks
    signal_ref[:own, :] = jnp.zeros((own, LANES), F32)
    for p in range(seq_devs):
        for q in range(local_blocks):
            at = p * part_rows + q * own
            lanes = slice(q * LANES, (q + 1) * LANES)
            signal_ref[own + at : 2 * own + at, :] = parts_ref[p, 0, :, lanes].astype(F32)
            in_gate_ref[at : at + own, :] = parts_ref[p, 1, :, lanes].astype(F32)
            out_gate_ref[at : at + own, :] = parts_ref[p, 2, :, lanes].astype(F32)
    gated = []
    for c in range(own):
        window = jnp.concatenate(
            [
                signal_ref[pl.ds(c, blocks, stride=own), :],
                signal_ref[pl.ds(own + c, blocks, stride=own), :],
            ],
            axis=1,
        ).astype(BF16)
        both = matmul(window, toeplitz_ref[c])
        gated.append(
            in_gate_ref[pl.ds(c, blocks, stride=own), :] * (both[:, :LANES] + both[:, LANES:])
        )
    vals = forward(gated, outer_ref, twiddle_ref, inner_ref)
    real, imag = vals[:, :LANES], vals[:, LANES:]
    filt_real, filt_imag = spectrum_ref[:, :LANES], spectrum_ref[:, LANES:]
    product = jnp.concatenate(
        [real * filt_real - imag * filt_imag, real * filt_imag + imag * filt_real], axis=1
    )
    conv = backward(product, own, inner_back_ref, twiddle_ref, outer_back_ref)
    for c in range(own):
        mixed_ref[pl.ds(c, blocks, stride=own), :] = out_gate_ref[
            pl.ds(c, blocks, stride=own), :
        ] * (conv[:, c * LANES : (c + 1) * LANES] + skip_ref[c : c + 1, :] * gated[c])
    for q in range(local_blocks):
        if own % 8 == 0:
            column = jnp.concatenate(
                [
                    mixed_ref[p * part_rows + q * own : p * part_rows + (q + 1) * own, :]
                    for p in range(seq_devs)
                ],
                axis=0,
            )
            out_ref[:, q * LANES : (q + 1) * LANES] = column.astype(BF16)
        else:
            for c in range(own):
                signal_ref[pl.ds(c, seq_devs, stride=own), :] = mixed_ref[
                    pl.ds(q * own + c, seq_devs, stride=part_rows), :
                ]
            out_ref[:, q * LANES : (q + 1) * LANES] = signal_ref[: seq_devs * own, :].astype(BF16)


def pack(parts, seq_devs, own):
    local_len = parts[0].shape[1]
    hbm = pl.BlockSpec(memory_space=pltpu.HBM)
    return pl.pallas_call(
        pack_kernel,
        out_shape=pltpu.VMEM((seq_devs, 3, own, local_len), BF16),
        in_specs=[hbm] * 3,
        out_specs=pl.BlockSpec(memory_space=pltpu.VMEM),
        scratch_shapes=[pltpu.SemaphoreType.DMA((3,))],
    )(*[in_space(part.reshape(seq_devs, own, local_len), pltpu.HBM) for part in parts])


def make_filter(params, own, full_len):
    blocks = full_len // LANES
    hidden, channels = params[5].shape
    tap_count = params[8].shape[1]
    embed = embed_table(full_len)
    tables = transform_tables(full_len)
    operands = (embed,) + params + tables
    padded = round_up(params[0].shape[0] + 1, 8)
    return pl.pallas_call(
        functools.partial(filter_kernel, own),
        out_shape=(
            pltpu.VMEM((own * blocks, 2 * LANES), F32),
            pltpu.VMEM((own, 2 * tap_count, 2 * tap_count), BF16),
            pltpu.VMEM((own, LANES), F32),
        )
        + tuple(pltpu.VMEM(table.shape, table.dtype) for table in tables),
        in_specs=[pl.BlockSpec(memory_space=pltpu.HBM)] * len(operands),
        out_specs=(pl.BlockSpec(memory_space=pltpu.VMEM),) * (3 + len(tables)),
        scratch_shapes=[pltpu.VMEM(embed.shape, BF16)]
        + [pltpu.VMEM(vals.shape, F32) for vals in params]
        + [
            pltpu.VMEM((padded, hidden), F32),
            pltpu.VMEM((8, hidden), F32),
            pltpu.VMEM((8, channels), F32),
            pltpu.VMEM((channels, 8), F32),
            pltpu.VMEM((2, channels, 2 * hidden), F32),
            pltpu.VMEM((blocks * own, LANES), F32),
            pltpu.SemaphoreType.DMA((len(operands) - 1,)),
            pltpu.SemaphoreType.DMA((TILES,)),
        ],
        compiler_params=pltpu.CompilerParams(vmem_limit_bytes=48 * 2**20),
    )(*[in_space(jnp.asarray(vals), pltpu.HBM) for vals in operands])


def mix(parts, shared):
    seq_devs, _, own, local_len = parts.shape
    rows = seq_devs * own * (local_len // LANES)
    vmem = pl.BlockSpec(memory_space=pltpu.VMEM)
    return pl.pallas_call(
        functools.partial(mix_kernel, own),
        out_shape=jax.ShapeDtypeStruct((seq_devs * own, local_len), BF16),
        in_specs=[vmem] * (1 + len(shared)),
        out_specs=vmem,
        scratch_shapes=[pltpu.VMEM((rows + own, LANES), F32)]
        + [pltpu.VMEM((rows, LANES), F32)] * 3,
        compiler_params=pltpu.CompilerParams(vmem_limit_bytes=48 * 2**20),
    )(parts, *[in_space(vals, pltpu.VMEM) for vals in shared])


def on_device(
    signal,
    in_gate,
    out_gate,
    short_taps,
    skip_gain,
    decay_rate,
    embed_weight,
    embed_bias,
    sine_freq,
    mid_weight,
    mid_bias,
    out_weight,
):
    channels, local_len = signal.shape
    seq_devs = lax.axis_size("seq")
    own = -(-channels // seq_devs)
    spare = own * seq_devs - channels
    parts = [signal, in_gate, out_gate]
    if spare:
        parts = [jnp.pad(part, ((0, spare), (0, 0))) for part in parts]
        short_taps = jnp.pad(short_taps, ((0, spare), (0, 0)))
        skip_gain = jnp.pad(skip_gain, (0, spare))
        decay_rate = jnp.pad(decay_rate, (0, spare), mode="edge")
        out_weight = jnp.pad(out_weight, ((0, 0), (0, spare)))
    parts = pack(parts, seq_devs, own)
    parts = lax.all_to_all(parts, "seq", split_axis=0, concat_axis=0, tiled=True)
    params = (
        embed_weight,
        embed_bias[None, :],
        sine_freq[None, :],
        mid_weight,
        mid_bias[None, :],
        out_weight,
        decay_rate[None, :],
        skip_gain[None, :],
        short_taps,
    )
    shared = make_filter(params, own, seq_devs * local_len)
    mixed = mix(parts, shared)
    return lax.all_to_all(mixed, "seq", split_axis=0, concat_axis=0, tiled=True)[:channels]


def solution(mesh):
    in_specs = (
        P("ch", "seq"),
        P("ch", "seq"),
        P("ch", "seq"),
        P("ch", None),
        P("ch"),
        P("ch"),
        P(),
        P(),
        P(),
        P(),
        P(),
        P(None, "ch"),
    )
    out_specs = P("ch", "seq")
    return jax.shard_map(
        on_device, mesh=mesh, in_specs=in_specs, out_specs=out_specs, check_vma=False
    )
```

```python
import functools
import math

import jax
import jax.numpy as jnp
import numpy as np
from jax import lax
from jax.experimental import pallas as pl
from jax.experimental.pallas import tpu as pltpu
from jax.sharding import PartitionSpec as P

BANDS = 16
LANES = 128
TILES = 4
F32 = jnp.float32
BF16 = jnp.bfloat16
in_space = pltpu.with_memory_space_constraint


def round_up(count, step):
    return (count + step - 1) // step * step


def halves(table):
    high = table.astype(BF16)
    low = (table - high.astype(np.float64)).astype(BF16)
    return high, low


@functools.lru_cache(maxsize=None)
def embed_table(full_len):
    positions = np.arange(full_len, dtype=np.int64)
    rows = [positions / full_len]
    phase = positions
    for _ in range(BANDS):
        angle = phase * (2.0 * math.pi / full_len)
        rows += [np.cos(angle), np.sin(angle)]
        phase = 2 * phase % full_len
    rows.append(np.ones(full_len))
    table = np.zeros((round_up(len(rows), 8), full_len))
    table[: len(rows)] = np.stack(rows)
    first, rest = halves(table)
    second, third = halves(table - first.astype(np.float64))
    stacked = np.concatenate([first, second, third], axis=0)
    return np.pad(stacked, ((0, -len(stacked) % 16), (0, 0)))


@functools.lru_cache(maxsize=None)
def transform_tables(full_len):
    blocks = full_len // LANES
    a = np.arange(blocks)
    k1 = np.arange(blocks)
    b = np.arange(LANES)
    theta = 2.0 * math.pi / blocks * ((4 * k1 + 1)[:, None] * a[None, :] % (4 * blocks)) / 4.0
    phi = 2.0 * math.pi / full_len * ((4 * k1 + 1)[:, None] * b[None, :]) / 4.0
    psi = 2.0 * math.pi / LANES * (b[:, None] * b[None, :] % LANES)
    outer_high, outer_low = halves(np.concatenate([np.cos(theta), -np.sin(theta)], axis=0))
    outer = np.concatenate([outer_high, outer_high, outer_low], axis=1)
    back = np.concatenate([np.cos(theta).T, -np.sin(theta).T], axis=1) / full_len
    back_high, back_low = halves(back)
    outer_back = np.concatenate([back_high, back_high, back_low], axis=1)
    twiddle = np.stack([np.cos(phi), np.sin(phi)]).astype(np.float32)
    cos_in, sin_in = np.cos(psi), np.sin(psi)
    inner = np.stack(halves(np.block([[cos_in, -sin_in], [sin_in, cos_in]])))
    inner_back = np.stack(halves(np.block([[cos_in, sin_in], [-sin_in, cos_in]])))
    return outer, twiddle, inner, inner_back, outer_back


def sine_fit(terms):
    nodes = np.cos((np.arange(400) + 0.5) * math.pi / 400) * 0.5
    basis = np.stack([nodes ** (2 * p + 1) for p in range(terms)], axis=1)
    fit = np.linalg.lstsq(basis, np.sin(2.0 * math.pi * nodes), rcond=None)[0]
    return [float(v) for v in fit]


SINE_FIT = sine_fit(7)


def sine_of_turns(turns):
    part = turns - jnp.round(turns)
    square = part * part
    value = SINE_FIT[-1]
    for term in SINE_FIT[-2::-1]:
        value = value * square + term
    return value * part


def split_two(vals):
    high = vals.astype(BF16)
    return high, (vals - high.astype(F32)).astype(BF16)


def split_three(vals):
    first = vals.astype(BF16).astype(F32)
    rest = vals - first
    second = rest.astype(BF16).astype(F32)
    return first, second, rest - second


def matmul(lhs, rhs):
    return jnp.dot(lhs, rhs, preferred_element_type=F32)


def stack_three(vals):
    high, low = split_two(vals)
    return jnp.concatenate([high, low, high], axis=0)


def inner_product(vals, table_ref):
    high, low = split_two(vals)
    return (
        matmul(high, table_ref[0]) + matmul(low, table_ref[0]) + matmul(high, table_ref[1])
    )


def forward(columns, outer_ref, twiddle_ref, inner_ref):
    blocks = columns[0].shape[0]
    mixed = matmul(outer_ref[...], stack_three(jnp.concatenate(columns, axis=1)))
    cos_vals, sin_vals = twiddle_ref[0], twiddle_ref[1]
    rows = []
    for c in range(len(columns)):
        real = mixed[:blocks, c * LANES : (c + 1) * LANES]
        imag = mixed[blocks:, c * LANES : (c + 1) * LANES]
        rows.append(
            jnp.concatenate(
                [real * cos_vals + imag * sin_vals, imag * cos_vals - real * sin_vals], axis=1
            )
        )
    return inner_product(jnp.concatenate(rows, axis=0), inner_ref)


def backward(spectrum, channels, inner_back_ref, twiddle_ref, outer_back_ref):
    vals = inner_product(spectrum, inner_back_ref)
    blocks = vals.shape[0] // channels
    cos_vals, sin_vals = twiddle_ref[0], twiddle_ref[1]
    columns = []
    for c in range(channels):
        real = vals[c * blocks : (c + 1) * blocks, :LANES]
        imag = vals[c * blocks : (c + 1) * blocks, LANES:]
        columns.append(
            jnp.concatenate(
                [real * cos_vals - imag * sin_vals, imag * cos_vals + real * sin_vals], axis=0
            )
        )
    return matmul(outer_back_ref[...], stack_three(jnp.concatenate(columns, axis=1)))


def pack_kernel(signal_ref, in_gate_ref, parts_ref, sems):
    copies = [
        pltpu.make_async_copy(ref, parts_ref.at[:, i], sems.at[i])
        for i, ref in enumerate((signal_ref, in_gate_ref))
    ]
    for copy in copies:
        copy.start()
    for copy in copies:
        copy.wait()


def filter_kernel(
    own,
    embed_hbm,
    embed_weight_hbm,
    embed_bias_hbm,
    sine_freq_hbm,
    mid_weight_hbm,
    mid_bias_hbm,
    out_weight_hbm,
    decay_hbm,
    skip_hbm,
    taps_hbm,
    outer_hbm,
    twiddle_hbm,
    inner_hbm,
    inner_back_hbm,
    outer_back_hbm,
    spectrum_ref,
    toeplitz_ref,
    skip_ref,
    outer_ref,
    twiddle_ref,
    inner_ref,
    inner_back_ref,
    outer_back_ref,
    embed_ref,
    embed_weight_ref,
    embed_bias_ref,
    sine_freq_ref,
    mid_weight_ref,
    mid_bias_ref,
    out_weight_ref,
    decay_ref,
    skip_row_ref,
    taps_ref,
    pad_ref,
    vec_ref,
    row_ref,
    column_ref,
    out_rows_ref,
    filter_ref,
    sems,
    embed_sems,
):
    full_len = embed_ref.shape[1]
    tile_len = full_len // TILES
    hidden = mid_weight_ref.shape[0]
    pairs = [
        (embed_weight_hbm, embed_weight_ref),
        (embed_bias_hbm, embed_bias_ref),
        (sine_freq_hbm, sine_freq_ref),
        (mid_weight_hbm, mid_weight_ref),
        (mid_bias_hbm, mid_bias_ref),
        (out_weight_hbm, out_weight_ref),
        (decay_hbm, decay_ref),
        (skip_hbm, skip_row_ref),
        (taps_hbm, taps_ref),
        (outer_hbm, outer_ref),
        (twiddle_hbm, twiddle_ref),
        (inner_hbm, inner_ref),
        (inner_back_hbm, inner_back_ref),
        (outer_back_hbm, outer_back_ref),
    ]
    copies = [pltpu.make_async_copy(*pair, sems.at[i]) for i, pair in enumerate(pairs)]
    embed_copies = []
    for i in range(TILES):
        lanes = pl.ds(i * tile_len, tile_len)
        embed_copies.append(
            pltpu.make_async_copy(
                embed_hbm.at[:, lanes], embed_ref.at[:, lanes], embed_sems.at[i]
            )
        )
    for copy in copies[:8] + embed_copies + copies[8:]:
        copy.start()
    first_channel = pl.multiple_of(lax.axis_index("seq") * own, own)
    pad_ref[...] = jnp.zeros_like(pad_ref)
    vec_ref[...] = jnp.zeros_like(vec_ref)
    row_ref[...] = jnp.zeros_like(row_ref)
    for copy in copies[:8]:
        copy.wait()

    freq = sine_freq_ref[...] * (0.5 / math.pi)
    features = embed_weight_ref.shape[0]
    pad_ref[:features, :] = embed_weight_ref[...] * freq
    pad_ref[features : features + 1, :] = embed_bias_ref[...] * freq
    one, two, three = split_three(pad_ref[...])
    none = jnp.zeros_like(one)
    rest = jnp.zeros((embed_ref.shape[0] - 3 * one.shape[0], hidden), F32)
    weight_one = jnp.concatenate(
        [
            jnp.concatenate([one, one, one, rest], axis=0).T,
            jnp.concatenate([two, two, none, rest], axis=0).T,
            jnp.concatenate([three, none, none, rest], axis=0).T,
        ],
        axis=0,
    ).astype(BF16)
    one, two, _ = split_three(mid_weight_ref[...] * freq)
    weight_two = jnp.concatenate(
        [jnp.concatenate([one, one], axis=0).T, jnp.concatenate([two, two], axis=0).T], axis=0
    ).astype(BF16)
    vec_ref[0:1, :] = mid_bias_ref[...] * freq
    bias_two = vec_ref[...].T[:, 0:1]
    one, two, _ = split_three(out_weight_ref[...])
    out_rows_ref[0] = jnp.concatenate([one, one], axis=0).T
    out_rows_ref[1] = jnp.concatenate([two, two], axis=0).T
    own_rows = pl.ds(first_channel, own)
    weight_three = jnp.concatenate(
        [out_rows_ref[0, own_rows, :], out_rows_ref[1, own_rows, :]], axis=0
    ).astype(BF16)
    row_ref[0:1, :] = decay_ref[...]
    row_ref[1:2, :] = skip_row_ref[...]
    column_ref[...] = row_ref[...].T
    decay = column_ref[own_rows, 0:1]
    skip_ref[...] = jnp.broadcast_to(column_ref[own_rows, 1:2], skip_ref.shape)
    scale = jnp.sqrt(2.0 * decay)

    for i in range(TILES):
        start = i * tile_len
        embed_copies[i].wait()
        turns = matmul(weight_one, embed_ref[:, start : start + tile_len])
        first = sine_of_turns(
            turns[:hidden] + turns[hidden : 2 * hidden] + turns[2 * hidden :]
        )
        turns = matmul(weight_two, jnp.concatenate(split_two(first), axis=0))
        second = sine_of_turns(turns[:hidden] + turns[hidden:] + bias_two)
        raw = matmul(weight_three, jnp.concatenate(split_two(second), axis=0))
        positions = (start + lax.broadcasted_iota(jnp.int32, (own, tile_len), 1)).astype(F32)
        vals = (raw[:own] + raw[own:]) * (scale * jnp.exp(-decay * positions))
        for j in range(tile_len // LANES):
            row = (start // LANES + j) * own
            filter_ref[row : row + own, :] = vals[:, j * LANES : (j + 1) * LANES]

    for copy in copies[8:]:
        copy.wait()
    blocks = full_len // LANES
    columns = [filter_ref[pl.ds(c, blocks, stride=own), :] for c in range(own)]
    spectrum_ref[...] = forward(columns, outer_ref, twiddle_ref, inner_ref)
    taps = taps_ref[own_rows, :]
    tap_count = taps.shape[1]
    square = (tap_count, tap_count)
    upper = lax.broadcasted_iota(jnp.int32, square, 1) >= lax.broadcasted_iota(
        jnp.int32, square, 0
    )
    for c in range(own):
        lags = pltpu.roll(
            jnp.broadcast_to(taps[c : c + 1], square), 0, 1, stride=1, stride_axis=0
        )
        high, low = split_two(
            jnp.concatenate([jnp.where(upper, 0.0, lags), jnp.where(upper, lags, 0.0)], axis=0)
        )
        toeplitz_ref[c] = jnp.concatenate([high, low], axis=1)


def mix_kernel(
    own,
    parts_ref,
    spectrum_ref,
    toeplitz_ref,
    skip_ref,
    outer_ref,
    twiddle_ref,
    inner_ref,
    inner_back_ref,
    outer_back_ref,
    out_ref,
    signal_ref,
    in_gate_ref,
    mixed_ref,
):
    seq_devs, _, _, local_len = parts_ref.shape
    local_blocks = local_len // LANES
    part_rows = local_blocks * own
    blocks = seq_devs * local_blocks
    signal_ref[:own, :] = jnp.zeros((own, LANES), F32)
    for p in range(seq_devs):
        for q in range(local_blocks):
            at = p * part_rows + q * own
            lanes = slice(q * LANES, (q + 1) * LANES)
            signal_ref[own + at : 2 * own + at, :] = parts_ref[p, 0, :, lanes].astype(F32)
            in_gate_ref[at : at + own, :] = parts_ref[p, 1, :, lanes].astype(F32)
    gated = []
    for c in range(own):
        window = jnp.concatenate(
            [
                signal_ref[pl.ds(c, blocks, stride=own), :],
                signal_ref[pl.ds(own + c, blocks, stride=own), :],
            ],
            axis=1,
        ).astype(BF16)
        both = matmul(window, toeplitz_ref[c])
        gated.append(
            in_gate_ref[pl.ds(c, blocks, stride=own), :] * (both[:, :LANES] + both[:, LANES:])
        )
    vals = forward(gated, outer_ref, twiddle_ref, inner_ref)
    real, imag = vals[:, :LANES], vals[:, LANES:]
    filt_real, filt_imag = spectrum_ref[:, :LANES], spectrum_ref[:, LANES:]
    product = jnp.concatenate(
        [real * filt_real - imag * filt_imag, real * filt_imag + imag * filt_real], axis=1
    )
    conv = backward(product, own, inner_back_ref, twiddle_ref, outer_back_ref)
    for c in range(own):
        mixed_ref[pl.ds(c, blocks, stride=own), :] = (
            conv[:, c * LANES : (c + 1) * LANES] + skip_ref[c : c + 1, :] * gated[c]
        )
    for q in range(local_blocks):
        if own % 8 == 0:
            column = jnp.concatenate(
                [
                    mixed_ref[p * part_rows + q * own : p * part_rows + (q + 1) * own, :]
                    for p in range(seq_devs)
                ],
                axis=0,
            )
            out_ref[:, q * LANES : (q + 1) * LANES] = column
        else:
            for c in range(own):
                signal_ref[pl.ds(c, seq_devs, stride=own), :] = mixed_ref[
                    pl.ds(q * own + c, seq_devs, stride=part_rows), :
                ]
            out_ref[:, q * LANES : (q + 1) * LANES] = signal_ref[: seq_devs * own, :]


def pack(parts, seq_devs, own):
    local_len = parts[0].shape[1]
    hbm = pl.BlockSpec(memory_space=pltpu.HBM)
    return pl.pallas_call(
        pack_kernel,
        out_shape=pltpu.VMEM((seq_devs, 2, own, local_len), BF16),
        in_specs=[hbm] * 2,
        out_specs=pl.BlockSpec(memory_space=pltpu.VMEM),
        scratch_shapes=[pltpu.SemaphoreType.DMA((2,))],
    )(*[in_space(part.reshape(seq_devs, own, local_len), pltpu.HBM) for part in parts])


def make_filter(params, own, full_len):
    blocks = full_len // LANES
    hidden, channels = params[5].shape
    tap_count = params[8].shape[1]
    embed = embed_table(full_len)
    tables = transform_tables(full_len)
    operands = (embed,) + params + tables
    padded = round_up(params[0].shape[0] + 1, 8)
    return pl.pallas_call(
        functools.partial(filter_kernel, own),
        out_shape=(
            pltpu.VMEM((own * blocks, 2 * LANES), F32),
            pltpu.VMEM((own, 2 * tap_count, 2 * tap_count), BF16),
            pltpu.VMEM((own, LANES), F32),
        )
        + tuple(pltpu.VMEM(table.shape, table.dtype) for table in tables),
        in_specs=[pl.BlockSpec(memory_space=pltpu.HBM)] * len(operands),
        out_specs=(pl.BlockSpec(memory_space=pltpu.VMEM),) * (3 + len(tables)),
        scratch_shapes=[pltpu.VMEM(embed.shape, BF16)]
        + [pltpu.VMEM(vals.shape, F32) for vals in params]
        + [
            pltpu.VMEM((padded, hidden), F32),
            pltpu.VMEM((8, hidden), F32),
            pltpu.VMEM((8, channels), F32),
            pltpu.VMEM((channels, 8), F32),
            pltpu.VMEM((2, channels, 2 * hidden), F32),
            pltpu.VMEM((blocks * own, LANES), F32),
            pltpu.SemaphoreType.DMA((len(operands) - 1,)),
            pltpu.SemaphoreType.DMA((TILES,)),
        ],
        compiler_params=pltpu.CompilerParams(vmem_limit_bytes=48 * 2**20),
    )(*[in_space(jnp.asarray(vals), pltpu.HBM) for vals in operands])


def mix(parts, shared):
    seq_devs, _, own, local_len = parts.shape
    rows = seq_devs * own * (local_len // LANES)
    vmem = pl.BlockSpec(memory_space=pltpu.VMEM)
    return pl.pallas_call(
        functools.partial(mix_kernel, own),
        out_shape=jax.ShapeDtypeStruct((seq_devs * own, local_len), F32),
        in_specs=[vmem] * (1 + len(shared)),
        out_specs=vmem,
        scratch_shapes=[pltpu.VMEM((rows + own, LANES), F32)]
        + [pltpu.VMEM((rows, LANES), F32)] * 2,
        compiler_params=pltpu.CompilerParams(vmem_limit_bytes=48 * 2**20),
    )(parts, *[in_space(vals, pltpu.VMEM) for vals in shared])


def on_device(
    signal,
    in_gate,
    out_gate,
    short_taps,
    skip_gain,
    decay_rate,
    embed_weight,
    embed_bias,
    sine_freq,
    mid_weight,
    mid_bias,
    out_weight,
):
    channels, local_len = signal.shape
    seq_devs = lax.axis_size("seq")
    own = -(-channels // seq_devs)
    spare = own * seq_devs - channels
    parts = [signal, in_gate]
    if spare:
        parts = [jnp.pad(part, ((0, spare), (0, 0))) for part in parts]
        short_taps = jnp.pad(short_taps, ((0, spare), (0, 0)))
        skip_gain = jnp.pad(skip_gain, (0, spare))
        decay_rate = jnp.pad(decay_rate, (0, spare), mode="edge")
        out_weight = jnp.pad(out_weight, ((0, 0), (0, spare)))
    parts = pack(parts, seq_devs, own)
    parts = lax.all_to_all(parts, "seq", split_axis=0, concat_axis=0, tiled=True)
    params = (
        embed_weight,
        embed_bias[None, :],
        sine_freq[None, :],
        mid_weight,
        mid_bias[None, :],
        out_weight,
        decay_rate[None, :],
        skip_gain[None, :],
        short_taps,
    )
    shared = make_filter(params, own, seq_devs * local_len)
    mixed = mix(parts, shared)
    mixed = lax.all_to_all(mixed, "seq", split_axis=0, concat_axis=0, tiled=True)[:channels]
    return (out_gate.astype(F32) * mixed).astype(BF16)


def solution(mesh):
    in_specs = (
        P("ch", "seq"),
        P("ch", "seq"),
        P("ch", "seq"),
        P("ch", None),
        P("ch"),
        P("ch"),
        P(),
        P(),
        P(),
        P(),
        P(),
        P(None, "ch"),
    )
    out_specs = P("ch", "seq")
    return jax.shard_map(
        on_device, mesh=mesh, in_specs=in_specs, out_specs=out_specs, check_vma=False
    )
```

```python
import functools
import math

import jax
import jax.numpy as jnp
import numpy as np
from jax import lax
from jax.experimental import pallas as pl
from jax.experimental.pallas import tpu as pltpu
from jax.sharding import PartitionSpec as P

BANDS = 16
LANES = 128
TILES = 4
LEVEL_BITS = 6
LEVELS = 2**LEVEL_BITS
F32 = jnp.float32
BF16 = jnp.bfloat16
in_space = pltpu.with_memory_space_constraint


def round_up(count, step):
    return (count + step - 1) // step * step


def halves(table):
    high = table.astype(BF16)
    low = (table - high.astype(np.float64)).astype(BF16)
    return high, low


@functools.lru_cache(maxsize=None)
def embed_table(full_len):
    positions = np.arange(full_len, dtype=np.int64)
    rows = [positions / full_len]
    phase = positions
    for _ in range(BANDS):
        angle = phase * (2.0 * math.pi / full_len)
        rows += [np.cos(angle), np.sin(angle)]
        phase = 2 * phase % full_len
    rows.append(np.ones(full_len))
    table = np.zeros((round_up(len(rows), 8), full_len))
    table[: len(rows)] = np.stack(rows)
    first, rest = halves(table)
    second, third = halves(table - first.astype(np.float64))
    stacked = np.concatenate([first, second, third], axis=0)
    return np.pad(stacked, ((0, -len(stacked) % 16), (0, 0)))


@functools.lru_cache(maxsize=None)
def transform_tables(full_len):
    blocks = full_len // LANES
    a = np.arange(blocks)
    k1 = np.arange(blocks)
    b = np.arange(LANES)
    theta = 2.0 * math.pi / blocks * ((4 * k1 + 1)[:, None] * a[None, :] % (4 * blocks)) / 4.0
    phi = 2.0 * math.pi / full_len * ((4 * k1 + 1)[:, None] * b[None, :]) / 4.0
    psi = 2.0 * math.pi / LANES * (b[:, None] * b[None, :] % LANES)
    outer_high, outer_low = halves(np.concatenate([np.cos(theta), -np.sin(theta)], axis=0))
    outer = np.concatenate([outer_high, outer_high, outer_low], axis=1)
    back = np.concatenate([np.cos(theta).T, -np.sin(theta).T], axis=1) / full_len
    back_high, back_low = halves(back)
    outer_back = np.concatenate([back_high, back_high, back_low], axis=1)
    twiddle = np.stack([np.cos(phi), np.sin(phi)]).astype(np.float32)
    cos_in, sin_in = np.cos(psi), np.sin(psi)
    inner = np.stack(halves(np.block([[cos_in, -sin_in], [sin_in, cos_in]])))
    inner_back = np.stack(halves(np.block([[cos_in, sin_in], [-sin_in, cos_in]])))
    return outer, twiddle, inner, inner_back, outer_back


def sine_fit(terms):
    nodes = np.cos((np.arange(400) + 0.5) * math.pi / 400) * 0.5
    basis = np.stack([nodes ** (2 * p + 1) for p in range(terms)], axis=1)
    fit = np.linalg.lstsq(basis, np.sin(2.0 * math.pi * nodes), rcond=None)[0]
    return [float(v) for v in fit]


SINE_FIT = sine_fit(7)


def sine_of_turns(turns):
    part = turns - jnp.round(turns)
    square = part * part
    value = SINE_FIT[-1]
    for term in SINE_FIT[-2::-1]:
        value = value * square + term
    return value * part


def split_two(vals):
    high = vals.astype(BF16)
    return high, (vals - high.astype(F32)).astype(BF16)


def split_three(vals):
    first = vals.astype(BF16).astype(F32)
    rest = vals - first
    second = rest.astype(BF16).astype(F32)
    return first, second, rest - second


def matmul(lhs, rhs):
    return jnp.dot(lhs, rhs, preferred_element_type=F32)


def stack_three(vals):
    high, low = split_two(vals)
    return jnp.concatenate([high, low, high], axis=0)


def inner_product(vals, table_ref):
    high, low = split_two(vals)
    return (
        matmul(high, table_ref[0]) + matmul(low, table_ref[0]) + matmul(high, table_ref[1])
    )


def forward(columns, outer_ref, twiddle_ref, inner_ref):
    blocks = columns[0].shape[0]
    mixed = matmul(outer_ref[...], stack_three(jnp.concatenate(columns, axis=1)))
    cos_vals, sin_vals = twiddle_ref[0], twiddle_ref[1]
    rows = []
    for c in range(len(columns)):
        real = mixed[:blocks, c * LANES : (c + 1) * LANES]
        imag = mixed[blocks:, c * LANES : (c + 1) * LANES]
        rows.append(
            jnp.concatenate(
                [real * cos_vals + imag * sin_vals, imag * cos_vals - real * sin_vals], axis=1
            )
        )
    return inner_product(jnp.concatenate(rows, axis=0), inner_ref)


def backward(spectrum, channels, inner_back_ref, twiddle_ref, outer_back_ref):
    vals = inner_product(spectrum, inner_back_ref)
    blocks = vals.shape[0] // channels
    cos_vals, sin_vals = twiddle_ref[0], twiddle_ref[1]
    columns = []
    for c in range(channels):
        real = vals[c * blocks : (c + 1) * blocks, :LANES]
        imag = vals[c * blocks : (c + 1) * blocks, LANES:]
        columns.append(
            jnp.concatenate(
                [real * cos_vals - imag * sin_vals, imag * cos_vals + real * sin_vals], axis=0
            )
        )
    return matmul(outer_back_ref[...], stack_three(jnp.concatenate(columns, axis=1)))


def step_of(high):
    size = jnp.abs(high)
    return jnp.maximum(lax.reduce_precision(size * (1.0 + 0.75 / 128), 8, 7) - size, 1e-30)


def rest_level(vals, high):
    level = jnp.floor(((vals - high) / step_of(high) + 0.5) * LEVELS)
    return jnp.clip(level, 0.0, LEVELS - 1.0).astype(jnp.int32)


def pair_code(one, two):
    index = one * LEVELS + two
    size = jnp.left_shift(128 + (index & 127), (index >> 7) & 15).astype(F32)
    return jnp.where(index >= 2048, -size, size)


def pair_levels(code):
    size = jnp.abs(code).astype(jnp.int32)
    index = jnp.where(code < 0, 2048, 0)
    for shift in (8, 4, 2, 1):
        more = size >= (128 << shift)
        size = jnp.where(more, size >> shift, size)
        index = jnp.where(more, index + shift * 128, index)
    index = index + size - 128
    return index >> LEVEL_BITS, index & (LEVELS - 1)


def gate(coded, out_gate):
    local_len = out_gate.shape[1]
    half = local_len // 2
    parts = []
    for start, level in zip((0, half), pair_levels(coded[:, local_len:].astype(F32))):
        high = coded[:, start : start + half].astype(F32)
        vals = high + step_of(high) * ((level.astype(F32) + 0.5) * (1.0 / LEVELS) - 0.5)
        parts.append((out_gate[:, start : start + half].astype(F32) * vals).astype(BF16))
    return jnp.concatenate(parts, axis=1)


def pack_kernel(signal_ref, in_gate_ref, parts_ref, sems):
    copies = [
        pltpu.make_async_copy(ref, parts_ref.at[:, i], sems.at[i])
        for i, ref in enumerate((signal_ref, in_gate_ref))
    ]
    for copy in copies:
        copy.start()
    for copy in copies:
        copy.wait()


def filter_kernel(
    own,
    embed_hbm,
    embed_weight_hbm,
    embed_bias_hbm,
    sine_freq_hbm,
    mid_weight_hbm,
    mid_bias_hbm,
    out_weight_hbm,
    decay_hbm,
    skip_hbm,
    taps_hbm,
    outer_hbm,
    twiddle_hbm,
    inner_hbm,
    inner_back_hbm,
    outer_back_hbm,
    spectrum_ref,
    toeplitz_ref,
    skip_ref,
    outer_ref,
    twiddle_ref,
    inner_ref,
    inner_back_ref,
    outer_back_ref,
    embed_ref,
    embed_weight_ref,
    embed_bias_ref,
    sine_freq_ref,
    mid_weight_ref,
    mid_bias_ref,
    out_weight_ref,
    decay_ref,
    skip_row_ref,
    taps_ref,
    pad_ref,
    vec_ref,
    row_ref,
    column_ref,
    out_rows_ref,
    filter_ref,
    sems,
    embed_sems,
):
    full_len = embed_ref.shape[1]
    tile_len = full_len // TILES
    hidden = mid_weight_ref.shape[0]
    pairs = [
        (embed_weight_hbm, embed_weight_ref),
        (embed_bias_hbm, embed_bias_ref),
        (sine_freq_hbm, sine_freq_ref),
        (mid_weight_hbm, mid_weight_ref),
        (mid_bias_hbm, mid_bias_ref),
        (out_weight_hbm, out_weight_ref),
        (decay_hbm, decay_ref),
        (skip_hbm, skip_row_ref),
        (taps_hbm, taps_ref),
        (outer_hbm, outer_ref),
        (twiddle_hbm, twiddle_ref),
        (inner_hbm, inner_ref),
        (inner_back_hbm, inner_back_ref),
        (outer_back_hbm, outer_back_ref),
    ]
    copies = [pltpu.make_async_copy(*pair, sems.at[i]) for i, pair in enumerate(pairs)]
    embed_copies = []
    for i in range(TILES):
        lanes = pl.ds(i * tile_len, tile_len)
        embed_copies.append(
            pltpu.make_async_copy(
                embed_hbm.at[:, lanes], embed_ref.at[:, lanes], embed_sems.at[i]
            )
        )
    for copy in copies[:8] + embed_copies + copies[8:]:
        copy.start()
    first_channel = pl.multiple_of(lax.axis_index("seq") * own, own)
    pad_ref[...] = jnp.zeros_like(pad_ref)
    vec_ref[...] = jnp.zeros_like(vec_ref)
    row_ref[...] = jnp.zeros_like(row_ref)
    for copy in copies[:8]:
        copy.wait()

    freq = sine_freq_ref[...] * (0.5 / math.pi)
    features = embed_weight_ref.shape[0]
    pad_ref[:features, :] = embed_weight_ref[...] * freq
    pad_ref[features : features + 1, :] = embed_bias_ref[...] * freq
    one, two, three = split_three(pad_ref[...])
    none = jnp.zeros_like(one)
    rest = jnp.zeros((embed_ref.shape[0] - 3 * one.shape[0], hidden), F32)
    weight_one = jnp.concatenate(
        [
            jnp.concatenate([one, one, one, rest], axis=0).T,
            jnp.concatenate([two, two, none, rest], axis=0).T,
            jnp.concatenate([three, none, none, rest], axis=0).T,
        ],
        axis=0,
    ).astype(BF16)
    one, two, _ = split_three(mid_weight_ref[...] * freq)
    weight_two = jnp.concatenate(
        [jnp.concatenate([one, one], axis=0).T, jnp.concatenate([two, two], axis=0).T], axis=0
    ).astype(BF16)
    vec_ref[0:1, :] = mid_bias_ref[...] * freq
    bias_two = vec_ref[...].T[:, 0:1]
    one, two, _ = split_three(out_weight_ref[...])
    out_rows_ref[0] = jnp.concatenate([one, one], axis=0).T
    out_rows_ref[1] = jnp.concatenate([two, two], axis=0).T
    own_rows = pl.ds(first_channel, own)
    weight_three = jnp.concatenate(
        [out_rows_ref[0, own_rows, :], out_rows_ref[1, own_rows, :]], axis=0
    ).astype(BF16)
    row_ref[0:1, :] = decay_ref[...]
    row_ref[1:2, :] = skip_row_ref[...]
    column_ref[...] = row_ref[...].T
    decay = column_ref[own_rows, 0:1]
    skip_ref[...] = jnp.broadcast_to(column_ref[own_rows, 1:2], skip_ref.shape)
    scale = jnp.sqrt(2.0 * decay)

    for i in range(TILES):
        start = i * tile_len
        embed_copies[i].wait()
        turns = matmul(weight_one, embed_ref[:, start : start + tile_len])
        first = sine_of_turns(
            turns[:hidden] + turns[hidden : 2 * hidden] + turns[2 * hidden :]
        )
        turns = matmul(weight_two, jnp.concatenate(split_two(first), axis=0))
        second = sine_of_turns(turns[:hidden] + turns[hidden:] + bias_two)
        raw = matmul(weight_three, jnp.concatenate(split_two(second), axis=0))
        positions = (start + lax.broadcasted_iota(jnp.int32, (own, tile_len), 1)).astype(F32)
        vals = (raw[:own] + raw[own:]) * (scale * jnp.exp(-decay * positions))
        for j in range(tile_len // LANES):
            row = (start // LANES + j) * own
            filter_ref[row : row + own, :] = vals[:, j * LANES : (j + 1) * LANES]

    for copy in copies[8:]:
        copy.wait()
    blocks = full_len // LANES
    columns = [filter_ref[pl.ds(c, blocks, stride=own), :] for c in range(own)]
    spectrum_ref[...] = forward(columns, outer_ref, twiddle_ref, inner_ref)
    taps = taps_ref[own_rows, :]
    tap_count = taps.shape[1]
    square = (tap_count, tap_count)
    upper = lax.broadcasted_iota(jnp.int32, square, 1) >= lax.broadcasted_iota(
        jnp.int32, square, 0
    )
    for c in range(own):
        lags = pltpu.roll(
            jnp.broadcast_to(taps[c : c + 1], square), 0, 1, stride=1, stride_axis=0
        )
        high, low = split_two(
            jnp.concatenate([jnp.where(upper, 0.0, lags), jnp.where(upper, lags, 0.0)], axis=0)
        )
        toeplitz_ref[c] = jnp.concatenate([high, low], axis=1)


def mix_kernel(
    own,
    parts_ref,
    spectrum_ref,
    toeplitz_ref,
    skip_ref,
    outer_ref,
    twiddle_ref,
    inner_ref,
    inner_back_ref,
    outer_back_ref,
    out_ref,
    signal_ref,
    in_gate_ref,
    mixed_ref,
):
    seq_devs, _, _, local_len = parts_ref.shape
    local_blocks = local_len // LANES
    part_rows = local_blocks * own
    blocks = seq_devs * local_blocks
    signal_ref[:own, :] = jnp.zeros((own, LANES), F32)
    for p in range(seq_devs):
        for q in range(local_blocks):
            at = p * part_rows + q * own
            lanes = slice(q * LANES, (q + 1) * LANES)
            signal_ref[own + at : 2 * own + at, :] = parts_ref[p, 0, :, lanes].astype(F32)
            in_gate_ref[at : at + own, :] = parts_ref[p, 1, :, lanes].astype(F32)
    gated = []
    for c in range(own):
        window = jnp.concatenate(
            [
                signal_ref[pl.ds(c, blocks, stride=own), :],
                signal_ref[pl.ds(own + c, blocks, stride=own), :],
            ],
            axis=1,
        ).astype(BF16)
        both = matmul(window, toeplitz_ref[c])
        gated.append(
            in_gate_ref[pl.ds(c, blocks, stride=own), :] * (both[:, :LANES] + both[:, LANES:])
        )
    vals = forward(gated, outer_ref, twiddle_ref, inner_ref)
    real, imag = vals[:, :LANES], vals[:, LANES:]
    filt_real, filt_imag = spectrum_ref[:, :LANES], spectrum_ref[:, LANES:]
    product = jnp.concatenate(
        [real * filt_real - imag * filt_imag, real * filt_imag + imag * filt_real], axis=1
    )
    conv = backward(product, own, inner_back_ref, twiddle_ref, outer_back_ref)
    for c in range(own):
        mixed_ref[pl.ds(c, blocks, stride=own), :] = (
            conv[:, c * LANES : (c + 1) * LANES] + skip_ref[c : c + 1, :] * gated[c]
        )
    columns = []
    for q in range(local_blocks):
        if own % 8 == 0:
            column = jnp.concatenate(
                [
                    mixed_ref[p * part_rows + q * own : p * part_rows + (q + 1) * own, :]
                    for p in range(seq_devs)
                ],
                axis=0,
            )
        else:
            for c in range(own):
                signal_ref[pl.ds(c, seq_devs, stride=own), :] = mixed_ref[
                    pl.ds(q * own + c, seq_devs, stride=part_rows), :
                ]
            column = signal_ref[: seq_devs * own, :]
        high = column.astype(BF16)
        out_ref[:, q * LANES : (q + 1) * LANES] = high
        columns.append(rest_level(column, high.astype(F32)))
    for q in range(local_blocks // 2):
        code = pair_code(columns[q], columns[q + local_blocks // 2]).astype(BF16)
        out_ref[:, local_len + q * LANES : local_len + (q + 1) * LANES] = code


def pack(parts, seq_devs, own):
    local_len = parts[0].shape[1]
    hbm = pl.BlockSpec(memory_space=pltpu.HBM)
    return pl.pallas_call(
        pack_kernel,
        out_shape=pltpu.VMEM((seq_devs, 2, own, local_len), BF16),
        in_specs=[hbm] * 2,
        out_specs=pl.BlockSpec(memory_space=pltpu.VMEM),
        scratch_shapes=[pltpu.SemaphoreType.DMA((2,))],
    )(*[in_space(part.reshape(seq_devs, own, local_len), pltpu.HBM) for part in parts])


def make_filter(params, own, full_len):
    blocks = full_len // LANES
    hidden, channels = params[5].shape
    tap_count = params[8].shape[1]
    embed = embed_table(full_len)
    tables = transform_tables(full_len)
    operands = (embed,) + params + tables
    padded = round_up(params[0].shape[0] + 1, 8)
    return pl.pallas_call(
        functools.partial(filter_kernel, own),
        out_shape=(
            pltpu.VMEM((own * blocks, 2 * LANES), F32),
            pltpu.VMEM((own, 2 * tap_count, 2 * tap_count), BF16),
            pltpu.VMEM((own, LANES), F32),
        )
        + tuple(pltpu.VMEM(table.shape, table.dtype) for table in tables),
        in_specs=[pl.BlockSpec(memory_space=pltpu.HBM)] * len(operands),
        out_specs=(pl.BlockSpec(memory_space=pltpu.VMEM),) * (3 + len(tables)),
        scratch_shapes=[pltpu.VMEM(embed.shape, BF16)]
        + [pltpu.VMEM(vals.shape, F32) for vals in params]
        + [
            pltpu.VMEM((padded, hidden), F32),
            pltpu.VMEM((8, hidden), F32),
            pltpu.VMEM((8, channels), F32),
            pltpu.VMEM((channels, 8), F32),
            pltpu.VMEM((2, channels, 2 * hidden), F32),
            pltpu.VMEM((blocks * own, LANES), F32),
            pltpu.SemaphoreType.DMA((len(operands) - 1,)),
            pltpu.SemaphoreType.DMA((TILES,)),
        ],
        compiler_params=pltpu.CompilerParams(vmem_limit_bytes=48 * 2**20),
    )(*[in_space(jnp.asarray(vals), pltpu.HBM) for vals in operands])


def mix(parts, shared):
    seq_devs, _, own, local_len = parts.shape
    rows = seq_devs * own * (local_len // LANES)
    vmem = pl.BlockSpec(memory_space=pltpu.VMEM)
    return pl.pallas_call(
        functools.partial(mix_kernel, own),
        out_shape=jax.ShapeDtypeStruct((seq_devs * own, local_len * 3 // 2), BF16),
        in_specs=[vmem] * (1 + len(shared)),
        out_specs=vmem,
        scratch_shapes=[pltpu.VMEM((rows + own, LANES), F32)]
        + [pltpu.VMEM((rows, LANES), F32)] * 2,
        compiler_params=pltpu.CompilerParams(vmem_limit_bytes=48 * 2**20),
    )(parts, *[in_space(vals, pltpu.VMEM) for vals in shared])


def on_device(
    signal,
    in_gate,
    out_gate,
    short_taps,
    skip_gain,
    decay_rate,
    embed_weight,
    embed_bias,
    sine_freq,
    mid_weight,
    mid_bias,
    out_weight,
):
    channels, local_len = signal.shape
    seq_devs = lax.axis_size("seq")
    own = -(-channels // seq_devs)
    spare = own * seq_devs - channels
    parts = [signal, in_gate]
    if spare:
        parts = [jnp.pad(part, ((0, spare), (0, 0))) for part in parts]
        short_taps = jnp.pad(short_taps, ((0, spare), (0, 0)))
        skip_gain = jnp.pad(skip_gain, (0, spare))
        decay_rate = jnp.pad(decay_rate, (0, spare), mode="edge")
        out_weight = jnp.pad(out_weight, ((0, 0), (0, spare)))
    parts = pack(parts, seq_devs, own)
    parts = lax.all_to_all(parts, "seq", split_axis=0, concat_axis=0, tiled=True)
    params = (
        embed_weight,
        embed_bias[None, :],
        sine_freq[None, :],
        mid_weight,
        mid_bias[None, :],
        out_weight,
        decay_rate[None, :],
        skip_gain[None, :],
        short_taps,
    )
    shared = make_filter(params, own, seq_devs * local_len)
    mixed = mix(parts, shared)
    coded = lax.all_to_all(mixed, "seq", split_axis=0, concat_axis=0, tiled=True)[:channels]
    return gate(coded, out_gate)


def solution(mesh):
    in_specs = (
        P("ch", "seq"),
        P("ch", "seq"),
        P("ch", "seq"),
        P("ch", None),
        P("ch"),
        P("ch"),
        P(),
        P(),
        P(),
        P(),
        P(),
        P(None, "ch"),
    )
    out_specs = P("ch", "seq")
    return jax.shard_map(
        on_device, mesh=mesh, in_specs=in_specs, out_specs=out_specs, check_vma=False
    )
```

```python
import functools
import math

import jax
import jax.numpy as jnp
import numpy as np
from jax import lax
from jax.experimental import pallas as pl
from jax.experimental.pallas import tpu as pltpu
from jax.sharding import PartitionSpec as P

BANDS = 16
LANES = 128
GROUPS = 4
TILES = 4
LEVEL_BITS = 6
LEVELS = 2**LEVEL_BITS
F32 = jnp.float32
BF16 = jnp.bfloat16
in_space = pltpu.with_memory_space_constraint


def round_up(count, step):
    return (count + step - 1) // step * step


def halves(table):
    high = table.astype(BF16)
    low = (table - high.astype(np.float64)).astype(BF16)
    return high, low


@functools.lru_cache(maxsize=None)
def embed_table(full_len):
    positions = np.arange(full_len, dtype=np.int64)
    rows = [positions / full_len]
    phase = positions
    for _ in range(BANDS):
        angle = phase * (2.0 * math.pi / full_len)
        rows += [np.cos(angle), np.sin(angle)]
        phase = 2 * phase % full_len
    rows.append(np.ones(full_len))
    table = np.zeros((round_up(len(rows), 8), full_len))
    table[: len(rows)] = np.stack(rows)
    first, rest = halves(table)
    second, third = halves(table - first.astype(np.float64))
    stacked = np.concatenate([first, second, third], axis=0)
    return np.pad(stacked, ((0, -len(stacked) % 16), (0, 0)))


@functools.lru_cache(maxsize=None)
def transform_tables(full_len):
    blocks = full_len // LANES
    a = np.arange(blocks)
    k1 = np.arange(blocks)
    b = np.arange(LANES)
    theta = 2.0 * math.pi / blocks * ((4 * k1 + 1)[:, None] * a[None, :] % (4 * blocks)) / 4.0
    phi = 2.0 * math.pi / full_len * ((4 * k1 + 1)[:, None] * b[None, :]) / 4.0
    psi = 2.0 * math.pi / LANES * (b[:, None] * b[None, :] % LANES)
    outer_high, outer_low = halves(np.concatenate([np.cos(theta), -np.sin(theta)], axis=0))
    outer = np.concatenate([outer_high, outer_high, outer_low], axis=1)
    back = np.concatenate([np.cos(theta).T, -np.sin(theta).T], axis=1) / full_len
    back_high, back_low = halves(back)
    outer_back = np.concatenate([back_high, back_high, back_low], axis=1)
    twiddle = np.stack([np.cos(phi), np.sin(phi)]).astype(np.float32)
    cos_in, sin_in = np.cos(psi), np.sin(psi)
    inner = np.stack(halves(np.block([[cos_in, -sin_in], [sin_in, cos_in]])))
    inner_back = np.stack(halves(np.block([[cos_in, sin_in], [-sin_in, cos_in]])))
    return outer, twiddle, inner, inner_back, outer_back


def sine_fit(terms):
    nodes = np.cos((np.arange(400) + 0.5) * math.pi / 400) * 0.5
    basis = np.stack([nodes ** (2 * p + 1) for p in range(terms)], axis=1)
    fit = np.linalg.lstsq(basis, np.sin(2.0 * math.pi * nodes), rcond=None)[0]
    return [float(v) for v in fit]


SINE_FIT = sine_fit(7)


def sine_of_turns(turns):
    part = turns - jnp.round(turns)
    square = part * part
    value = SINE_FIT[-1]
    for term in SINE_FIT[-2::-1]:
        value = value * square + term
    return value * part


def split_two(vals):
    high = vals.astype(BF16)
    return high, (vals - high.astype(F32)).astype(BF16)


def split_three(vals):
    first = vals.astype(BF16).astype(F32)
    rest = vals - first
    second = rest.astype(BF16).astype(F32)
    return first, second, rest - second


def matmul(lhs, rhs):
    return jnp.dot(lhs, rhs, preferred_element_type=F32)


def stack_three(vals):
    high, low = split_two(vals)
    return jnp.concatenate([high, low, high], axis=0)


def inner_product(vals, table_ref):
    high, low = split_two(vals)
    return (
        matmul(high, table_ref[0]) + matmul(low, table_ref[0]) + matmul(high, table_ref[1])
    )


def outer_forward(columns, outer_ref, twiddle_ref):
    blocks = columns[0].shape[0]
    mixed = matmul(outer_ref[...], stack_three(jnp.concatenate(columns, axis=1)))
    cos_vals, sin_vals = twiddle_ref[0], twiddle_ref[1]
    rows = []
    for c in range(len(columns)):
        real = mixed[:blocks, c * LANES : (c + 1) * LANES]
        imag = mixed[blocks:, c * LANES : (c + 1) * LANES]
        rows.append(
            jnp.concatenate(
                [real * cos_vals + imag * sin_vals, imag * cos_vals - real * sin_vals], axis=1
            )
        )
    return rows


def outer_backward(vals, channels, twiddle_ref, outer_back_ref):
    blocks = vals.shape[0] // channels
    cos_vals, sin_vals = twiddle_ref[0], twiddle_ref[1]
    columns = []
    for c in range(channels):
        real = vals[c * blocks : (c + 1) * blocks, :LANES]
        imag = vals[c * blocks : (c + 1) * blocks, LANES:]
        columns.append(
            jnp.concatenate(
                [real * cos_vals - imag * sin_vals, imag * cos_vals + real * sin_vals], axis=0
            )
        )
    return matmul(outer_back_ref[...], stack_three(jnp.concatenate(columns, axis=1)))


def step_of(high):
    size = jnp.abs(high)
    return jnp.maximum(lax.reduce_precision(size * (1.0 + 0.75 / 128), 8, 7) - size, 1e-30)


def rest_level(vals, high):
    level = jnp.floor(((vals - high) / step_of(high) + 0.5) * LEVELS)
    return jnp.clip(level, 0.0, LEVELS - 1.0).astype(jnp.int32)


def pair_code(one, two):
    index = one * LEVELS + two
    size = jnp.left_shift(128 + (index & 127), (index >> 7) & 15).astype(F32)
    return jnp.where(index >= 2048, -size, size)


def pair_levels(code):
    size = jnp.abs(code).astype(jnp.int32)
    index = jnp.where(code < 0, 2048, 0)
    for shift in (8, 4, 2, 1):
        more = size >= (128 << shift)
        size = jnp.where(more, size >> shift, size)
        index = jnp.where(more, index + shift * 128, index)
    index = index + size - 128
    return index >> LEVEL_BITS, index & (LEVELS - 1)


def gate(coded, out_gate):
    local_len = out_gate.shape[1]
    half = local_len // 2
    parts = []
    code = coded[:, local_len:].astype(F32)
    for start, level in zip((0, half), pair_levels(code)):
        high = coded[:, start : start + half].astype(F32)
        vals = high + step_of(high) * ((level.astype(F32) + 0.5) * (1.0 / LEVELS) - 0.5)
        parts.append((out_gate[:, start : start + half].astype(F32) * vals).astype(BF16))
    return jnp.concatenate(parts, axis=1)


def filter_kernel(
    own,
    embed_hbm,
    embed_weight_hbm,
    embed_bias_hbm,
    sine_freq_hbm,
    mid_weight_hbm,
    mid_bias_hbm,
    out_weight_hbm,
    decay_hbm,
    skip_hbm,
    taps_hbm,
    outer_hbm,
    twiddle_hbm,
    inner_hbm,
    inner_back_hbm,
    outer_back_hbm,
    spectrum_ref,
    toeplitz_ref,
    skip_ref,
    outer_ref,
    twiddle_ref,
    inner_ref,
    inner_back_ref,
    outer_back_ref,
    embed_ref,
    embed_weight_ref,
    embed_bias_ref,
    sine_freq_ref,
    mid_weight_ref,
    mid_bias_ref,
    out_weight_ref,
    decay_ref,
    skip_row_ref,
    taps_ref,
    pad_ref,
    vec_ref,
    row_ref,
    column_ref,
    out_rows_ref,
    filter_ref,
    sems,
    embed_sems,
):
    full_len = embed_ref.shape[1]
    tile_len = full_len // TILES
    hidden = mid_weight_ref.shape[0]
    pairs = [
        (embed_weight_hbm, embed_weight_ref),
        (embed_bias_hbm, embed_bias_ref),
        (sine_freq_hbm, sine_freq_ref),
        (mid_weight_hbm, mid_weight_ref),
        (mid_bias_hbm, mid_bias_ref),
        (out_weight_hbm, out_weight_ref),
        (decay_hbm, decay_ref),
        (skip_hbm, skip_row_ref),
        (taps_hbm, taps_ref),
        (outer_hbm, outer_ref),
        (twiddle_hbm, twiddle_ref),
        (inner_hbm, inner_ref),
        (inner_back_hbm, inner_back_ref),
        (outer_back_hbm, outer_back_ref),
    ]
    copies = [pltpu.make_async_copy(*pair, sems.at[i]) for i, pair in enumerate(pairs)]
    embed_copies = []
    for i in range(TILES):
        lanes = pl.ds(i * tile_len, tile_len)
        embed_copies.append(
            pltpu.make_async_copy(
                embed_hbm.at[:, lanes], embed_ref.at[:, lanes], embed_sems.at[i]
            )
        )
    for copy in copies[:8] + embed_copies + copies[8:]:
        copy.start()
    first_channel = pl.multiple_of(lax.axis_index("seq") * own, own)
    pad_ref[...] = jnp.zeros_like(pad_ref)
    vec_ref[...] = jnp.zeros_like(vec_ref)
    row_ref[...] = jnp.zeros_like(row_ref)
    for copy in copies[:8]:
        copy.wait()

    freq = sine_freq_ref[...] * (0.5 / math.pi)
    features = embed_weight_ref.shape[0]
    pad_ref[:features, :] = embed_weight_ref[...] * freq
    pad_ref[features : features + 1, :] = embed_bias_ref[...] * freq
    one, two, three = split_three(pad_ref[...])
    none = jnp.zeros_like(one)
    rest = jnp.zeros((embed_ref.shape[0] - 3 * one.shape[0], hidden), F32)
    weight_one = jnp.concatenate(
        [
            jnp.concatenate([one, one, one, rest], axis=0).T,
            jnp.concatenate([two, two, none, rest], axis=0).T,
            jnp.concatenate([three, none, none, rest], axis=0).T,
        ],
        axis=0,
    ).astype(BF16)
    one, two, _ = split_three(mid_weight_ref[...] * freq)
    weight_two = jnp.concatenate(
        [jnp.concatenate([one, one], axis=0).T, jnp.concatenate([two, two], axis=0).T], axis=0
    ).astype(BF16)
    vec_ref[0:1, :] = mid_bias_ref[...] * freq
    bias_two = vec_ref[...].T[:, 0:1]
    one, two, _ = split_three(out_weight_ref[...])
    out_rows_ref[0] = jnp.concatenate([one, one], axis=0).T
    out_rows_ref[1] = jnp.concatenate([two, two], axis=0).T
    own_rows = pl.ds(first_channel, own)
    weight_three = jnp.concatenate(
        [out_rows_ref[0, own_rows, :], out_rows_ref[1, own_rows, :]], axis=0
    ).astype(BF16)
    row_ref[0:1, :] = decay_ref[...]
    row_ref[1:2, :] = skip_row_ref[...]
    column_ref[...] = row_ref[...].T
    decay = column_ref[own_rows, 0:1]
    skip_ref[...] = jnp.broadcast_to(column_ref[own_rows, 1:2], skip_ref.shape)
    scale = jnp.sqrt(2.0 * decay)

    for i in range(TILES):
        start = i * tile_len
        embed_copies[i].wait()
        turns = matmul(weight_one, embed_ref[:, start : start + tile_len])
        first = sine_of_turns(
            turns[:hidden] + turns[hidden : 2 * hidden] + turns[2 * hidden :]
        )
        turns = matmul(weight_two, jnp.concatenate(split_two(first), axis=0))
        second = sine_of_turns(turns[:hidden] + turns[hidden:] + bias_two)
        raw = matmul(weight_three, jnp.concatenate(split_two(second), axis=0))
        positions = (start + lax.broadcasted_iota(jnp.int32, (own, tile_len), 1)).astype(F32)
        vals = (raw[:own] + raw[own:]) * (scale * jnp.exp(-decay * positions))
        for j in range(tile_len // LANES):
            row = (start // LANES + j) * own
            filter_ref[row : row + own, :] = vals[:, j * LANES : (j + 1) * LANES]

    for copy in copies[8:]:
        copy.wait()
    blocks = full_len // LANES
    columns = [filter_ref[pl.ds(c, blocks, stride=own), :] for c in range(own)]
    spectrum_ref[...] = inner_product(
        jnp.concatenate(outer_forward(columns, outer_ref, twiddle_ref), axis=0), inner_ref
    )
    taps = taps_ref[own_rows, :]
    tap_count = taps.shape[1]
    square = (tap_count, tap_count)
    upper = lax.broadcasted_iota(jnp.int32, square, 1) >= lax.broadcasted_iota(
        jnp.int32, square, 0
    )
    for c in range(own):
        lags = pltpu.roll(
            jnp.broadcast_to(taps[c : c + 1], square), 0, 1, stride=1, stride_axis=0
        )
        high, low = split_two(
            jnp.concatenate([jnp.where(upper, 0.0, lags), jnp.where(upper, lags, 0.0)], axis=0)
        )
        toeplitz_ref[c] = jnp.concatenate([high, low], axis=1)


def mix_kernel(
    own,
    parts_ref,
    spectrum_ref,
    toeplitz_ref,
    skip_ref,
    outer_ref,
    twiddle_ref,
    inner_ref,
    inner_back_ref,
    outer_back_ref,
    out_ref,
    signal_ref,
    in_gate_ref,
    mixed_ref,
):
    seq_devs, _, _, local_len = parts_ref.shape
    local_blocks = local_len // LANES
    part_rows = local_blocks * own
    blocks = seq_devs * local_blocks
    signal_ref[:own, :] = jnp.zeros((own, LANES), F32)
    for p in range(seq_devs):
        for q in range(local_blocks):
            at = p * part_rows + q * own
            lanes = slice(q * LANES, (q + 1) * LANES)
            signal_ref[own + at : 2 * own + at, :] = parts_ref[p, 0, :, lanes].astype(F32)
            in_gate_ref[at : at + own, :] = parts_ref[p, 1, :, lanes].astype(F32)
    gated = []
    for c in range(own):
        window = jnp.concatenate(
            [
                signal_ref[pl.ds(c, blocks, stride=own), :],
                signal_ref[pl.ds(own + c, blocks, stride=own), :],
            ],
            axis=1,
        ).astype(BF16)
        both = matmul(window, toeplitz_ref[c])
        gated.append(
            in_gate_ref[pl.ds(c, blocks, stride=own), :] * (both[:, :LANES] + both[:, LANES:])
        )
    mid = outer_forward(gated, outer_ref, twiddle_ref)
    step = max(1, own // GROUPS)
    backs = []
    for start in range(0, own, step):
        rows = slice(start * blocks, (start + step) * blocks)
        vals = inner_product(jnp.concatenate(mid[start : start + step], axis=0), inner_ref)
        real, imag = vals[:, :LANES], vals[:, LANES:]
        filt_real, filt_imag = spectrum_ref[rows, :LANES], spectrum_ref[rows, LANES:]
        product = jnp.concatenate(
            [real * filt_real - imag * filt_imag, real * filt_imag + imag * filt_real], axis=1
        )
        backs.append(inner_product(product, inner_back_ref))
    conv = outer_backward(jnp.concatenate(backs, axis=0), own, twiddle_ref, outer_back_ref)
    for c in range(own):
        mixed_ref[pl.ds(c, blocks, stride=own), :] = (
            conv[:, c * LANES : (c + 1) * LANES] + skip_ref[c : c + 1, :] * gated[c]
        )
    columns = []
    for q in range(local_blocks):
        if own % 8 == 0:
            column = jnp.concatenate(
                [
                    mixed_ref[p * part_rows + q * own : p * part_rows + (q + 1) * own, :]
                    for p in range(seq_devs)
                ],
                axis=0,
            )
        else:
            for c in range(own):
                signal_ref[pl.ds(c, seq_devs, stride=own), :] = mixed_ref[
                    pl.ds(q * own + c, seq_devs, stride=part_rows), :
                ]
            column = signal_ref[: seq_devs * own, :]
        high = column.astype(BF16)
        out_ref[:, q * LANES : (q + 1) * LANES] = high
        columns.append(rest_level(column, high.astype(F32)))
    for q in range(local_blocks // 2):
        code = pair_code(columns[q], columns[q + local_blocks // 2]).astype(BF16)
        out_ref[:, local_len + q * LANES : local_len + (q + 1) * LANES] = code


def make_filter(params, own, full_len):
    blocks = full_len // LANES
    hidden, channels = params[5].shape
    tap_count = params[8].shape[1]
    embed = embed_table(full_len)
    tables = transform_tables(full_len)
    operands = (embed,) + params + tables
    padded = round_up(params[0].shape[0] + 1, 8)
    return pl.pallas_call(
        functools.partial(filter_kernel, own),
        out_shape=(
            pltpu.VMEM((own * blocks, 2 * LANES), F32),
            pltpu.VMEM((own, 2 * tap_count, 2 * tap_count), BF16),
            pltpu.VMEM((own, LANES), F32),
        )
        + tuple(pltpu.VMEM(table.shape, table.dtype) for table in tables),
        in_specs=[pl.BlockSpec(memory_space=pltpu.HBM)] * len(operands),
        out_specs=(pl.BlockSpec(memory_space=pltpu.VMEM),) * (3 + len(tables)),
        scratch_shapes=[pltpu.VMEM(embed.shape, BF16)]
        + [pltpu.VMEM(vals.shape, F32) for vals in params]
        + [
            pltpu.VMEM((padded, hidden), F32),
            pltpu.VMEM((8, hidden), F32),
            pltpu.VMEM((8, channels), F32),
            pltpu.VMEM((channels, 8), F32),
            pltpu.VMEM((2, channels, 2 * hidden), F32),
            pltpu.VMEM((blocks * own, LANES), F32),
            pltpu.SemaphoreType.DMA((len(operands) - 1,)),
            pltpu.SemaphoreType.DMA((TILES,)),
        ],
        compiler_params=pltpu.CompilerParams(vmem_limit_bytes=48 * 2**20),
    )(*[in_space(jnp.asarray(vals), pltpu.HBM) for vals in operands])


def mix(parts, shared):
    seq_devs, _, own, local_len = parts.shape
    rows = seq_devs * own * (local_len // LANES)
    vmem = pl.BlockSpec(memory_space=pltpu.VMEM)
    return pl.pallas_call(
        functools.partial(mix_kernel, own),
        out_shape=jax.ShapeDtypeStruct((seq_devs * own, local_len * 3 // 2), BF16),
        in_specs=[vmem] * (1 + len(shared)),
        out_specs=vmem,
        scratch_shapes=[pltpu.VMEM((rows + own, LANES), F32)]
        + [pltpu.VMEM((rows, LANES), F32)] * 2,
        compiler_params=pltpu.CompilerParams(vmem_limit_bytes=48 * 2**20),
    )(parts, *[in_space(vals, pltpu.VMEM) for vals in shared])


def on_device(
    signal,
    in_gate,
    out_gate,
    short_taps,
    skip_gain,
    decay_rate,
    embed_weight,
    embed_bias,
    sine_freq,
    mid_weight,
    mid_bias,
    out_weight,
):
    channels, local_len = signal.shape
    seq_devs = lax.axis_size("seq")
    own = -(-channels // seq_devs)
    spare = own * seq_devs - channels
    parts = [signal, in_gate]
    if spare:
        parts = [jnp.pad(part, ((0, spare), (0, 0))) for part in parts]
        short_taps = jnp.pad(short_taps, ((0, spare), (0, 0)))
        skip_gain = jnp.pad(skip_gain, (0, spare))
        decay_rate = jnp.pad(decay_rate, (0, spare), mode="edge")
        out_weight = jnp.pad(out_weight, ((0, 0), (0, spare)))
    parts = jnp.stack([part.reshape(seq_devs, own, local_len) for part in parts], axis=1)
    parts = lax.all_to_all(parts, "seq", split_axis=0, concat_axis=0, tiled=True)
    params = (
        embed_weight,
        embed_bias[None, :],
        sine_freq[None, :],
        mid_weight,
        mid_bias[None, :],
        out_weight,
        decay_rate[None, :],
        skip_gain[None, :],
        short_taps,
    )
    shared = make_filter(params, own, seq_devs * local_len)
    mixed = mix(parts, shared)
    coded = lax.all_to_all(mixed, "seq", split_axis=0, concat_axis=0, tiled=True)[:channels]
    return gate(coded, out_gate)


def solution(mesh):
    in_specs = (
        P("ch", "seq"),
        P("ch", "seq"),
        P("ch", "seq"),
        P("ch", None),
        P("ch"),
        P("ch"),
        P(),
        P(),
        P(),
        P(),
        P(),
        P(None, "ch"),
    )
    out_specs = P("ch", "seq")
    return jax.shard_map(
        on_device, mesh=mesh, in_specs=in_specs, out_specs=out_specs, check_vma=False
    )
```

```python
import functools
import math

import jax
import jax.numpy as jnp
import numpy as np
from jax import lax
from jax.experimental import pallas as pl
from jax.experimental.pallas import tpu as pltpu
from jax.sharding import PartitionSpec as P

BANDS = 16
LANES = 128
GROUPS = 4
TILES = 4
SPAN = 120.0
F32 = jnp.float32
BF16 = jnp.bfloat16
in_space = pltpu.with_memory_space_constraint


def round_up(count, step):
    return (count + step - 1) // step * step


def halves(table):
    high = table.astype(BF16)
    low = (table - high.astype(np.float64)).astype(BF16)
    return high, low


@functools.lru_cache(maxsize=None)
def embed_table(full_len):
    positions = np.arange(full_len, dtype=np.int64)
    rows = [positions / full_len]
    phase = positions
    for _ in range(BANDS):
        angle = phase * (2.0 * math.pi / full_len)
        rows += [np.cos(angle), np.sin(angle)]
        phase = 2 * phase % full_len
    rows.append(np.ones(full_len))
    table = np.zeros((round_up(len(rows), 8), full_len))
    table[: len(rows)] = np.stack(rows)
    first, rest = halves(table)
    second, third = halves(table - first.astype(np.float64))
    stacked = np.concatenate([first, second, third], axis=0)
    return np.pad(stacked, ((0, -len(stacked) % 16), (0, 0)))


@functools.lru_cache(maxsize=None)
def transform_tables(full_len):
    blocks = full_len // LANES
    a = np.arange(blocks)
    k1 = np.arange(blocks)
    b = np.arange(LANES)
    theta = 2.0 * math.pi / blocks * ((4 * k1 + 1)[:, None] * a[None, :] % (4 * blocks)) / 4.0
    phi = 2.0 * math.pi / full_len * ((4 * k1 + 1)[:, None] * b[None, :]) / 4.0
    psi = 2.0 * math.pi / LANES * (b[:, None] * b[None, :] % LANES)
    outer_high, outer_low = halves(np.concatenate([np.cos(theta), -np.sin(theta)], axis=0))
    outer = np.concatenate([outer_high, outer_high, outer_low], axis=1)
    back = np.concatenate([np.cos(theta).T, -np.sin(theta).T], axis=1) / full_len
    back_high, back_low = halves(back)
    outer_back = np.concatenate([back_high, back_high, back_low], axis=1)
    twiddle = np.stack([np.cos(phi), np.sin(phi)]).astype(np.float32)
    cos_in, sin_in = np.cos(psi), np.sin(psi)
    inner = np.stack(halves(np.block([[cos_in, -sin_in], [sin_in, cos_in]])))
    inner_back = np.stack(halves(np.block([[cos_in, sin_in], [-sin_in, cos_in]])))
    return outer, twiddle, inner, inner_back, outer_back


def sine_fit(terms):
    nodes = np.cos((np.arange(400) + 0.5) * math.pi / 400) * 0.5
    basis = np.stack([nodes ** (2 * p + 1) for p in range(terms)], axis=1)
    fit = np.linalg.lstsq(basis, np.sin(2.0 * math.pi * nodes), rcond=None)[0]
    return [float(v) for v in fit]


SINE_FIT = sine_fit(7)


def sine_of_turns(turns):
    part = turns - jnp.round(turns)
    square = part * part
    value = SINE_FIT[-1]
    for term in SINE_FIT[-2::-1]:
        value = value * square + term
    return value * part


def split_two(vals):
    high = vals.astype(BF16)
    return high, (vals - high.astype(F32)).astype(BF16)


def split_three(vals):
    first = vals.astype(BF16).astype(F32)
    rest = vals - first
    second = rest.astype(BF16).astype(F32)
    return first, second, rest - second


def matmul(lhs, rhs):
    return jnp.dot(lhs, rhs, preferred_element_type=F32)


def stack_three(vals):
    high, low = split_two(vals)
    return jnp.concatenate([high, low, high], axis=0)


def inner_product(vals, table_ref):
    high, low = split_two(vals)
    return (
        matmul(high, table_ref[0]) + matmul(low, table_ref[0]) + matmul(high, table_ref[1])
    )


def outer_forward(columns, outer_ref, twiddle_ref):
    blocks = columns[0].shape[0]
    mixed = matmul(outer_ref[...], stack_three(jnp.concatenate(columns, axis=1)))
    cos_vals, sin_vals = twiddle_ref[0], twiddle_ref[1]
    rows = []
    for c in range(len(columns)):
        real = mixed[:blocks, c * LANES : (c + 1) * LANES]
        imag = mixed[blocks:, c * LANES : (c + 1) * LANES]
        rows.append(
            jnp.concatenate(
                [real * cos_vals + imag * sin_vals, imag * cos_vals - real * sin_vals], axis=1
            )
        )
    return rows


def outer_backward(vals, channels, twiddle_ref, outer_back_ref):
    blocks = vals.shape[0] // channels
    cos_vals, sin_vals = twiddle_ref[0], twiddle_ref[1]
    columns = []
    for c in range(channels):
        real = vals[c * blocks : (c + 1) * blocks, :LANES]
        imag = vals[c * blocks : (c + 1) * blocks, LANES:]
        columns.append(
            jnp.concatenate(
                [real * cos_vals - imag * sin_vals, imag * cos_vals + real * sin_vals], axis=0
            )
        )
    return matmul(outer_back_ref[...], stack_three(jnp.concatenate(columns, axis=1)))


def code_group(columns):
    top = functools.reduce(jnp.maximum, [jnp.abs(column) for column in columns])
    scale = lax.reduce_precision(jnp.maximum(top, 1e-30) * (1.0 + 1.0 / 128), 8, 7)
    factor = 2.0 * SPAN / scale
    codes = []
    for column in columns:
        size = jnp.exp2(jnp.abs(column) * factor - SPAN)
        codes.append(jnp.where(column < 0, -size, size).astype(BF16))
    return codes, scale.astype(BF16)


def decode_group(codes, scale):
    codes = codes.astype(F32)
    share = jnp.log(jnp.abs(codes)) * (0.5 / SPAN / math.log(2.0)) + 0.5
    return jnp.where(codes < 0, -share, share) * scale.astype(F32)


def filter_kernel(
    own,
    embed_hbm,
    embed_weight_hbm,
    embed_bias_hbm,
    sine_freq_hbm,
    mid_weight_hbm,
    mid_bias_hbm,
    out_weight_hbm,
    decay_hbm,
    skip_hbm,
    taps_hbm,
    outer_hbm,
    twiddle_hbm,
    inner_hbm,
    inner_back_hbm,
    outer_back_hbm,
    spectrum_ref,
    toeplitz_ref,
    skip_ref,
    outer_ref,
    twiddle_ref,
    inner_ref,
    inner_back_ref,
    outer_back_ref,
    embed_ref,
    embed_weight_ref,
    embed_bias_ref,
    sine_freq_ref,
    mid_weight_ref,
    mid_bias_ref,
    out_weight_ref,
    decay_ref,
    skip_row_ref,
    taps_ref,
    pad_ref,
    vec_ref,
    row_ref,
    column_ref,
    out_rows_ref,
    filter_ref,
    sems,
    embed_sems,
):
    full_len = embed_ref.shape[1]
    tile_len = full_len // TILES
    hidden = mid_weight_ref.shape[0]
    pairs = [
        (embed_weight_hbm, embed_weight_ref),
        (embed_bias_hbm, embed_bias_ref),
        (sine_freq_hbm, sine_freq_ref),
        (mid_weight_hbm, mid_weight_ref),
        (mid_bias_hbm, mid_bias_ref),
        (out_weight_hbm, out_weight_ref),
        (decay_hbm, decay_ref),
        (skip_hbm, skip_row_ref),
        (taps_hbm, taps_ref),
        (outer_hbm, outer_ref),
        (twiddle_hbm, twiddle_ref),
        (inner_hbm, inner_ref),
        (inner_back_hbm, inner_back_ref),
        (outer_back_hbm, outer_back_ref),
    ]
    copies = [pltpu.make_async_copy(*pair, sems.at[i]) for i, pair in enumerate(pairs)]
    embed_copies = []
    for i in range(TILES):
        lanes = pl.ds(i * tile_len, tile_len)
        embed_copies.append(
            pltpu.make_async_copy(
                embed_hbm.at[:, lanes], embed_ref.at[:, lanes], embed_sems.at[i]
            )
        )
    for copy in copies[:8] + embed_copies + copies[8:]:
        copy.start()
    first_channel = pl.multiple_of(lax.axis_index("seq") * own, own)
    pad_ref[...] = jnp.zeros_like(pad_ref)
    vec_ref[...] = jnp.zeros_like(vec_ref)
    row_ref[...] = jnp.zeros_like(row_ref)
    for copy in copies[:8]:
        copy.wait()

    freq = sine_freq_ref[...] * (0.5 / math.pi)
    features = embed_weight_ref.shape[0]
    pad_ref[:features, :] = embed_weight_ref[...] * freq
    pad_ref[features : features + 1, :] = embed_bias_ref[...] * freq
    one, two, three = split_three(pad_ref[...])
    none = jnp.zeros_like(one)
    rest = jnp.zeros((embed_ref.shape[0] - 3 * one.shape[0], hidden), F32)
    weight_one = jnp.concatenate(
        [
            jnp.concatenate([one, one, one, rest], axis=0).T,
            jnp.concatenate([two, two, none, rest], axis=0).T,
            jnp.concatenate([three, none, none, rest], axis=0).T,
        ],
        axis=0,
    ).astype(BF16)
    one, two, _ = split_three(mid_weight_ref[...] * freq)
    weight_two = jnp.concatenate(
        [jnp.concatenate([one, one], axis=0).T, jnp.concatenate([two, two], axis=0).T], axis=0
    ).astype(BF16)
    vec_ref[0:1, :] = mid_bias_ref[...] * freq
    bias_two = vec_ref[...].T[:, 0:1]
    one, two, _ = split_three(out_weight_ref[...])
    out_rows_ref[0] = jnp.concatenate([one, one], axis=0).T
    out_rows_ref[1] = jnp.concatenate([two, two], axis=0).T
    own_rows = pl.ds(first_channel, own)
    weight_three = jnp.concatenate(
        [out_rows_ref[0, own_rows, :], out_rows_ref[1, own_rows, :]], axis=0
    ).astype(BF16)
    row_ref[0:1, :] = decay_ref[...]
    row_ref[1:2, :] = skip_row_ref[...]
    column_ref[...] = row_ref[...].T
    decay = column_ref[own_rows, 0:1]
    skip_ref[...] = jnp.broadcast_to(column_ref[own_rows, 1:2], skip_ref.shape)
    scale = jnp.sqrt(2.0 * decay)

    for i in range(TILES):
        start = i * tile_len
        embed_copies[i].wait()
        turns = matmul(weight_one, embed_ref[:, start : start + tile_len])
        first = sine_of_turns(
            turns[:hidden] + turns[hidden : 2 * hidden] + turns[2 * hidden :]
        )
        turns = matmul(weight_two, jnp.concatenate(split_two(first), axis=0))
        second = sine_of_turns(turns[:hidden] + turns[hidden:] + bias_two)
        raw = matmul(weight_three, jnp.concatenate(split_two(second), axis=0))
        positions = (start + lax.broadcasted_iota(jnp.int32, (own, tile_len), 1)).astype(F32)
        vals = (raw[:own] + raw[own:]) * (scale * jnp.exp(-decay * positions))
        for j in range(tile_len // LANES):
            row = (start // LANES + j) * own
            filter_ref[row : row + own, :] = vals[:, j * LANES : (j + 1) * LANES]

    for copy in copies[8:]:
        copy.wait()
    blocks = full_len // LANES
    columns = [filter_ref[pl.ds(c, blocks, stride=own), :] for c in range(own)]
    spectrum_ref[...] = inner_product(
        jnp.concatenate(outer_forward(columns, outer_ref, twiddle_ref), axis=0), inner_ref
    )
    taps = taps_ref[own_rows, :]
    tap_count = taps.shape[1]
    square = (tap_count, tap_count)
    upper = lax.broadcasted_iota(jnp.int32, square, 1) >= lax.broadcasted_iota(
        jnp.int32, square, 0
    )
    for c in range(own):
        lags = pltpu.roll(
            jnp.broadcast_to(taps[c : c + 1], square), 0, 1, stride=1, stride_axis=0
        )
        high, low = split_two(
            jnp.concatenate([jnp.where(upper, 0.0, lags), jnp.where(upper, lags, 0.0)], axis=0)
        )
        toeplitz_ref[c] = jnp.concatenate([high, low], axis=1)


def mix_kernel(
    own,
    parts_ref,
    spectrum_ref,
    toeplitz_ref,
    skip_ref,
    outer_ref,
    twiddle_ref,
    inner_ref,
    inner_back_ref,
    outer_back_ref,
    out_ref,
    signal_ref,
    in_gate_ref,
    mixed_ref,
):
    seq_devs, _, _, local_len = parts_ref.shape
    local_blocks = local_len // LANES
    part_rows = local_blocks * own
    blocks = seq_devs * local_blocks
    signal_ref[:own, :] = jnp.zeros((own, LANES), F32)
    for p in range(seq_devs):
        for q in range(local_blocks):
            at = p * part_rows + q * own
            lanes = slice(q * LANES, (q + 1) * LANES)
            signal_ref[own + at : 2 * own + at, :] = parts_ref[p, 0, :, lanes].astype(F32)
            in_gate_ref[at : at + own, :] = parts_ref[p, 1, :, lanes].astype(F32)
    gated = []
    for c in range(own):
        window = jnp.concatenate(
            [
                signal_ref[pl.ds(c, blocks, stride=own), :],
                signal_ref[pl.ds(own + c, blocks, stride=own), :],
            ],
            axis=1,
        ).astype(BF16)
        both = matmul(window, toeplitz_ref[c])
        gated.append(
            in_gate_ref[pl.ds(c, blocks, stride=own), :] * (both[:, :LANES] + both[:, LANES:])
        )
    mid = outer_forward(gated, outer_ref, twiddle_ref)
    step = max(1, own // GROUPS)
    backs = []
    for start in range(0, own, step):
        rows = slice(start * blocks, (start + step) * blocks)
        vals = inner_product(jnp.concatenate(mid[start : start + step], axis=0), inner_ref)
        real, imag = vals[:, :LANES], vals[:, LANES:]
        filt_real, filt_imag = spectrum_ref[rows, :LANES], spectrum_ref[rows, LANES:]
        product = jnp.concatenate(
            [real * filt_real - imag * filt_imag, real * filt_imag + imag * filt_real], axis=1
        )
        backs.append(inner_product(product, inner_back_ref))
    conv = outer_backward(jnp.concatenate(backs, axis=0), own, twiddle_ref, outer_back_ref)
    for c in range(own):
        mixed_ref[pl.ds(c, blocks, stride=own), :] = (
            conv[:, c * LANES : (c + 1) * LANES] + skip_ref[c : c + 1, :] * gated[c]
        )
    columns = []
    for q in range(local_blocks):
        if own % 8 == 0:
            column = jnp.concatenate(
                [
                    mixed_ref[p * part_rows + q * own : p * part_rows + (q + 1) * own, :]
                    for p in range(seq_devs)
                ],
                axis=0,
            )
        else:
            for c in range(own):
                signal_ref[pl.ds(c, seq_devs, stride=own), :] = mixed_ref[
                    pl.ds(q * own + c, seq_devs, stride=part_rows), :
                ]
            column = signal_ref[: seq_devs * own, :]
        columns.append(column)
    codes, scale = code_group(columns)
    for q in range(local_blocks):
        out_ref[:, q * LANES : (q + 1) * LANES] = codes[q]
    out_ref[:, local_len:] = scale


def make_filter(params, own, full_len):
    blocks = full_len // LANES
    hidden, channels = params[5].shape
    tap_count = params[8].shape[1]
    embed = embed_table(full_len)
    tables = transform_tables(full_len)
    operands = (embed,) + params + tables
    padded = round_up(params[0].shape[0] + 1, 8)
    return pl.pallas_call(
        functools.partial(filter_kernel, own),
        out_shape=(
            pltpu.VMEM((own * blocks, 2 * LANES), F32),
            pltpu.VMEM((own, 2 * tap_count, 2 * tap_count), BF16),
            pltpu.VMEM((own, LANES), F32),
        )
        + tuple(pltpu.VMEM(table.shape, table.dtype) for table in tables),
        in_specs=[pl.BlockSpec(memory_space=pltpu.HBM)] * len(operands),
        out_specs=(pl.BlockSpec(memory_space=pltpu.VMEM),) * (3 + len(tables)),
        scratch_shapes=[pltpu.VMEM(embed.shape, BF16)]
        + [pltpu.VMEM(vals.shape, F32) for vals in params]
        + [
            pltpu.VMEM((padded, hidden), F32),
            pltpu.VMEM((8, hidden), F32),
            pltpu.VMEM((8, channels), F32),
            pltpu.VMEM((channels, 8), F32),
            pltpu.VMEM((2, channels, 2 * hidden), F32),
            pltpu.VMEM((blocks * own, LANES), F32),
            pltpu.SemaphoreType.DMA((len(operands) - 1,)),
            pltpu.SemaphoreType.DMA((TILES,)),
        ],
        compiler_params=pltpu.CompilerParams(vmem_limit_bytes=48 * 2**20),
    )(*[in_space(jnp.asarray(vals), pltpu.HBM) for vals in operands])


def mix(parts, shared):
    seq_devs, _, own, local_len = parts.shape
    rows = seq_devs * own * (local_len // LANES)
    vmem = pl.BlockSpec(memory_space=pltpu.VMEM)
    return pl.pallas_call(
        functools.partial(mix_kernel, own),
        out_shape=jax.ShapeDtypeStruct((seq_devs * own, local_len + LANES), BF16),
        in_specs=[vmem] * (1 + len(shared)),
        out_specs=vmem,
        scratch_shapes=[pltpu.VMEM((rows + own, LANES), F32)]
        + [pltpu.VMEM((rows, LANES), F32)] * 2,
        compiler_params=pltpu.CompilerParams(vmem_limit_bytes=48 * 2**20),
    )(parts, *[in_space(vals, pltpu.VMEM) for vals in shared])


def on_device(
    signal,
    in_gate,
    out_gate,
    short_taps,
    skip_gain,
    decay_rate,
    embed_weight,
    embed_bias,
    sine_freq,
    mid_weight,
    mid_bias,
    out_weight,
):
    channels, local_len = signal.shape
    seq_devs = lax.axis_size("seq")
    own = -(-channels // seq_devs)
    spare = own * seq_devs - channels
    parts = [signal, in_gate]
    if spare:
        parts = [jnp.pad(part, ((0, spare), (0, 0))) for part in parts]
        short_taps = jnp.pad(short_taps, ((0, spare), (0, 0)))
        skip_gain = jnp.pad(skip_gain, (0, spare))
        decay_rate = jnp.pad(decay_rate, (0, spare), mode="edge")
        out_weight = jnp.pad(out_weight, ((0, 0), (0, spare)))
    parts = jnp.stack([part.reshape(seq_devs, own, local_len) for part in parts], axis=1)
    parts = lax.all_to_all(parts, "seq", split_axis=0, concat_axis=0, tiled=True)
    params = (
        embed_weight,
        embed_bias[None, :],
        sine_freq[None, :],
        mid_weight,
        mid_bias[None, :],
        out_weight,
        decay_rate[None, :],
        skip_gain[None, :],
        short_taps,
    )
    shared = make_filter(params, own, seq_devs * local_len)
    mixed = mix(parts, shared)
    coded = lax.all_to_all(mixed, "seq", split_axis=0, concat_axis=0, tiled=True)[:channels]
    scale = jnp.concatenate([coded[:, local_len:]] * (local_len // LANES), axis=1)
    vals = decode_group(coded[:, :local_len], scale)
    return (out_gate.astype(F32) * vals).astype(BF16)


def solution(mesh):
    in_specs = (
        P("ch", "seq"),
        P("ch", "seq"),
        P("ch", "seq"),
        P("ch", None),
        P("ch"),
        P("ch"),
        P(),
        P(),
        P(),
        P(),
        P(),
        P(None, "ch"),
    )
    out_specs = P("ch", "seq")
    return jax.shard_map(
        on_device, mesh=mesh, in_specs=in_specs, out_specs=out_specs, check_vma=False
    )
```

```python
import functools
import math

import jax
import jax.numpy as jnp
import numpy as np
from jax import lax
from jax.experimental import pallas as pl
from jax.experimental.pallas import tpu as pltpu
from jax.sharding import PartitionSpec as P

BANDS = 16
LANES = 128
GROUPS = 4
TILES = 2
SPAN = 120.0
F32 = jnp.float32
BF16 = jnp.bfloat16
in_space = pltpu.with_memory_space_constraint


def round_up(count, step):
    return (count + step - 1) // step * step


def halves(table):
    high = table.astype(BF16)
    low = (table - high.astype(np.float64)).astype(BF16)
    return high, low


@functools.lru_cache(maxsize=None)
def embed_table(full_len):
    positions = np.arange(full_len, dtype=np.int64)
    rows = [positions / full_len]
    phase = positions
    for _ in range(BANDS):
        angle = phase * (2.0 * math.pi / full_len)
        rows += [np.cos(angle), np.sin(angle)]
        phase = 2 * phase % full_len
    rows.append(np.ones(full_len))
    table = np.zeros((round_up(len(rows), 8), full_len))
    table[: len(rows)] = np.stack(rows)
    first, rest = halves(table)
    second, third = halves(table - first.astype(np.float64))
    stacked = np.concatenate([first, second, third], axis=0)
    return np.pad(stacked, ((0, -len(stacked) % 16), (0, 0)))


@functools.lru_cache(maxsize=None)
def transform_tables(full_len):
    blocks = full_len // LANES
    a = np.arange(blocks)
    k1 = np.arange(blocks)
    b = np.arange(LANES)
    theta = 2.0 * math.pi / blocks * ((4 * k1 + 1)[:, None] * a[None, :] % (4 * blocks)) / 4.0
    phi = 2.0 * math.pi / full_len * ((4 * k1 + 1)[:, None] * b[None, :]) / 4.0
    psi = 2.0 * math.pi / LANES * (b[:, None] * b[None, :] % LANES)
    outer_high, outer_low = halves(np.concatenate([np.cos(theta), -np.sin(theta)], axis=0))
    outer = np.concatenate([outer_high, outer_high, outer_low], axis=1)
    back = np.concatenate([np.cos(theta).T, -np.sin(theta).T], axis=1) / full_len
    back_high, back_low = halves(back)
    outer_back = np.concatenate([back_high, back_high, back_low], axis=1)
    twiddle = np.stack([np.cos(phi), np.sin(phi)]).astype(np.float32)
    cos_in, sin_in = np.cos(psi), np.sin(psi)
    inner = np.stack(halves(np.block([[cos_in, -sin_in], [sin_in, cos_in]])))
    inner_back = np.stack(halves(np.block([[cos_in, sin_in], [-sin_in, cos_in]])))
    return outer, twiddle, inner, inner_back, outer_back


def sine_fit(terms):
    nodes = np.cos((np.arange(400) + 0.5) * math.pi / 400) * 0.5
    basis = np.stack([nodes ** (2 * p + 1) for p in range(terms)], axis=1)
    fit = np.linalg.lstsq(basis, np.sin(2.0 * math.pi * nodes), rcond=None)[0]
    return [float(v) for v in fit]


SINE_FIT = sine_fit(6)


def sine_of_turns(turns):
    part = turns - jnp.round(turns)
    square = part * part
    value = SINE_FIT[-1]
    for term in SINE_FIT[-2::-1]:
        value = value * square + term
    return value * part


def split_two(vals):
    high = vals.astype(BF16)
    return high, (vals - high.astype(F32)).astype(BF16)


def split_three(vals):
    first = vals.astype(BF16).astype(F32)
    rest = vals - first
    second = rest.astype(BF16).astype(F32)
    return first, second, rest - second


def matmul(lhs, rhs):
    return jnp.dot(lhs, rhs, preferred_element_type=F32)


def stack_three(vals):
    high, low = split_two(vals)
    return jnp.concatenate([high, low, high], axis=0)


def inner_product(vals, table_ref):
    high, low = split_two(vals)
    return (
        matmul(high, table_ref[0]) + matmul(low, table_ref[0]) + matmul(high, table_ref[1])
    )


def outer_forward(columns, outer_ref, twiddle_ref):
    blocks = columns[0].shape[0]
    mixed = matmul(outer_ref[...], stack_three(jnp.concatenate(columns, axis=1)))
    cos_vals, sin_vals = twiddle_ref[0], twiddle_ref[1]
    rows = []
    for c in range(len(columns)):
        real = mixed[:blocks, c * LANES : (c + 1) * LANES]
        imag = mixed[blocks:, c * LANES : (c + 1) * LANES]
        rows.append(
            jnp.concatenate(
                [real * cos_vals + imag * sin_vals, imag * cos_vals - real * sin_vals], axis=1
            )
        )
    return rows


def outer_backward(vals, channels, twiddle_ref, outer_back_ref):
    blocks = vals.shape[0] // channels
    cos_vals, sin_vals = twiddle_ref[0], twiddle_ref[1]
    columns = []
    for c in range(channels):
        real = vals[c * blocks : (c + 1) * blocks, :LANES]
        imag = vals[c * blocks : (c + 1) * blocks, LANES:]
        columns.append(
            jnp.concatenate(
                [real * cos_vals - imag * sin_vals, imag * cos_vals + real * sin_vals], axis=0
            )
        )
    return matmul(outer_back_ref[...], stack_three(jnp.concatenate(columns, axis=1)))


def code_group(columns):
    top = functools.reduce(jnp.maximum, [jnp.abs(column) for column in columns])
    scale = lax.reduce_precision(jnp.maximum(top, 1e-30) * (1.0 + 1.0 / 128), 8, 7)
    factor = 2.0 * SPAN / scale
    codes = []
    for column in columns:
        size = jnp.exp2(jnp.abs(column) * factor - SPAN)
        codes.append(jnp.where(column < 0, -size, size).astype(BF16))
    return codes, scale.astype(BF16)


def decode_group(codes, scale):
    codes = codes.astype(F32)
    share = jnp.log(jnp.abs(codes)) * (0.5 / SPAN / math.log(2.0)) + 0.5
    return jnp.where(codes < 0, -share, share) * scale.astype(F32)


def filter_kernel(
    own,
    embed_hbm,
    embed_weight_hbm,
    embed_bias_hbm,
    sine_freq_hbm,
    mid_weight_hbm,
    mid_bias_hbm,
    out_weight_hbm,
    decay_hbm,
    skip_hbm,
    taps_hbm,
    outer_hbm,
    twiddle_hbm,
    inner_hbm,
    inner_back_hbm,
    outer_back_hbm,
    spectrum_ref,
    toeplitz_ref,
    skip_ref,
    outer_ref,
    twiddle_ref,
    inner_ref,
    inner_back_ref,
    outer_back_ref,
    embed_ref,
    embed_weight_ref,
    embed_bias_ref,
    sine_freq_ref,
    mid_weight_ref,
    mid_bias_ref,
    out_weight_ref,
    decay_ref,
    skip_row_ref,
    taps_ref,
    pad_ref,
    vec_ref,
    row_ref,
    column_ref,
    out_rows_ref,
    filter_ref,
    sems,
    embed_sems,
):
    full_len = embed_ref.shape[1]
    tile_len = full_len // TILES
    hidden = mid_weight_ref.shape[0]
    pairs = [
        (embed_weight_hbm, embed_weight_ref),
        (embed_bias_hbm, embed_bias_ref),
        (sine_freq_hbm, sine_freq_ref),
        (mid_weight_hbm, mid_weight_ref),
        (mid_bias_hbm, mid_bias_ref),
        (out_weight_hbm, out_weight_ref),
        (decay_hbm, decay_ref),
        (skip_hbm, skip_row_ref),
        (taps_hbm, taps_ref),
        (outer_hbm, outer_ref),
        (twiddle_hbm, twiddle_ref),
        (inner_hbm, inner_ref),
        (inner_back_hbm, inner_back_ref),
        (outer_back_hbm, outer_back_ref),
    ]
    copies = [pltpu.make_async_copy(*pair, sems.at[i]) for i, pair in enumerate(pairs)]
    embed_copies = []
    for i in range(TILES):
        lanes = pl.ds(i * tile_len, tile_len)
        embed_copies.append(
            pltpu.make_async_copy(
                embed_hbm.at[:, lanes], embed_ref.at[:, lanes], embed_sems.at[i]
            )
        )
    for copy in copies[:8] + embed_copies + copies[8:]:
        copy.start()
    first_channel = pl.multiple_of(lax.axis_index("seq") * own, own)
    pad_ref[...] = jnp.zeros_like(pad_ref)
    vec_ref[...] = jnp.zeros_like(vec_ref)
    row_ref[...] = jnp.zeros_like(row_ref)
    for copy in copies[:8]:
        copy.wait()

    freq = sine_freq_ref[...] * (0.5 / math.pi)
    features = embed_weight_ref.shape[0]
    pad_ref[:features, :] = embed_weight_ref[...] * freq
    pad_ref[features : features + 1, :] = embed_bias_ref[...] * freq
    one, two, three = split_three(pad_ref[...])
    none = jnp.zeros_like(one)
    rest = jnp.zeros((embed_ref.shape[0] - 3 * one.shape[0], hidden), F32)
    weight_one = jnp.concatenate(
        [
            jnp.concatenate([one, one, one, rest], axis=0).T,
            jnp.concatenate([two, two, none, rest], axis=0).T,
            jnp.concatenate([three, none, none, rest], axis=0).T,
        ],
        axis=0,
    ).astype(BF16)
    one, two, _ = split_three(mid_weight_ref[...] * freq)
    weight_two = jnp.concatenate([one, one, two], axis=0).T.astype(BF16)
    vec_ref[0:1, :] = mid_bias_ref[...] * freq
    bias_two = vec_ref[...].T[:, 0:1]
    one, two, _ = split_three(out_weight_ref[...])
    out_rows_ref[0] = jnp.concatenate([one, one], axis=0).T
    out_rows_ref[1] = jnp.concatenate([two, two], axis=0).T
    own_rows = pl.ds(first_channel, own)
    weight_three = jnp.concatenate(
        [out_rows_ref[0, own_rows, :], out_rows_ref[1, own_rows, :]], axis=0
    ).astype(BF16)
    row_ref[0:1, :] = decay_ref[...]
    row_ref[1:2, :] = skip_row_ref[...]
    column_ref[...] = row_ref[...].T
    decay = column_ref[own_rows, 0:1]
    skip_ref[...] = jnp.broadcast_to(column_ref[own_rows, 1:2], skip_ref.shape)
    scale = jnp.sqrt(2.0 * decay)

    for i in range(TILES):
        start = i * tile_len
        embed_copies[i].wait()
        turns = matmul(weight_one, embed_ref[:, start : start + tile_len])
        first = sine_of_turns(
            turns[:hidden] + turns[hidden : 2 * hidden] + turns[2 * hidden :]
        )
        second = sine_of_turns(matmul(weight_two, stack_three(first)) + bias_two)
        raw = matmul(weight_three, jnp.concatenate(split_two(second), axis=0))
        positions = (start + lax.broadcasted_iota(jnp.int32, (own, tile_len), 1)).astype(F32)
        vals = (raw[:own] + raw[own:]) * (scale * jnp.exp(-decay * positions))
        for j in range(tile_len // LANES):
            row = (start // LANES + j) * own
            filter_ref[row : row + own, :] = vals[:, j * LANES : (j + 1) * LANES]

    for copy in copies[8:]:
        copy.wait()
    blocks = full_len // LANES
    columns = [filter_ref[pl.ds(c, blocks, stride=own), :] for c in range(own)]
    spectrum_ref[...] = inner_product(
        jnp.concatenate(outer_forward(columns, outer_ref, twiddle_ref), axis=0), inner_ref
    )
    taps = taps_ref[own_rows, :]
    tap_count = taps.shape[1]
    square = (tap_count, tap_count)
    upper = lax.broadcasted_iota(jnp.int32, square, 1) >= lax.broadcasted_iota(
        jnp.int32, square, 0
    )
    for c in range(own):
        lags = pltpu.roll(
            jnp.broadcast_to(taps[c : c + 1], square), 0, 1, stride=1, stride_axis=0
        )
        high, low = split_two(
            jnp.concatenate([jnp.where(upper, 0.0, lags), jnp.where(upper, lags, 0.0)], axis=0)
        )
        toeplitz_ref[c] = jnp.concatenate([high, low], axis=1)


def mix_kernel(
    own,
    parts_ref,
    spectrum_ref,
    toeplitz_ref,
    skip_ref,
    outer_ref,
    twiddle_ref,
    inner_ref,
    inner_back_ref,
    outer_back_ref,
    out_ref,
    signal_ref,
    in_gate_ref,
    mixed_ref,
):
    seq_devs, _, _, local_len = parts_ref.shape
    local_blocks = local_len // LANES
    part_rows = local_blocks * own
    blocks = seq_devs * local_blocks
    signal_ref[:own, :] = jnp.zeros((own, LANES), F32)
    for p in range(seq_devs):
        for q in range(local_blocks):
            at = p * part_rows + q * own
            lanes = slice(q * LANES, (q + 1) * LANES)
            signal_ref[own + at : 2 * own + at, :] = parts_ref[p, 0, :, lanes].astype(F32)
            in_gate_ref[at : at + own, :] = parts_ref[p, 1, :, lanes].astype(F32)
    gated = []
    for c in range(own):
        window = jnp.concatenate(
            [
                signal_ref[pl.ds(c, blocks, stride=own), :],
                signal_ref[pl.ds(own + c, blocks, stride=own), :],
            ],
            axis=1,
        ).astype(BF16)
        both = matmul(window, toeplitz_ref[c])
        gated.append(
            in_gate_ref[pl.ds(c, blocks, stride=own), :] * (both[:, :LANES] + both[:, LANES:])
        )
    mid = outer_forward(gated, outer_ref, twiddle_ref)
    step = max(1, own // GROUPS)
    backs = []
    for start in range(0, own, step):
        rows = slice(start * blocks, (start + step) * blocks)
        vals = inner_product(jnp.concatenate(mid[start : start + step], axis=0), inner_ref)
        real, imag = vals[:, :LANES], vals[:, LANES:]
        filt_real, filt_imag = spectrum_ref[rows, :LANES], spectrum_ref[rows, LANES:]
        product = jnp.concatenate(
            [real * filt_real - imag * filt_imag, real * filt_imag + imag * filt_real], axis=1
        )
        backs.append(inner_product(product, inner_back_ref))
    conv = outer_backward(jnp.concatenate(backs, axis=0), own, twiddle_ref, outer_back_ref)
    for c in range(own):
        mixed_ref[pl.ds(c, blocks, stride=own), :] = (
            conv[:, c * LANES : (c + 1) * LANES] + skip_ref[c : c + 1, :] * gated[c]
        )
    columns = []
    for q in range(local_blocks):
        if own % 8 == 0:
            column = jnp.concatenate(
                [
                    mixed_ref[p * part_rows + q * own : p * part_rows + (q + 1) * own, :]
                    for p in range(seq_devs)
                ],
                axis=0,
            )
        else:
            for c in range(own):
                signal_ref[pl.ds(c, seq_devs, stride=own), :] = mixed_ref[
                    pl.ds(q * own + c, seq_devs, stride=part_rows), :
                ]
            column = signal_ref[: seq_devs * own, :]
        columns.append(column)
    codes, scale = code_group(columns)
    for q in range(local_blocks):
        out_ref[:, q * LANES : (q + 1) * LANES] = codes[q]
    out_ref[:, local_len:] = scale


def make_filter(params, own, full_len):
    blocks = full_len // LANES
    hidden, channels = params[5].shape
    tap_count = params[8].shape[1]
    embed = embed_table(full_len)
    tables = transform_tables(full_len)
    operands = (embed,) + params + tables
    padded = round_up(params[0].shape[0] + 1, 8)
    return pl.pallas_call(
        functools.partial(filter_kernel, own),
        out_shape=(
            pltpu.VMEM((own * blocks, 2 * LANES), F32),
            pltpu.VMEM((own, 2 * tap_count, 2 * tap_count), BF16),
            pltpu.VMEM((own, LANES), F32),
        )
        + tuple(pltpu.VMEM(table.shape, table.dtype) for table in tables),
        in_specs=[pl.BlockSpec(memory_space=pltpu.HBM)] * len(operands),
        out_specs=(pl.BlockSpec(memory_space=pltpu.VMEM),) * (3 + len(tables)),
        scratch_shapes=[pltpu.VMEM(embed.shape, BF16)]
        + [pltpu.VMEM(vals.shape, F32) for vals in params]
        + [
            pltpu.VMEM((padded, hidden), F32),
            pltpu.VMEM((8, hidden), F32),
            pltpu.VMEM((8, channels), F32),
            pltpu.VMEM((channels, 8), F32),
            pltpu.VMEM((2, channels, 2 * hidden), F32),
            pltpu.VMEM(((blocks + 1) * own, LANES), F32),
            pltpu.SemaphoreType.DMA((len(operands) - 1,)),
            pltpu.SemaphoreType.DMA((TILES,)),
        ],
        compiler_params=pltpu.CompilerParams(vmem_limit_bytes=48 * 2**20),
    )(*[in_space(jnp.asarray(vals), pltpu.HBM) for vals in operands])


def mix(parts, shared):
    seq_devs, _, own, local_len = parts.shape
    rows = seq_devs * own * (local_len // LANES)
    vmem = pl.BlockSpec(memory_space=pltpu.VMEM)
    return pl.pallas_call(
        functools.partial(mix_kernel, own),
        out_shape=jax.ShapeDtypeStruct((seq_devs * own, local_len + LANES), BF16),
        in_specs=[vmem] * (1 + len(shared)),
        out_specs=vmem,
        scratch_shapes=[pltpu.VMEM((rows + 2 * own, LANES), F32)]
        + [pltpu.VMEM((rows + own, LANES), F32)] * 2,
        compiler_params=pltpu.CompilerParams(vmem_limit_bytes=48 * 2**20),
    )(parts, *[in_space(vals, pltpu.VMEM) for vals in shared])


def on_device(
    signal,
    in_gate,
    out_gate,
    short_taps,
    skip_gain,
    decay_rate,
    embed_weight,
    embed_bias,
    sine_freq,
    mid_weight,
    mid_bias,
    out_weight,
):
    channels, local_len = signal.shape
    seq_devs = lax.axis_size("seq")
    own = -(-channels // seq_devs)
    spare = own * seq_devs - channels
    parts = [signal, in_gate]
    if spare:
        parts = [jnp.pad(part, ((0, spare), (0, 0))) for part in parts]
        short_taps = jnp.pad(short_taps, ((0, spare), (0, 0)))
        skip_gain = jnp.pad(skip_gain, (0, spare))
        decay_rate = jnp.pad(decay_rate, (0, spare), mode="edge")
        out_weight = jnp.pad(out_weight, ((0, 0), (0, spare)))
    parts = jnp.stack([part.reshape(seq_devs, own, local_len) for part in parts], axis=1)
    parts = lax.all_to_all(parts, "seq", split_axis=0, concat_axis=0, tiled=True)
    params = (
        embed_weight,
        embed_bias[None, :],
        sine_freq[None, :],
        mid_weight,
        mid_bias[None, :],
        out_weight,
        decay_rate[None, :],
        skip_gain[None, :],
        short_taps,
    )
    shared = make_filter(params, own, seq_devs * local_len)
    mixed = mix(parts, shared)
    coded = lax.all_to_all(mixed, "seq", split_axis=0, concat_axis=0, tiled=True)[:channels]
    scale = jnp.concatenate([coded[:, local_len:]] * (local_len // LANES), axis=1)
    vals = decode_group(coded[:, :local_len], scale)
    return (out_gate.astype(F32) * vals).astype(BF16)


def solution(mesh):
    in_specs = (
        P("ch", "seq"),
        P("ch", "seq"),
        P("ch", "seq"),
        P("ch", None),
        P("ch"),
        P("ch"),
        P(),
        P(),
        P(),
        P(),
        P(),
        P(None, "ch"),
    )
    out_specs = P("ch", "seq")
    return jax.shard_map(
        on_device, mesh=mesh, in_specs=in_specs, out_specs=out_specs, check_vma=False
    )
```

```python
import functools
import math

import jax
import jax.numpy as jnp
import numpy as np
from jax import lax
from jax.experimental import pallas as pl
from jax.experimental.pallas import tpu as pltpu
from jax.sharding import PartitionSpec as P

BANDS = 16
LANES = 128
GROUPS = 4
TILES = 2
SPAN = 120.0
ORDER_SEED = 115
F32 = jnp.float32
BF16 = jnp.bfloat16
in_space = pltpu.with_memory_space_constraint


def round_up(count, step):
    return (count + step - 1) // step * step


def halves(table):
    high = table.astype(BF16)
    low = (table - high.astype(np.float64)).astype(BF16)
    return high, low


@functools.lru_cache(maxsize=None)
def embed_table(full_len):
    positions = np.arange(full_len, dtype=np.int64)
    rows = [positions / full_len]
    phase = positions
    for _ in range(BANDS):
        angle = phase * (2.0 * math.pi / full_len)
        rows += [np.cos(angle), np.sin(angle)]
        phase = 2 * phase % full_len
    rows.append(np.ones(full_len))
    table = np.zeros((round_up(len(rows), 8), full_len))
    table[: len(rows)] = np.stack(rows)
    first, rest = halves(table)
    second, third = halves(table - first.astype(np.float64))
    stacked = np.concatenate([first, second, third], axis=0)
    return np.pad(stacked, ((0, -len(stacked) % 16), (0, 0)))


@functools.lru_cache(maxsize=None)
def transform_tables(full_len):
    blocks = full_len // LANES
    a = np.arange(blocks)
    k1 = np.arange(blocks)
    b = np.arange(LANES)
    theta = 2.0 * math.pi / blocks * ((4 * k1 + 1)[:, None] * a[None, :] % (4 * blocks)) / 4.0
    phi = 2.0 * math.pi / full_len * ((4 * k1 + 1)[:, None] * b[None, :]) / 4.0
    psi = 2.0 * math.pi / LANES * (b[:, None] * b[None, :] % LANES)
    outer_high, outer_low = halves(np.concatenate([np.cos(theta), -np.sin(theta)], axis=0))
    outer = np.concatenate([outer_high, outer_high, outer_low], axis=1)
    back = np.concatenate([np.cos(theta).T, -np.sin(theta).T], axis=1) / full_len
    back_high, back_low = halves(back)
    outer_back = np.concatenate([back_high, back_high, back_low], axis=1)
    twiddle = np.stack([np.cos(phi), np.sin(phi)]).astype(np.float32)
    cos_in, sin_in = np.cos(psi), np.sin(psi)
    inner = np.stack(halves(np.block([[cos_in, -sin_in], [sin_in, cos_in]])))
    inner_back = np.stack(halves(np.block([[cos_in, sin_in], [-sin_in, cos_in]])))
    return outer, twiddle, inner, inner_back, outer_back


def sine_fit(terms):
    nodes = np.cos((np.arange(400) + 0.5) * math.pi / 400) * 0.5
    basis = np.stack([nodes ** (2 * p + 1) for p in range(terms)], axis=1)
    fit = np.linalg.lstsq(basis, np.sin(2.0 * math.pi * nodes), rcond=None)[0]
    return [float(v) for v in fit]


SINE_FIT = sine_fit(6)


def sine_of_turns(turns):
    part = turns - jnp.round(turns)
    square = part * part
    value = SINE_FIT[-1]
    for term in SINE_FIT[-2::-1]:
        value = value * square + term
    return value * part


def split_two(vals):
    high = vals.astype(BF16)
    return high, (vals - high.astype(F32)).astype(BF16)


def split_three(vals):
    first = vals.astype(BF16).astype(F32)
    rest = vals - first
    second = rest.astype(BF16).astype(F32)
    return first, second, rest - second


def matmul(lhs, rhs):
    return jnp.dot(lhs, rhs, preferred_element_type=F32)


def stack_three(vals):
    high, low = split_two(vals)
    return jnp.concatenate([high, low, high], axis=0)


def inner_product(vals, table_ref):
    high, low = split_two(vals)
    return (
        matmul(high, table_ref[0]) + matmul(low, table_ref[0]) + matmul(high, table_ref[1])
    )


def outer_forward(columns, outer_ref, twiddle_ref):
    blocks = columns[0].shape[0]
    mixed = matmul(outer_ref[...], stack_three(jnp.concatenate(columns, axis=1)))
    cos_vals, sin_vals = twiddle_ref[0], twiddle_ref[1]
    rows = []
    for c in range(len(columns)):
        real = mixed[:blocks, c * LANES : (c + 1) * LANES]
        imag = mixed[blocks:, c * LANES : (c + 1) * LANES]
        rows.append(
            jnp.concatenate(
                [real * cos_vals + imag * sin_vals, imag * cos_vals - real * sin_vals], axis=1
            )
        )
    return rows


def outer_backward(vals, channels, twiddle_ref, outer_back_ref):
    blocks = vals.shape[0] // channels
    cos_vals, sin_vals = twiddle_ref[0], twiddle_ref[1]
    columns = []
    for c in range(channels):
        real = vals[c * blocks : (c + 1) * blocks, :LANES]
        imag = vals[c * blocks : (c + 1) * blocks, LANES:]
        columns.append(
            jnp.concatenate(
                [real * cos_vals - imag * sin_vals, imag * cos_vals + real * sin_vals], axis=0
            )
        )
    return matmul(outer_back_ref[...], stack_three(jnp.concatenate(columns, axis=1)))


def code_group(columns):
    top = functools.reduce(jnp.maximum, [jnp.abs(column) for column in columns])
    scale = lax.reduce_precision(jnp.maximum(top, 1e-30) * (1.0 + 1.0 / 128), 8, 7)
    factor = 2.0 * SPAN / scale
    codes = []
    for column in columns:
        size = jnp.exp2(jnp.abs(column) * factor - SPAN)
        codes.append(jnp.where(column < 0, -size, size).astype(BF16))
    return codes, scale.astype(BF16)


def decode_group(codes, scale):
    codes = codes.astype(F32)
    share = jnp.log(jnp.abs(codes)) * (0.5 / SPAN / math.log(2.0)) + 0.5
    return jnp.where(codes < 0, -share, share) * scale.astype(F32)


def exchange_order(count):
    return [int(place) for place in np.random.RandomState(ORDER_SEED).permutation(count)]


def exchange(chunks, order):
    return lax.all_to_all(
        chunks, "seq", split_axis=0, concat_axis=0, tiled=True, axis_index_groups=[order]
    )


def filter_kernel(
    own,
    embed_hbm,
    embed_weight_hbm,
    embed_bias_hbm,
    sine_freq_hbm,
    mid_weight_hbm,
    mid_bias_hbm,
    out_weight_hbm,
    decay_hbm,
    skip_hbm,
    taps_hbm,
    outer_hbm,
    twiddle_hbm,
    inner_hbm,
    inner_back_hbm,
    outer_back_hbm,
    spectrum_ref,
    toeplitz_ref,
    skip_ref,
    outer_ref,
    twiddle_ref,
    inner_ref,
    inner_back_ref,
    outer_back_ref,
    embed_ref,
    embed_weight_ref,
    embed_bias_ref,
    sine_freq_ref,
    mid_weight_ref,
    mid_bias_ref,
    out_weight_ref,
    decay_ref,
    skip_row_ref,
    taps_ref,
    pad_ref,
    vec_ref,
    row_ref,
    column_ref,
    out_rows_ref,
    filter_ref,
    sems,
    embed_sems,
):
    full_len = embed_ref.shape[1]
    tile_len = full_len // TILES
    hidden = mid_weight_ref.shape[0]
    pairs = [
        (embed_weight_hbm, embed_weight_ref),
        (embed_bias_hbm, embed_bias_ref),
        (sine_freq_hbm, sine_freq_ref),
        (mid_weight_hbm, mid_weight_ref),
        (mid_bias_hbm, mid_bias_ref),
        (out_weight_hbm, out_weight_ref),
        (decay_hbm, decay_ref),
        (skip_hbm, skip_row_ref),
        (taps_hbm, taps_ref),
        (outer_hbm, outer_ref),
        (twiddle_hbm, twiddle_ref),
        (inner_hbm, inner_ref),
        (inner_back_hbm, inner_back_ref),
        (outer_back_hbm, outer_back_ref),
    ]
    copies = [pltpu.make_async_copy(*pair, sems.at[i]) for i, pair in enumerate(pairs)]
    embed_copies = []
    for i in range(TILES):
        lanes = pl.ds(i * tile_len, tile_len)
        embed_copies.append(
            pltpu.make_async_copy(
                embed_hbm.at[:, lanes], embed_ref.at[:, lanes], embed_sems.at[i]
            )
        )
    for copy in copies[:8] + embed_copies + copies[8:]:
        copy.start()
    seq_index = lax.axis_index("seq")
    first_channel = 0
    for place, device in enumerate(exchange_order(lax.axis_size("seq"))):
        first_channel = jnp.where(seq_index == device, place * own, first_channel)
    first_channel = pl.multiple_of(first_channel, own)
    pad_ref[...] = jnp.zeros_like(pad_ref)
    vec_ref[...] = jnp.zeros_like(vec_ref)
    row_ref[...] = jnp.zeros_like(row_ref)
    for copy in copies[:8]:
        copy.wait()

    freq = sine_freq_ref[...] * (0.5 / math.pi)
    features = embed_weight_ref.shape[0]
    pad_ref[:features, :] = embed_weight_ref[...] * freq
    pad_ref[features : features + 1, :] = embed_bias_ref[...] * freq
    one, two, three = split_three(pad_ref[...])
    none = jnp.zeros_like(one)
    rest = jnp.zeros((embed_ref.shape[0] - 3 * one.shape[0], hidden), F32)
    weight_one = jnp.concatenate(
        [
            jnp.concatenate([one, one, one, rest], axis=0).T,
            jnp.concatenate([two, two, none, rest], axis=0).T,
            jnp.concatenate([three, none, none, rest], axis=0).T,
        ],
        axis=0,
    ).astype(BF16)
    one, two, _ = split_three(mid_weight_ref[...] * freq)
    weight_two = jnp.concatenate([one, one, two], axis=0).T.astype(BF16)
    vec_ref[0:1, :] = mid_bias_ref[...] * freq
    bias_two = vec_ref[...].T[:, 0:1]
    one, two, _ = split_three(out_weight_ref[...])
    out_rows_ref[0] = jnp.concatenate([one, one], axis=0).T
    out_rows_ref[1] = jnp.concatenate([two, two], axis=0).T
    own_rows = pl.ds(first_channel, own)
    weight_three = jnp.concatenate(
        [out_rows_ref[0, own_rows, :], out_rows_ref[1, own_rows, :]], axis=0
    ).astype(BF16)
    row_ref[0:1, :] = decay_ref[...]
    row_ref[1:2, :] = skip_row_ref[...]
    column_ref[...] = row_ref[...].T
    decay = column_ref[own_rows, 0:1]
    skip_ref[...] = jnp.broadcast_to(column_ref[own_rows, 1:2], skip_ref.shape)
    scale = jnp.sqrt(2.0 * decay)

    for i in range(TILES):
        start = i * tile_len
        embed_copies[i].wait()
        turns = matmul(weight_one, embed_ref[:, start : start + tile_len])
        first = sine_of_turns(
            turns[:hidden] + turns[hidden : 2 * hidden] + turns[2 * hidden :]
        )
        second = sine_of_turns(matmul(weight_two, stack_three(first)) + bias_two)
        raw = matmul(weight_three, jnp.concatenate(split_two(second), axis=0))
        positions = (start + lax.broadcasted_iota(jnp.int32, (own, tile_len), 1)).astype(F32)
        vals = (raw[:own] + raw[own:]) * (scale * jnp.exp(-decay * positions))
        for j in range(tile_len // LANES):
            row = (start // LANES + j) * own
            filter_ref[row : row + own, :] = vals[:, j * LANES : (j + 1) * LANES]

    for copy in copies[8:]:
        copy.wait()
    blocks = full_len // LANES
    columns = [filter_ref[pl.ds(c, blocks, stride=own), :] for c in range(own)]
    spectrum_ref[...] = inner_product(
        jnp.concatenate(outer_forward(columns, outer_ref, twiddle_ref), axis=0), inner_ref
    )
    taps = taps_ref[own_rows, :]
    tap_count = taps.shape[1]
    square = (tap_count, tap_count)
    upper = lax.broadcasted_iota(jnp.int32, square, 1) >= lax.broadcasted_iota(
        jnp.int32, square, 0
    )
    for c in range(own):
        lags = pltpu.roll(
            jnp.broadcast_to(taps[c : c + 1], square), 0, 1, stride=1, stride_axis=0
        )
        high, low = split_two(
            jnp.concatenate([jnp.where(upper, 0.0, lags), jnp.where(upper, lags, 0.0)], axis=0)
        )
        toeplitz_ref[c] = jnp.concatenate([high, low], axis=1)


def mix_kernel(
    own,
    parts_ref,
    spectrum_ref,
    toeplitz_ref,
    skip_ref,
    outer_ref,
    twiddle_ref,
    inner_ref,
    inner_back_ref,
    outer_back_ref,
    out_ref,
    signal_ref,
    in_gate_ref,
    mixed_ref,
):
    seq_devs, _, _, local_len = parts_ref.shape
    local_blocks = local_len // LANES
    part_rows = local_blocks * own
    blocks = seq_devs * local_blocks
    signal_ref[:own, :] = jnp.zeros((own, LANES), F32)
    order = exchange_order(seq_devs)
    for place, p in enumerate(order):
        for q in range(local_blocks):
            at = p * part_rows + q * own
            lanes = slice(q * LANES, (q + 1) * LANES)
            signal_ref[own + at : 2 * own + at, :] = parts_ref[place, 0, :, lanes].astype(F32)
            in_gate_ref[at : at + own, :] = parts_ref[place, 1, :, lanes].astype(F32)
    gated = []
    for c in range(own):
        window = jnp.concatenate(
            [
                signal_ref[pl.ds(c, blocks, stride=own), :],
                signal_ref[pl.ds(own + c, blocks, stride=own), :],
            ],
            axis=1,
        ).astype(BF16)
        both = matmul(window, toeplitz_ref[c])
        gated.append(
            in_gate_ref[pl.ds(c, blocks, stride=own), :] * (both[:, :LANES] + both[:, LANES:])
        )
    mid = outer_forward(gated, outer_ref, twiddle_ref)
    step = max(1, own // GROUPS)
    backs = []
    for start in range(0, own, step):
        rows = slice(start * blocks, (start + step) * blocks)
        vals = inner_product(jnp.concatenate(mid[start : start + step], axis=0), inner_ref)
        real, imag = vals[:, :LANES], vals[:, LANES:]
        filt_real, filt_imag = spectrum_ref[rows, :LANES], spectrum_ref[rows, LANES:]
        product = jnp.concatenate(
            [real * filt_real - imag * filt_imag, real * filt_imag + imag * filt_real], axis=1
        )
        backs.append(inner_product(product, inner_back_ref))
    conv = outer_backward(jnp.concatenate(backs, axis=0), own, twiddle_ref, outer_back_ref)
    for c in range(own):
        mixed_ref[pl.ds(c, blocks, stride=own), :] = (
            conv[:, c * LANES : (c + 1) * LANES] + skip_ref[c : c + 1, :] * gated[c]
        )
    columns = []
    for q in range(local_blocks):
        if own % 8 == 0:
            column = jnp.concatenate(
                [
                    mixed_ref[p * part_rows + q * own : p * part_rows + (q + 1) * own, :]
                    for p in order
                ],
                axis=0,
            )
        else:
            for place, p in enumerate(order):
                at = p * part_rows + q * own
                signal_ref[place * own : (place + 1) * own, :] = mixed_ref[at : at + own, :]
            column = signal_ref[: seq_devs * own, :]
        columns.append(column)
    codes, scale = code_group(columns)
    for q in range(local_blocks):
        out_ref[:, q * LANES : (q + 1) * LANES] = codes[q]
    out_ref[:, local_len:] = scale


def make_filter(params, own, full_len):
    blocks = full_len // LANES
    hidden, channels = params[5].shape
    tap_count = params[8].shape[1]
    embed = embed_table(full_len)
    tables = transform_tables(full_len)
    operands = (embed,) + params + tables
    padded = round_up(params[0].shape[0] + 1, 8)
    return pl.pallas_call(
        functools.partial(filter_kernel, own),
        out_shape=(
            pltpu.VMEM((own * blocks, 2 * LANES), F32),
            pltpu.VMEM((own, 2 * tap_count, 2 * tap_count), BF16),
            pltpu.VMEM((own, LANES), F32),
        )
        + tuple(pltpu.VMEM(table.shape, table.dtype) for table in tables),
        in_specs=[pl.BlockSpec(memory_space=pltpu.HBM)] * len(operands),
        out_specs=(pl.BlockSpec(memory_space=pltpu.VMEM),) * (3 + len(tables)),
        scratch_shapes=[pltpu.VMEM(embed.shape, BF16)]
        + [pltpu.VMEM(vals.shape, F32) for vals in params]
        + [
            pltpu.VMEM((padded, hidden), F32),
            pltpu.VMEM((8, hidden), F32),
            pltpu.VMEM((8, channels), F32),
            pltpu.VMEM((channels, 8), F32),
            pltpu.VMEM((2, channels, 2 * hidden), F32),
            pltpu.VMEM(((blocks + 1) * own, LANES), F32),
            pltpu.SemaphoreType.DMA((len(operands) - 1,)),
            pltpu.SemaphoreType.DMA((TILES,)),
        ],
        compiler_params=pltpu.CompilerParams(vmem_limit_bytes=48 * 2**20),
    )(*[in_space(jnp.asarray(vals), pltpu.HBM) for vals in operands])


def mix(parts, shared):
    seq_devs, _, own, local_len = parts.shape
    rows = seq_devs * own * (local_len // LANES)
    vmem = pl.BlockSpec(memory_space=pltpu.VMEM)
    return pl.pallas_call(
        functools.partial(mix_kernel, own),
        out_shape=jax.ShapeDtypeStruct((seq_devs * own, local_len + LANES), BF16),
        in_specs=[vmem] * (1 + len(shared)),
        out_specs=vmem,
        scratch_shapes=[pltpu.VMEM((rows + 2 * own, LANES), F32)]
        + [pltpu.VMEM((rows + own, LANES), F32)] * 2,
        compiler_params=pltpu.CompilerParams(vmem_limit_bytes=48 * 2**20),
    )(parts, *[in_space(vals, pltpu.VMEM) for vals in shared])


def on_device(
    signal,
    in_gate,
    out_gate,
    short_taps,
    skip_gain,
    decay_rate,
    embed_weight,
    embed_bias,
    sine_freq,
    mid_weight,
    mid_bias,
    out_weight,
):
    channels, local_len = signal.shape
    seq_devs = lax.axis_size("seq")
    own = -(-channels // seq_devs)
    spare = own * seq_devs - channels
    parts = [signal, in_gate]
    if spare:
        parts = [jnp.pad(part, ((0, spare), (0, 0))) for part in parts]
        short_taps = jnp.pad(short_taps, ((0, spare), (0, 0)))
        skip_gain = jnp.pad(skip_gain, (0, spare))
        decay_rate = jnp.pad(decay_rate, (0, spare), mode="edge")
        out_weight = jnp.pad(out_weight, ((0, 0), (0, spare)))
    parts = jnp.stack([part.reshape(seq_devs, own, local_len) for part in parts], axis=1)
    order = exchange_order(seq_devs)
    parts = exchange(parts, order)
    params = (
        embed_weight,
        embed_bias[None, :],
        sine_freq[None, :],
        mid_weight,
        mid_bias[None, :],
        out_weight,
        decay_rate[None, :],
        skip_gain[None, :],
        short_taps,
    )
    shared = make_filter(params, own, seq_devs * local_len)
    mixed = mix(parts, shared)
    coded = exchange(mixed.reshape(seq_devs, own, -1), order).reshape(
        seq_devs * own, -1
    )[:channels]
    scale = jnp.concatenate([coded[:, local_len:]] * (local_len // LANES), axis=1)
    vals = decode_group(coded[:, :local_len], scale)
    return (out_gate.astype(F32) * vals).astype(BF16)


def solution(mesh):
    in_specs = (
        P("ch", "seq"),
        P("ch", "seq"),
        P("ch", "seq"),
        P("ch", None),
        P("ch"),
        P("ch"),
        P(),
        P(),
        P(),
        P(),
        P(),
        P(None, "ch"),
    )
    out_specs = P("ch", "seq")
    return jax.shard_map(
        on_device, mesh=mesh, in_specs=in_specs, out_specs=out_specs, check_vma=False
    )
```

```python
import functools
import math

import jax
import jax.numpy as jnp
import numpy as np
from jax import lax
from jax.experimental import pallas as pl
from jax.experimental.pallas import tpu as pltpu
from jax.sharding import PartitionSpec as P

BANDS = 16
LANES = 128
GROUPS = 4
TILES = 2
SPAN = 120.0
F32 = jnp.float32
BF16 = jnp.bfloat16
in_space = pltpu.with_memory_space_constraint


def round_up(count, step):
    return (count + step - 1) // step * step


def halves(table):
    high = table.astype(BF16)
    low = (table - high.astype(np.float64)).astype(BF16)
    return high, low


@functools.lru_cache(maxsize=None)
def embed_table(full_len):
    positions = np.arange(full_len, dtype=np.int64)
    rows = [positions / full_len]
    phase = positions
    for _ in range(BANDS):
        angle = phase * (2.0 * math.pi / full_len)
        rows += [np.cos(angle), np.sin(angle)]
        phase = 2 * phase % full_len
    rows.append(np.ones(full_len))
    table = np.zeros((round_up(len(rows), 8), full_len))
    table[: len(rows)] = np.stack(rows)
    first, rest = halves(table)
    second, third = halves(table - first.astype(np.float64))
    stacked = np.concatenate([first, second, third], axis=0)
    return np.pad(stacked, ((0, -len(stacked) % 16), (0, 0)))


@functools.lru_cache(maxsize=None)
def transform_tables(full_len):
    blocks = full_len // LANES
    a = np.arange(blocks)
    k1 = np.arange(blocks)
    b = np.arange(LANES)
    theta = 2.0 * math.pi / blocks * ((4 * k1 + 1)[:, None] * a[None, :] % (4 * blocks)) / 4.0
    phi = 2.0 * math.pi / full_len * ((4 * k1 + 1)[:, None] * b[None, :]) / 4.0
    psi = 2.0 * math.pi / LANES * (b[:, None] * b[None, :] % LANES)
    outer_high, outer_low = halves(np.concatenate([np.cos(theta), -np.sin(theta)], axis=0))
    outer = np.concatenate([outer_high, outer_high, outer_low], axis=1)
    back = np.concatenate([np.cos(theta).T, -np.sin(theta).T], axis=1) / full_len
    back_high, back_low = halves(back)
    outer_back = np.concatenate([back_high, back_high, back_low], axis=1)
    twiddle = np.stack([np.cos(phi), np.sin(phi)]).astype(np.float32)
    cos_in, sin_in = np.cos(psi), np.sin(psi)
    inner = np.stack(halves(np.block([[cos_in, -sin_in], [sin_in, cos_in]])))
    inner_back = np.stack(halves(np.block([[cos_in, sin_in], [-sin_in, cos_in]])))
    return outer, twiddle, inner, inner_back, outer_back


def sine_fit(terms):
    nodes = np.cos((np.arange(400) + 0.5) * math.pi / 400) * 0.5
    basis = np.stack([nodes ** (2 * p + 1) for p in range(terms)], axis=1)
    fit = np.linalg.lstsq(basis, np.sin(2.0 * math.pi * nodes), rcond=None)[0]
    return [float(v) for v in fit]


SINE_FIT = sine_fit(6)


def sine_of_turns(turns):
    part = turns - jnp.round(turns)
    square = part * part
    value = SINE_FIT[-1]
    for term in SINE_FIT[-2::-1]:
        value = value * square + term
    return value * part


def split_two(vals):
    high = vals.astype(BF16)
    return high, (vals - high.astype(F32)).astype(BF16)


def split_three(vals):
    first = vals.astype(BF16).astype(F32)
    rest = vals - first
    second = rest.astype(BF16).astype(F32)
    return first, second, rest - second


def matmul(lhs, rhs):
    return jnp.dot(lhs, rhs, preferred_element_type=F32)


def stack_three(vals):
    high, low = split_two(vals)
    return jnp.concatenate([high, low, high], axis=0)


def inner_product(vals, table_ref):
    high, low = split_two(vals)
    return (
        matmul(high, table_ref[0]) + matmul(low, table_ref[0]) + matmul(high, table_ref[1])
    )


def outer_forward(columns, outer_ref, twiddle_ref):
    blocks = columns[0].shape[0]
    mixed = matmul(outer_ref[...], stack_three(jnp.concatenate(columns, axis=1)))
    cos_vals, sin_vals = twiddle_ref[0], twiddle_ref[1]
    rows = []
    for c in range(len(columns)):
        real = mixed[:blocks, c * LANES : (c + 1) * LANES]
        imag = mixed[blocks:, c * LANES : (c + 1) * LANES]
        rows.append(
            jnp.concatenate(
                [real * cos_vals + imag * sin_vals, imag * cos_vals - real * sin_vals], axis=1
            )
        )
    return rows


def outer_backward(vals, channels, twiddle_ref, outer_back_ref):
    blocks = vals.shape[0] // channels
    cos_vals, sin_vals = twiddle_ref[0], twiddle_ref[1]
    columns = []
    for c in range(channels):
        real = vals[c * blocks : (c + 1) * blocks, :LANES]
        imag = vals[c * blocks : (c + 1) * blocks, LANES:]
        columns.append(
            jnp.concatenate(
                [real * cos_vals - imag * sin_vals, imag * cos_vals + real * sin_vals], axis=0
            )
        )
    return matmul(outer_back_ref[...], stack_three(jnp.concatenate(columns, axis=1)))


def code_group(columns):
    top = functools.reduce(jnp.maximum, [jnp.abs(column) for column in columns])
    scale = lax.reduce_precision(jnp.maximum(top, 1e-30) * (1.0 + 1.0 / 128), 8, 7)
    factor = 2.0 * SPAN / scale
    codes = []
    for column in columns:
        size = jnp.exp2(jnp.abs(column) * factor - SPAN)
        codes.append(jnp.where(column < 0, -size, size).astype(BF16))
    return codes, scale.astype(BF16)


def decode_group(codes, scale):
    codes = codes.astype(F32)
    share = jnp.log(jnp.abs(codes)) * (0.5 / SPAN / math.log(2.0)) + 0.5
    return jnp.where(codes < 0, -share, share) * scale.astype(F32)


def exchange_order(count):
    first = count // 2 + count // 8
    return [(first + place) % count for place in range(count)]


def exchange(chunks, order):
    return lax.all_to_all(
        chunks, "seq", split_axis=0, concat_axis=0, tiled=True, axis_index_groups=[order]
    )


def filter_kernel(
    own,
    embed_hbm,
    embed_weight_hbm,
    embed_bias_hbm,
    sine_freq_hbm,
    mid_weight_hbm,
    mid_bias_hbm,
    out_weight_hbm,
    decay_hbm,
    skip_hbm,
    taps_hbm,
    outer_hbm,
    twiddle_hbm,
    inner_hbm,
    inner_back_hbm,
    outer_back_hbm,
    spectrum_ref,
    toeplitz_ref,
    skip_ref,
    outer_ref,
    twiddle_ref,
    inner_ref,
    inner_back_ref,
    outer_back_ref,
    embed_ref,
    embed_weight_ref,
    embed_bias_ref,
    sine_freq_ref,
    mid_weight_ref,
    mid_bias_ref,
    out_weight_ref,
    decay_ref,
    skip_row_ref,
    taps_ref,
    pad_ref,
    vec_ref,
    row_ref,
    column_ref,
    out_rows_ref,
    filter_ref,
    sems,
    embed_sems,
):
    full_len = embed_ref.shape[1]
    tile_len = full_len // TILES
    hidden = mid_weight_ref.shape[0]
    pairs = [
        (embed_weight_hbm, embed_weight_ref),
        (embed_bias_hbm, embed_bias_ref),
        (sine_freq_hbm, sine_freq_ref),
        (mid_weight_hbm, mid_weight_ref),
        (mid_bias_hbm, mid_bias_ref),
        (out_weight_hbm, out_weight_ref),
        (decay_hbm, decay_ref),
        (skip_hbm, skip_row_ref),
        (taps_hbm, taps_ref),
        (outer_hbm, outer_ref),
        (twiddle_hbm, twiddle_ref),
        (inner_hbm, inner_ref),
        (inner_back_hbm, inner_back_ref),
        (outer_back_hbm, outer_back_ref),
    ]
    copies = [pltpu.make_async_copy(*pair, sems.at[i]) for i, pair in enumerate(pairs)]
    embed_copies = []
    for i in range(TILES):
        lanes = pl.ds(i * tile_len, tile_len)
        embed_copies.append(
            pltpu.make_async_copy(
                embed_hbm.at[:, lanes], embed_ref.at[:, lanes], embed_sems.at[i]
            )
        )
    for copy in copies[:8] + embed_copies + copies[8:]:
        copy.start()
    seq_index = lax.axis_index("seq")
    first_channel = 0
    for place, device in enumerate(exchange_order(lax.axis_size("seq"))):
        first_channel = jnp.where(seq_index == device, place * own, first_channel)
    first_channel = pl.multiple_of(first_channel, own)
    pad_ref[...] = jnp.zeros_like(pad_ref)
    vec_ref[...] = jnp.zeros_like(vec_ref)
    row_ref[...] = jnp.zeros_like(row_ref)
    for copy in copies[:8]:
        copy.wait()

    freq = sine_freq_ref[...] * (0.5 / math.pi)
    features = embed_weight_ref.shape[0]
    pad_ref[:features, :] = embed_weight_ref[...] * freq
    pad_ref[features : features + 1, :] = embed_bias_ref[...] * freq
    one, two, three = split_three(pad_ref[...])
    none = jnp.zeros_like(one)
    rest = jnp.zeros((embed_ref.shape[0] - 3 * one.shape[0], hidden), F32)
    weight_one = jnp.concatenate(
        [
            jnp.concatenate([one, one, one, rest], axis=0).T,
            jnp.concatenate([two, two, none, rest], axis=0).T,
            jnp.concatenate([three, none, none, rest], axis=0).T,
        ],
        axis=0,
    ).astype(BF16)
    one, two, _ = split_three(mid_weight_ref[...] * freq)
    weight_two = jnp.concatenate([one, one, two], axis=0).T.astype(BF16)
    vec_ref[0:1, :] = mid_bias_ref[...] * freq
    bias_two = vec_ref[...].T[:, 0:1]
    one, two, _ = split_three(out_weight_ref[...])
    out_rows_ref[0] = jnp.concatenate([one, one], axis=0).T
    out_rows_ref[1] = jnp.concatenate([two, two], axis=0).T
    own_rows = pl.ds(first_channel, own)
    weight_three = jnp.concatenate(
        [out_rows_ref[0, own_rows, :], out_rows_ref[1, own_rows, :]], axis=0
    ).astype(BF16)
    row_ref[0:1, :] = decay_ref[...]
    row_ref[1:2, :] = skip_row_ref[...]
    column_ref[...] = row_ref[...].T
    decay = column_ref[own_rows, 0:1]
    skip_ref[...] = jnp.broadcast_to(column_ref[own_rows, 1:2], skip_ref.shape)
    scale = jnp.sqrt(2.0 * decay)

    for i in range(TILES):
        start = i * tile_len
        embed_copies[i].wait()
        turns = matmul(weight_one, embed_ref[:, start : start + tile_len])
        first = sine_of_turns(
            turns[:hidden] + turns[hidden : 2 * hidden] + turns[2 * hidden :]
        )
        second = sine_of_turns(matmul(weight_two, stack_three(first)) + bias_two)
        raw = matmul(weight_three, jnp.concatenate(split_two(second), axis=0))
        positions = (start + lax.broadcasted_iota(jnp.int32, (own, tile_len), 1)).astype(F32)
        vals = (raw[:own] + raw[own:]) * (scale * jnp.exp(-decay * positions))
        for j in range(tile_len // LANES):
            row = (start // LANES + j) * own
            filter_ref[row : row + own, :] = vals[:, j * LANES : (j + 1) * LANES]

    for copy in copies[8:]:
        copy.wait()
    blocks = full_len // LANES
    columns = [filter_ref[pl.ds(c, blocks, stride=own), :] for c in range(own)]
    spectrum_ref[...] = inner_product(
        jnp.concatenate(outer_forward(columns, outer_ref, twiddle_ref), axis=0), inner_ref
    )
    taps = taps_ref[own_rows, :]
    tap_count = taps.shape[1]
    square = (tap_count, tap_count)
    upper = lax.broadcasted_iota(jnp.int32, square, 1) >= lax.broadcasted_iota(
        jnp.int32, square, 0
    )
    for c in range(own):
        lags = pltpu.roll(
            jnp.broadcast_to(taps[c : c + 1], square), 0, 1, stride=1, stride_axis=0
        )
        high, low = split_two(
            jnp.concatenate([jnp.where(upper, 0.0, lags), jnp.where(upper, lags, 0.0)], axis=0)
        )
        toeplitz_ref[c] = jnp.concatenate([high, low], axis=1)


def mix_kernel(
    own,
    parts_ref,
    spectrum_ref,
    toeplitz_ref,
    skip_ref,
    outer_ref,
    twiddle_ref,
    inner_ref,
    inner_back_ref,
    outer_back_ref,
    out_ref,
    signal_ref,
    in_gate_ref,
    mixed_ref,
):
    seq_devs, _, _, local_len = parts_ref.shape
    local_blocks = local_len // LANES
    part_rows = local_blocks * own
    blocks = seq_devs * local_blocks
    signal_ref[:own, :] = jnp.zeros((own, LANES), F32)
    order = exchange_order(seq_devs)
    for place, p in enumerate(order):
        for q in range(local_blocks):
            at = p * part_rows + q * own
            lanes = slice(q * LANES, (q + 1) * LANES)
            signal_ref[own + at : 2 * own + at, :] = parts_ref[place, 0, :, lanes].astype(F32)
            in_gate_ref[at : at + own, :] = parts_ref[place, 1, :, lanes].astype(F32)
    gated = []
    for c in range(own):
        window = jnp.concatenate(
            [
                signal_ref[pl.ds(c, blocks, stride=own), :],
                signal_ref[pl.ds(own + c, blocks, stride=own), :],
            ],
            axis=1,
        ).astype(BF16)
        both = matmul(window, toeplitz_ref[c])
        gated.append(
            in_gate_ref[pl.ds(c, blocks, stride=own), :] * (both[:, :LANES] + both[:, LANES:])
        )
    mid = outer_forward(gated, outer_ref, twiddle_ref)
    step = max(1, own // GROUPS)
    backs = []
    for start in range(0, own, step):
        rows = slice(start * blocks, (start + step) * blocks)
        vals = inner_product(jnp.concatenate(mid[start : start + step], axis=0), inner_ref)
        real, imag = vals[:, :LANES], vals[:, LANES:]
        filt_real, filt_imag = spectrum_ref[rows, :LANES], spectrum_ref[rows, LANES:]
        product = jnp.concatenate(
            [real * filt_real - imag * filt_imag, real * filt_imag + imag * filt_real], axis=1
        )
        backs.append(inner_product(product, inner_back_ref))
    conv = outer_backward(jnp.concatenate(backs, axis=0), own, twiddle_ref, outer_back_ref)
    for c in range(own):
        mixed_ref[pl.ds(c, blocks, stride=own), :] = (
            conv[:, c * LANES : (c + 1) * LANES] + skip_ref[c : c + 1, :] * gated[c]
        )
    columns = []
    for q in range(local_blocks):
        if own % 8 == 0:
            column = jnp.concatenate(
                [
                    mixed_ref[p * part_rows + q * own : p * part_rows + (q + 1) * own, :]
                    for p in order
                ],
                axis=0,
            )
        else:
            for place, p in enumerate(order):
                at = p * part_rows + q * own
                signal_ref[place * own : (place + 1) * own, :] = mixed_ref[at : at + own, :]
            column = signal_ref[: seq_devs * own, :]
        columns.append(column)
    codes, scale = code_group(columns)
    for q in range(local_blocks):
        out_ref[:, q * LANES : (q + 1) * LANES] = codes[q]
    out_ref[:, local_len:] = scale


def make_filter(params, own, full_len):
    blocks = full_len // LANES
    hidden, channels = params[5].shape
    tap_count = params[8].shape[1]
    embed = embed_table(full_len)
    tables = transform_tables(full_len)
    operands = (embed,) + params + tables
    padded = round_up(params[0].shape[0] + 1, 8)
    return pl.pallas_call(
        functools.partial(filter_kernel, own),
        out_shape=(
            pltpu.VMEM((own * blocks, 2 * LANES), F32),
            pltpu.VMEM((own, 2 * tap_count, 2 * tap_count), BF16),
            pltpu.VMEM((own, LANES), F32),
        )
        + tuple(pltpu.VMEM(table.shape, table.dtype) for table in tables),
        in_specs=[pl.BlockSpec(memory_space=pltpu.HBM)] * len(operands),
        out_specs=(pl.BlockSpec(memory_space=pltpu.VMEM),) * (3 + len(tables)),
        scratch_shapes=[pltpu.VMEM(embed.shape, BF16)]
        + [pltpu.VMEM(vals.shape, F32) for vals in params]
        + [
            pltpu.VMEM((padded, hidden), F32),
            pltpu.VMEM((8, hidden), F32),
            pltpu.VMEM((8, channels), F32),
            pltpu.VMEM((channels, 8), F32),
            pltpu.VMEM((2, channels, 2 * hidden), F32),
            pltpu.VMEM(((blocks + 1) * own, LANES), F32),
            pltpu.SemaphoreType.DMA((len(operands) - 1,)),
            pltpu.SemaphoreType.DMA((TILES,)),
        ],
        compiler_params=pltpu.CompilerParams(vmem_limit_bytes=48 * 2**20),
    )(*[in_space(jnp.asarray(vals), pltpu.HBM) for vals in operands])


def mix(parts, shared):
    seq_devs, _, own, local_len = parts.shape
    rows = seq_devs * own * (local_len // LANES)
    vmem = pl.BlockSpec(memory_space=pltpu.VMEM)
    return pl.pallas_call(
        functools.partial(mix_kernel, own),
        out_shape=jax.ShapeDtypeStruct((seq_devs * own, local_len + LANES), BF16),
        in_specs=[vmem] * (1 + len(shared)),
        out_specs=vmem,
        scratch_shapes=[pltpu.VMEM((rows + 2 * own, LANES), F32)]
        + [pltpu.VMEM((rows + own, LANES), F32)] * 2,
        compiler_params=pltpu.CompilerParams(vmem_limit_bytes=48 * 2**20),
    )(parts, *[in_space(vals, pltpu.VMEM) for vals in shared])


def on_device(
    signal,
    in_gate,
    out_gate,
    short_taps,
    skip_gain,
    decay_rate,
    embed_weight,
    embed_bias,
    sine_freq,
    mid_weight,
    mid_bias,
    out_weight,
):
    channels, local_len = signal.shape
    seq_devs = lax.axis_size("seq")
    own = -(-channels // seq_devs)
    spare = own * seq_devs - channels
    parts = [signal, in_gate]
    if spare:
        parts = [jnp.pad(part, ((0, spare), (0, 0))) for part in parts]
        short_taps = jnp.pad(short_taps, ((0, spare), (0, 0)))
        skip_gain = jnp.pad(skip_gain, (0, spare))
        decay_rate = jnp.pad(decay_rate, (0, spare), mode="edge")
        out_weight = jnp.pad(out_weight, ((0, 0), (0, spare)))
    parts = jnp.stack([part.reshape(seq_devs, own, local_len) for part in parts], axis=1)
    order = exchange_order(seq_devs)
    parts = exchange(parts, order)
    params = (
        embed_weight,
        embed_bias[None, :],
        sine_freq[None, :],
        mid_weight,
        mid_bias[None, :],
        out_weight,
        decay_rate[None, :],
        skip_gain[None, :],
        short_taps,
    )
    shared = make_filter(params, own, seq_devs * local_len)
    mixed = mix(parts, shared)
    coded = exchange(mixed.reshape(seq_devs, own, -1), order).reshape(
        seq_devs * own, -1
    )[:channels]
    scale = jnp.concatenate([coded[:, local_len:]] * (local_len // LANES), axis=1)
    vals = decode_group(coded[:, :local_len], scale)
    return (out_gate.astype(F32) * vals).astype(BF16)


def solution(mesh):
    in_specs = (
        P("ch", "seq"),
        P("ch", "seq"),
        P("ch", "seq"),
        P("ch", None),
        P("ch"),
        P("ch"),
        P(),
        P(),
        P(),
        P(),
        P(),
        P(None, "ch"),
    )
    out_specs = P("ch", "seq")
    return jax.shard_map(
        on_device, mesh=mesh, in_specs=in_specs, out_specs=out_specs, check_vma=False
    )
```

```python
import functools
import math

import jax
import jax.numpy as jnp
import numpy as np
from jax import lax
from jax.experimental import pallas as pl
from jax.experimental.pallas import tpu as pltpu
from jax.sharding import PartitionSpec as P

BANDS = 16
LANES = 128
GROUPS = 4
TILES = 2
F32 = jnp.float32
BF16 = jnp.bfloat16
in_space = pltpu.with_memory_space_constraint


def round_up(count, step):
    return (count + step - 1) // step * step


def halves(table):
    high = table.astype(BF16)
    low = (table - high.astype(np.float64)).astype(BF16)
    return high, low


@functools.lru_cache(maxsize=None)
def embed_table(full_len):
    positions = np.arange(full_len, dtype=np.int64)
    rows = [positions / full_len]
    phase = positions
    for _ in range(BANDS):
        angle = phase * (2.0 * math.pi / full_len)
        rows += [np.cos(angle), np.sin(angle)]
        phase = 2 * phase % full_len
    rows.append(np.ones(full_len))
    table = np.zeros((round_up(len(rows), 8), full_len))
    table[: len(rows)] = np.stack(rows)
    first, rest = halves(table)
    second, third = halves(table - first.astype(np.float64))
    stacked = np.concatenate([first, second, third], axis=0)
    return np.pad(stacked, ((0, -len(stacked) % 16), (0, 0)))


@functools.lru_cache(maxsize=None)
def transform_tables(full_len):
    blocks = full_len // LANES
    a = np.arange(blocks)
    k1 = np.arange(blocks)
    b = np.arange(LANES)
    theta = 2.0 * math.pi / blocks * ((4 * k1 + 1)[:, None] * a[None, :] % (4 * blocks)) / 4.0
    phi = 2.0 * math.pi / full_len * ((4 * k1 + 1)[:, None] * b[None, :]) / 4.0
    psi = 2.0 * math.pi / LANES * (b[:, None] * b[None, :] % LANES)
    outer_high, outer_low = halves(np.concatenate([np.cos(theta), -np.sin(theta)], axis=0))
    outer = np.concatenate([outer_high, outer_high, outer_low], axis=1)
    back = np.concatenate([np.cos(theta).T, -np.sin(theta).T], axis=1) / full_len
    back_high, back_low = halves(back)
    outer_back = np.concatenate([back_high, back_high, back_low], axis=1)
    twiddle = np.stack([np.cos(phi), np.sin(phi)]).astype(np.float32)
    cos_in, sin_in = np.cos(psi), np.sin(psi)
    inner = np.stack(halves(np.block([[cos_in, -sin_in], [sin_in, cos_in]])))
    inner_back = np.stack(halves(np.block([[cos_in, sin_in], [-sin_in, cos_in]])))
    return outer, twiddle, inner, inner_back, outer_back


def sine_fit(terms):
    nodes = np.cos((np.arange(400) + 0.5) * math.pi / 400) * 0.5
    basis = np.stack([nodes ** (2 * p + 1) for p in range(terms)], axis=1)
    fit = np.linalg.lstsq(basis, np.sin(2.0 * math.pi * nodes), rcond=None)[0]
    return [float(v) for v in fit]


SINE_FIT = sine_fit(6)


def sine_of_turns(turns):
    part = turns - jnp.round(turns)
    square = part * part
    value = SINE_FIT[-1]
    for term in SINE_FIT[-2::-1]:
        value = value * square + term
    return value * part


def split_two(vals):
    high = vals.astype(BF16)
    return high, (vals - high.astype(F32)).astype(BF16)


def split_three(vals):
    first = vals.astype(BF16).astype(F32)
    rest = vals - first
    second = rest.astype(BF16).astype(F32)
    return first, second, rest - second


def matmul(lhs, rhs):
    return jnp.dot(lhs, rhs, preferred_element_type=F32)


def stack_three(vals):
    high, low = split_two(vals)
    return jnp.concatenate([high, low, high], axis=0)


def inner_product(vals, table_ref):
    high, low = split_two(vals)
    return (
        matmul(high, table_ref[0]) + matmul(low, table_ref[0]) + matmul(high, table_ref[1])
    )


def outer_forward(columns, outer_ref, twiddle_ref):
    blocks = columns[0].shape[0]
    mixed = matmul(outer_ref[...], stack_three(jnp.concatenate(columns, axis=1)))
    cos_vals, sin_vals = twiddle_ref[0], twiddle_ref[1]
    rows = []
    for c in range(len(columns)):
        real = mixed[:blocks, c * LANES : (c + 1) * LANES]
        imag = mixed[blocks:, c * LANES : (c + 1) * LANES]
        rows.append(
            jnp.concatenate(
                [real * cos_vals + imag * sin_vals, imag * cos_vals - real * sin_vals], axis=1
            )
        )
    return rows


def outer_backward(vals, channels, twiddle_ref, outer_back_ref):
    blocks = vals.shape[0] // channels
    cos_vals, sin_vals = twiddle_ref[0], twiddle_ref[1]
    columns = []
    for c in range(channels):
        real = vals[c * blocks : (c + 1) * blocks, :LANES]
        imag = vals[c * blocks : (c + 1) * blocks, LANES:]
        columns.append(
            jnp.concatenate(
                [real * cos_vals - imag * sin_vals, imag * cos_vals + real * sin_vals], axis=0
            )
        )
    return matmul(outer_back_ref[...], stack_three(jnp.concatenate(columns, axis=1)))


def exchange_order(count):
    first = count // 2 + count // 8
    return [(first + place) % count for place in range(count)]


def exchange(chunks, order):
    return lax.all_to_all(
        chunks, "seq", split_axis=0, concat_axis=0, tiled=True, axis_index_groups=[order]
    )


def filter_kernel(
    own,
    embed_hbm,
    embed_weight_hbm,
    embed_bias_hbm,
    sine_freq_hbm,
    mid_weight_hbm,
    mid_bias_hbm,
    out_weight_hbm,
    decay_hbm,
    skip_hbm,
    taps_hbm,
    outer_hbm,
    twiddle_hbm,
    inner_hbm,
    inner_back_hbm,
    outer_back_hbm,
    spectrum_ref,
    toeplitz_ref,
    skip_ref,
    outer_ref,
    twiddle_ref,
    inner_ref,
    inner_back_ref,
    outer_back_ref,
    embed_ref,
    embed_weight_ref,
    embed_bias_ref,
    sine_freq_ref,
    mid_weight_ref,
    mid_bias_ref,
    out_weight_ref,
    decay_ref,
    skip_row_ref,
    taps_ref,
    pad_ref,
    vec_ref,
    row_ref,
    column_ref,
    out_rows_ref,
    filter_ref,
    sems,
    embed_sems,
):
    full_len = embed_ref.shape[1]
    tile_len = full_len // TILES
    hidden = mid_weight_ref.shape[0]
    pairs = [
        (embed_weight_hbm, embed_weight_ref),
        (embed_bias_hbm, embed_bias_ref),
        (sine_freq_hbm, sine_freq_ref),
        (mid_weight_hbm, mid_weight_ref),
        (mid_bias_hbm, mid_bias_ref),
        (out_weight_hbm, out_weight_ref),
        (decay_hbm, decay_ref),
        (skip_hbm, skip_row_ref),
        (taps_hbm, taps_ref),
        (outer_hbm, outer_ref),
        (twiddle_hbm, twiddle_ref),
        (inner_hbm, inner_ref),
        (inner_back_hbm, inner_back_ref),
        (outer_back_hbm, outer_back_ref),
    ]
    copies = [pltpu.make_async_copy(*pair, sems.at[i]) for i, pair in enumerate(pairs)]
    embed_copies = []
    for i in range(TILES):
        lanes = pl.ds(i * tile_len, tile_len)
        embed_copies.append(
            pltpu.make_async_copy(
                embed_hbm.at[:, lanes], embed_ref.at[:, lanes], embed_sems.at[i]
            )
        )
    for copy in copies[:8] + embed_copies + copies[8:]:
        copy.start()
    seq_index = lax.axis_index("seq")
    first_channel = 0
    for place, device in enumerate(exchange_order(lax.axis_size("seq"))):
        first_channel = jnp.where(seq_index == device, place * own, first_channel)
    first_channel = pl.multiple_of(first_channel, own)
    pad_ref[...] = jnp.zeros_like(pad_ref)
    vec_ref[...] = jnp.zeros_like(vec_ref)
    row_ref[...] = jnp.zeros_like(row_ref)
    for copy in copies[:8]:
        copy.wait()

    freq = sine_freq_ref[...] * (0.5 / math.pi)
    features = embed_weight_ref.shape[0]
    pad_ref[:features, :] = embed_weight_ref[...] * freq
    pad_ref[features : features + 1, :] = embed_bias_ref[...] * freq
    one, two, three = split_three(pad_ref[...])
    none = jnp.zeros_like(one)
    rest = jnp.zeros((embed_ref.shape[0] - 3 * one.shape[0], hidden), F32)
    weight_one = jnp.concatenate(
        [
            jnp.concatenate([one, one, one, rest], axis=0).T,
            jnp.concatenate([two, two, none, rest], axis=0).T,
            jnp.concatenate([three, none, none, rest], axis=0).T,
        ],
        axis=0,
    ).astype(BF16)
    one, two, _ = split_three(mid_weight_ref[...] * freq)
    weight_two = jnp.concatenate([one, one, two], axis=0).T.astype(BF16)
    vec_ref[0:1, :] = mid_bias_ref[...] * freq
    bias_two = vec_ref[...].T[:, 0:1]
    one, two, _ = split_three(out_weight_ref[...])
    out_rows_ref[0] = jnp.concatenate([one, one], axis=0).T
    out_rows_ref[1] = jnp.concatenate([two, two], axis=0).T
    own_rows = pl.ds(first_channel, own)
    weight_three = jnp.concatenate(
        [out_rows_ref[0, own_rows, :], out_rows_ref[1, own_rows, :]], axis=0
    ).astype(BF16)
    row_ref[0:1, :] = decay_ref[...]
    row_ref[1:2, :] = skip_row_ref[...]
    column_ref[...] = row_ref[...].T
    decay = column_ref[own_rows, 0:1]
    skip_ref[...] = jnp.broadcast_to(column_ref[own_rows, 1:2], skip_ref.shape)
    scale = jnp.sqrt(2.0 * decay)

    for i in range(TILES):
        start = i * tile_len
        embed_copies[i].wait()
        turns = matmul(weight_one, embed_ref[:, start : start + tile_len])
        first = sine_of_turns(
            turns[:hidden] + turns[hidden : 2 * hidden] + turns[2 * hidden :]
        )
        second = sine_of_turns(matmul(weight_two, stack_three(first)) + bias_two)
        raw = matmul(weight_three, jnp.concatenate(split_two(second), axis=0))
        positions = (start + lax.broadcasted_iota(jnp.int32, (own, tile_len), 1)).astype(F32)
        vals = (raw[:own] + raw[own:]) * (scale * jnp.exp(-decay * positions))
        for j in range(tile_len // LANES):
            row = (start // LANES + j) * own
            filter_ref[row : row + own, :] = vals[:, j * LANES : (j + 1) * LANES]

    for copy in copies[8:]:
        copy.wait()
    blocks = full_len // LANES
    columns = [filter_ref[pl.ds(c, blocks, stride=own), :] for c in range(own)]
    spectrum_ref[...] = inner_product(
        jnp.concatenate(outer_forward(columns, outer_ref, twiddle_ref), axis=0), inner_ref
    )
    taps = taps_ref[own_rows, :]
    tap_count = taps.shape[1]
    square = (tap_count, tap_count)
    upper = lax.broadcasted_iota(jnp.int32, square, 1) >= lax.broadcasted_iota(
        jnp.int32, square, 0
    )
    for c in range(own):
        lags = pltpu.roll(
            jnp.broadcast_to(taps[c : c + 1], square), 0, 1, stride=1, stride_axis=0
        )
        high, low = split_two(
            jnp.concatenate([jnp.where(upper, 0.0, lags), jnp.where(upper, lags, 0.0)], axis=0)
        )
        toeplitz_ref[c] = jnp.concatenate([high, low], axis=1)


def mix_kernel(
    own,
    parts_ref,
    spectrum_ref,
    toeplitz_ref,
    skip_ref,
    outer_ref,
    twiddle_ref,
    inner_ref,
    inner_back_ref,
    outer_back_ref,
    out_ref,
    signal_ref,
    in_gate_ref,
    mixed_ref,
):
    seq_devs, _, _, local_len = parts_ref.shape
    local_blocks = local_len // LANES
    part_rows = local_blocks * own
    blocks = seq_devs * local_blocks
    signal_ref[:own, :] = jnp.zeros((own, LANES), F32)
    order = exchange_order(seq_devs)
    for place, p in enumerate(order):
        for q in range(local_blocks):
            at = p * part_rows + q * own
            lanes = slice(q * LANES, (q + 1) * LANES)
            signal_ref[own + at : 2 * own + at, :] = parts_ref[place, 0, :, lanes].astype(F32)
            in_gate_ref[at : at + own, :] = parts_ref[place, 1, :, lanes].astype(F32)
    gated = []
    for c in range(own):
        window = jnp.concatenate(
            [
                signal_ref[pl.ds(c, blocks, stride=own), :],
                signal_ref[pl.ds(own + c, blocks, stride=own), :],
            ],
            axis=1,
        ).astype(BF16)
        both = matmul(window, toeplitz_ref[c])
        gated.append(
            in_gate_ref[pl.ds(c, blocks, stride=own), :] * (both[:, :LANES] + both[:, LANES:])
        )
    mid = outer_forward(gated, outer_ref, twiddle_ref)
    step = max(1, own // GROUPS)
    backs = []
    for start in range(0, own, step):
        rows = slice(start * blocks, (start + step) * blocks)
        vals = inner_product(jnp.concatenate(mid[start : start + step], axis=0), inner_ref)
        real, imag = vals[:, :LANES], vals[:, LANES:]
        filt_real, filt_imag = spectrum_ref[rows, :LANES], spectrum_ref[rows, LANES:]
        product = jnp.concatenate(
            [real * filt_real - imag * filt_imag, real * filt_imag + imag * filt_real], axis=1
        )
        backs.append(inner_product(product, inner_back_ref))
    conv = outer_backward(jnp.concatenate(backs, axis=0), own, twiddle_ref, outer_back_ref)
    for c in range(own):
        mixed_ref[pl.ds(c, blocks, stride=own), :] = (
            conv[:, c * LANES : (c + 1) * LANES] + skip_ref[c : c + 1, :] * gated[c]
        )
    for q in range(local_blocks):
        if own % 8 == 0:
            column = jnp.concatenate(
                [
                    mixed_ref[p * part_rows + q * own : p * part_rows + (q + 1) * own, :]
                    for p in order
                ],
                axis=0,
            )
        else:
            for place, p in enumerate(order):
                at = p * part_rows + q * own
                signal_ref[place * own : (place + 1) * own, :] = mixed_ref[at : at + own, :]
            column = signal_ref[: seq_devs * own, :]
        out_ref[:, q * LANES : (q + 1) * LANES] = column


def make_filter(params, own, full_len):
    blocks = full_len // LANES
    hidden, channels = params[5].shape
    tap_count = params[8].shape[1]
    embed = embed_table(full_len)
    tables = transform_tables(full_len)
    operands = (embed,) + params + tables
    padded = round_up(params[0].shape[0] + 1, 8)
    return pl.pallas_call(
        functools.partial(filter_kernel, own),
        out_shape=(
            pltpu.VMEM((own * blocks, 2 * LANES), F32),
            pltpu.VMEM((own, 2 * tap_count, 2 * tap_count), BF16),
            pltpu.VMEM((own, LANES), F32),
        )
        + tuple(pltpu.VMEM(table.shape, table.dtype) for table in tables),
        in_specs=[pl.BlockSpec(memory_space=pltpu.HBM)] * len(operands),
        out_specs=(pl.BlockSpec(memory_space=pltpu.VMEM),) * (3 + len(tables)),
        scratch_shapes=[pltpu.VMEM(embed.shape, BF16)]
        + [pltpu.VMEM(vals.shape, F32) for vals in params]
        + [
            pltpu.VMEM((padded, hidden), F32),
            pltpu.VMEM((8, hidden), F32),
            pltpu.VMEM((8, channels), F32),
            pltpu.VMEM((channels, 8), F32),
            pltpu.VMEM((2, channels, 2 * hidden), F32),
            pltpu.VMEM(((blocks + 1) * own, LANES), F32),
            pltpu.SemaphoreType.DMA((len(operands) - 1,)),
            pltpu.SemaphoreType.DMA((TILES,)),
        ],
        compiler_params=pltpu.CompilerParams(vmem_limit_bytes=48 * 2**20),
    )(*[in_space(jnp.asarray(vals), pltpu.HBM) for vals in operands])


def mix(parts, shared):
    seq_devs, _, own, local_len = parts.shape
    rows = seq_devs * own * (local_len // LANES)
    vmem = pl.BlockSpec(memory_space=pltpu.VMEM)
    return pl.pallas_call(
        functools.partial(mix_kernel, own),
        out_shape=jax.ShapeDtypeStruct((seq_devs * own, local_len), F32),
        in_specs=[vmem] * (1 + len(shared)),
        out_specs=vmem,
        scratch_shapes=[pltpu.VMEM((rows + 2 * own, LANES), F32)]
        + [pltpu.VMEM((rows + own, LANES), F32)] * 2,
        compiler_params=pltpu.CompilerParams(vmem_limit_bytes=48 * 2**20),
    )(parts, *[in_space(vals, pltpu.VMEM) for vals in shared])


def on_device(
    signal,
    in_gate,
    out_gate,
    short_taps,
    skip_gain,
    decay_rate,
    embed_weight,
    embed_bias,
    sine_freq,
    mid_weight,
    mid_bias,
    out_weight,
):
    channels, local_len = signal.shape
    seq_devs = lax.axis_size("seq")
    own = -(-channels // seq_devs)
    spare = own * seq_devs - channels
    parts = [signal, in_gate]
    if spare:
        parts = [jnp.pad(part, ((0, spare), (0, 0))) for part in parts]
        short_taps = jnp.pad(short_taps, ((0, spare), (0, 0)))
        skip_gain = jnp.pad(skip_gain, (0, spare))
        decay_rate = jnp.pad(decay_rate, (0, spare), mode="edge")
        out_weight = jnp.pad(out_weight, ((0, 0), (0, spare)))
    parts = jnp.stack([part.reshape(seq_devs, own, local_len) for part in parts], axis=1)
    order = exchange_order(seq_devs)
    parts = exchange(parts, order)
    params = (
        embed_weight,
        embed_bias[None, :],
        sine_freq[None, :],
        mid_weight,
        mid_bias[None, :],
        out_weight,
        decay_rate[None, :],
        skip_gain[None, :],
        short_taps,
    )
    shared = make_filter(params, own, seq_devs * local_len)
    mixed = mix(parts, shared)
    vals = exchange(mixed.reshape(seq_devs, own, local_len), order)
    vals = vals.reshape(seq_devs * own, local_len)[:channels]
    return (out_gate.astype(F32) * vals).astype(BF16)


def solution(mesh):
    in_specs = (
        P("ch", "seq"),
        P("ch", "seq"),
        P("ch", "seq"),
        P("ch", None),
        P("ch"),
        P("ch"),
        P(),
        P(),
        P(),
        P(),
        P(),
        P(None, "ch"),
    )
    out_specs = P("ch", "seq")
    return jax.shard_map(
        on_device, mesh=mesh, in_specs=in_specs, out_specs=out_specs, check_vma=False
    )
```

```python
import functools
import math

import jax
import jax.numpy as jnp
import numpy as np
from jax import lax
from jax.experimental import pallas as pl
from jax.experimental.pallas import tpu as pltpu
from jax.sharding import PartitionSpec as P

BANDS = 16
LANES = 128
GROUPS = 4
TILES = 2
SPAN = 120.0
F32 = jnp.float32
BF16 = jnp.bfloat16
in_space = pltpu.with_memory_space_constraint


def round_up(count, step):
    return (count + step - 1) // step * step


def halves(table):
    high = table.astype(BF16)
    low = (table - high.astype(np.float64)).astype(BF16)
    return high, low


@functools.lru_cache(maxsize=None)
def embed_table(full_len):
    positions = np.arange(full_len, dtype=np.int64)
    rows = [positions / full_len]
    phase = positions
    for _ in range(BANDS):
        angle = phase * (2.0 * math.pi / full_len)
        rows += [np.cos(angle), np.sin(angle)]
        phase = 2 * phase % full_len
    rows.append(np.ones(full_len))
    table = np.zeros((round_up(len(rows), 8), full_len))
    table[: len(rows)] = np.stack(rows)
    first, rest = halves(table)
    second, third = halves(table - first.astype(np.float64))
    stacked = np.concatenate([first, second, third], axis=0)
    return np.pad(stacked, ((0, -len(stacked) % 16), (0, 0)))


@functools.lru_cache(maxsize=None)
def transform_tables(full_len):
    blocks = full_len // LANES
    a = np.arange(blocks)
    k1 = np.arange(blocks)
    b = np.arange(LANES)
    theta = 2.0 * math.pi / blocks * ((4 * k1 + 1)[:, None] * a[None, :] % (4 * blocks)) / 4.0
    phi = 2.0 * math.pi / full_len * ((4 * k1 + 1)[:, None] * b[None, :]) / 4.0
    psi = 2.0 * math.pi / LANES * (b[:, None] * b[None, :] % LANES)
    outer_high, outer_low = halves(np.concatenate([np.cos(theta), -np.sin(theta)], axis=0))
    outer = np.concatenate([outer_high, outer_high, outer_low], axis=1)
    back = np.concatenate([np.cos(theta).T, -np.sin(theta).T], axis=1) / full_len
    back_high, back_low = halves(back)
    outer_back = np.concatenate([back_high, back_high, back_low], axis=1)
    twiddle = np.stack([np.cos(phi), np.sin(phi)]).astype(np.float32)
    cos_in, sin_in = np.cos(psi), np.sin(psi)
    inner = np.stack(halves(np.block([[cos_in, -sin_in], [sin_in, cos_in]])))
    inner_back = np.stack(halves(np.block([[cos_in, sin_in], [-sin_in, cos_in]])))
    return outer, twiddle, inner, inner_back, outer_back


def sine_fit(terms):
    nodes = np.cos((np.arange(400) + 0.5) * math.pi / 400) * 0.5
    basis = np.stack([nodes ** (2 * p + 1) for p in range(terms)], axis=1)
    fit = np.linalg.lstsq(basis, np.sin(2.0 * math.pi * nodes), rcond=None)[0]
    return [float(v) for v in fit]


SINE_FIT = sine_fit(6)


def sine_of_turns(turns):
    part = turns - jnp.round(turns)
    square = part * part
    value = SINE_FIT[-1]
    for term in SINE_FIT[-2::-1]:
        value = value * square + term
    return value * part


def split_two(vals):
    high = vals.astype(BF16)
    return high, (vals - high.astype(F32)).astype(BF16)


def split_three(vals):
    first = vals.astype(BF16).astype(F32)
    rest = vals - first
    second = rest.astype(BF16).astype(F32)
    return first, second, rest - second


def matmul(lhs, rhs):
    return jnp.dot(lhs, rhs, preferred_element_type=F32)


def stack_three(vals):
    high, low = split_two(vals)
    return jnp.concatenate([high, low, high], axis=0)


def inner_product(vals, table_ref):
    high, low = split_two(vals)
    return (
        matmul(high, table_ref[0]) + matmul(low, table_ref[0]) + matmul(high, table_ref[1])
    )


def outer_forward(columns, outer_ref, twiddle_ref):
    blocks = columns[0].shape[0]
    mixed = matmul(outer_ref[...], stack_three(jnp.concatenate(columns, axis=1)))
    cos_vals, sin_vals = twiddle_ref[0], twiddle_ref[1]
    rows = []
    for c in range(len(columns)):
        real = mixed[:blocks, c * LANES : (c + 1) * LANES]
        imag = mixed[blocks:, c * LANES : (c + 1) * LANES]
        rows.append(
            jnp.concatenate(
                [real * cos_vals + imag * sin_vals, imag * cos_vals - real * sin_vals], axis=1
            )
        )
    return rows


def outer_backward(vals, channels, twiddle_ref, outer_back_ref):
    blocks = vals.shape[0] // channels
    cos_vals, sin_vals = twiddle_ref[0], twiddle_ref[1]
    columns = []
    for c in range(channels):
        real = vals[c * blocks : (c + 1) * blocks, :LANES]
        imag = vals[c * blocks : (c + 1) * blocks, LANES:]
        columns.append(
            jnp.concatenate(
                [real * cos_vals - imag * sin_vals, imag * cos_vals + real * sin_vals], axis=0
            )
        )
    return matmul(outer_back_ref[...], stack_three(jnp.concatenate(columns, axis=1)))


def code_group(columns):
    top = functools.reduce(jnp.maximum, [jnp.abs(column) for column in columns])
    scale = lax.reduce_precision(jnp.maximum(top, 1e-30) * (1.0 + 1.0 / 128), 8, 7)
    factor = 2.0 * SPAN / scale
    codes = []
    for column in columns:
        size = jnp.exp2(jnp.abs(column) * factor - SPAN)
        codes.append(jnp.where(column < 0, -size, size).astype(BF16))
    return codes, scale.astype(BF16)


def decode_group(codes, scale):
    codes = codes.astype(F32)
    share = jnp.log(jnp.abs(codes)) * (0.5 / SPAN / math.log(2.0)) + 0.5
    return jnp.where(codes < 0, -share, share) * scale.astype(F32)


def exchange_order(count):
    first = count // 2 + count // 8
    return [(first + place) % count for place in range(count)]


def exchange(chunks, order):
    return lax.all_to_all(
        chunks, "seq", split_axis=0, concat_axis=0, tiled=True, axis_index_groups=[order]
    )


def filter_kernel(
    own,
    embed_hbm,
    embed_weight_hbm,
    embed_bias_hbm,
    sine_freq_hbm,
    mid_weight_hbm,
    mid_bias_hbm,
    out_weight_hbm,
    decay_hbm,
    skip_hbm,
    taps_hbm,
    outer_hbm,
    twiddle_hbm,
    inner_hbm,
    inner_back_hbm,
    outer_back_hbm,
    spectrum_ref,
    toeplitz_ref,
    skip_ref,
    outer_ref,
    twiddle_ref,
    inner_ref,
    inner_back_ref,
    outer_back_ref,
    embed_ref,
    embed_weight_ref,
    embed_bias_ref,
    sine_freq_ref,
    mid_weight_ref,
    mid_bias_ref,
    out_weight_ref,
    decay_ref,
    skip_row_ref,
    taps_ref,
    pad_ref,
    vec_ref,
    row_ref,
    column_ref,
    out_rows_ref,
    filter_ref,
    sems,
    embed_sems,
):
    full_len = embed_ref.shape[1]
    tile_len = full_len // TILES
    hidden = mid_weight_ref.shape[0]
    pairs = [
        (embed_weight_hbm, embed_weight_ref),
        (embed_bias_hbm, embed_bias_ref),
        (sine_freq_hbm, sine_freq_ref),
        (mid_weight_hbm, mid_weight_ref),
        (mid_bias_hbm, mid_bias_ref),
        (out_weight_hbm, out_weight_ref),
        (decay_hbm, decay_ref),
        (skip_hbm, skip_row_ref),
        (taps_hbm, taps_ref),
        (outer_hbm, outer_ref),
        (twiddle_hbm, twiddle_ref),
        (inner_hbm, inner_ref),
        (inner_back_hbm, inner_back_ref),
        (outer_back_hbm, outer_back_ref),
    ]
    copies = [pltpu.make_async_copy(*pair, sems.at[i]) for i, pair in enumerate(pairs)]
    embed_copies = []
    for i in range(TILES):
        lanes = pl.ds(i * tile_len, tile_len)
        embed_copies.append(
            pltpu.make_async_copy(
                embed_hbm.at[:, lanes], embed_ref.at[:, lanes], embed_sems.at[i]
            )
        )
    for copy in copies[:9] + embed_copies + copies[9:]:
        copy.start()
    seq_index = lax.axis_index("seq")
    first_channel = 0
    for place, device in enumerate(exchange_order(lax.axis_size("seq"))):
        first_channel = jnp.where(seq_index == device, place * own, first_channel)
    first_channel = pl.multiple_of(first_channel, own)
    pad_ref[...] = jnp.zeros_like(pad_ref)
    vec_ref[...] = jnp.zeros_like(vec_ref)
    row_ref[...] = jnp.zeros_like(row_ref)
    for copy in copies[:9]:
        copy.wait()

    freq = sine_freq_ref[...] * (0.5 / math.pi)
    features = embed_weight_ref.shape[0]
    pad_ref[:features, :] = embed_weight_ref[...] * freq
    pad_ref[features : features + 1, :] = embed_bias_ref[...] * freq
    one, two, three = split_three(pad_ref[...])
    none = jnp.zeros_like(one)
    rest = jnp.zeros((embed_ref.shape[0] - 3 * one.shape[0], hidden), F32)
    weight_one = jnp.concatenate(
        [
            jnp.concatenate([one, one, one, rest], axis=0).T,
            jnp.concatenate([two, two, none, rest], axis=0).T,
            jnp.concatenate([three, none, none, rest], axis=0).T,
        ],
        axis=0,
    ).astype(BF16)
    one, two, _ = split_three(mid_weight_ref[...] * freq)
    weight_two = jnp.concatenate([one, one, two], axis=0).T.astype(BF16)
    vec_ref[0:1, :] = mid_bias_ref[...] * freq
    bias_two = vec_ref[...].T[:, 0:1]
    one, two, _ = split_three(out_weight_ref[...])
    out_rows_ref[0] = jnp.concatenate([one, one], axis=0).T
    out_rows_ref[1] = jnp.concatenate([two, two], axis=0).T
    own_rows = pl.ds(first_channel, own)
    weight_three = jnp.concatenate(
        [out_rows_ref[0, own_rows, :], out_rows_ref[1, own_rows, :]], axis=0
    ).astype(BF16)
    row_ref[0:1, :] = decay_ref[...]
    row_ref[1:2, :] = skip_row_ref[...]
    column_ref[...] = row_ref[...].T
    decay = column_ref[own_rows, 0:1]
    skip_ref[...] = jnp.broadcast_to(column_ref[own_rows, 1:2], skip_ref.shape)
    scale = jnp.sqrt(2.0 * decay)

    taps = taps_ref[own_rows, :]
    tap_count = taps.shape[1]
    square = (tap_count, tap_count)
    upper = lax.broadcasted_iota(jnp.int32, square, 1) >= lax.broadcasted_iota(
        jnp.int32, square, 0
    )
    for c in range(own):
        lags = pltpu.roll(
            jnp.broadcast_to(taps[c : c + 1], square), 0, 1, stride=1, stride_axis=0
        )
        high, low = split_two(
            jnp.concatenate([jnp.where(upper, 0.0, lags), jnp.where(upper, lags, 0.0)], axis=0)
        )
        toeplitz_ref[c] = jnp.concatenate([high, low], axis=1)

    for i in range(TILES):
        start = i * tile_len
        embed_copies[i].wait()
        turns = matmul(weight_one, embed_ref[:, start : start + tile_len])
        first = sine_of_turns(
            turns[:hidden] + turns[hidden : 2 * hidden] + turns[2 * hidden :]
        )
        second = sine_of_turns(matmul(weight_two, stack_three(first)) + bias_two)
        raw = matmul(weight_three, jnp.concatenate(split_two(second), axis=0))
        positions = (start + lax.broadcasted_iota(jnp.int32, (own, tile_len), 1)).astype(F32)
        vals = (raw[:own] + raw[own:]) * (scale * jnp.exp(-decay * positions))
        for j in range(tile_len // LANES):
            row = (start // LANES + j) * own
            filter_ref[row : row + own, :] = vals[:, j * LANES : (j + 1) * LANES]

    for copy in copies[9:]:
        copy.wait()
    blocks = full_len // LANES
    columns = [filter_ref[pl.ds(c, blocks, stride=own), :] for c in range(own)]
    spectrum_ref[...] = inner_product(
        jnp.concatenate(outer_forward(columns, outer_ref, twiddle_ref), axis=0), inner_ref
    )


def mix_kernel(
    own,
    parts_ref,
    spectrum_ref,
    toeplitz_ref,
    skip_ref,
    outer_ref,
    twiddle_ref,
    inner_ref,
    inner_back_ref,
    outer_back_ref,
    out_ref,
    signal_ref,
    in_gate_ref,
    mixed_ref,
):
    seq_devs, _, _, local_len = parts_ref.shape
    local_blocks = local_len // LANES
    part_rows = local_blocks * own
    blocks = seq_devs * local_blocks
    signal_ref[:own, :] = jnp.zeros((own, LANES), F32)
    order = exchange_order(seq_devs)
    for place, p in enumerate(order):
        for q in range(local_blocks):
            at = p * part_rows + q * own
            lanes = slice(q * LANES, (q + 1) * LANES)
            signal_ref[own + at : 2 * own + at, :] = parts_ref[place, 0, :, lanes].astype(F32)
            in_gate_ref[at : at + own, :] = parts_ref[place, 1, :, lanes].astype(F32)
    gated = []
    for c in range(own):
        window = jnp.concatenate(
            [
                signal_ref[pl.ds(c, blocks, stride=own), :],
                signal_ref[pl.ds(own + c, blocks, stride=own), :],
            ],
            axis=1,
        ).astype(BF16)
        both = matmul(window, toeplitz_ref[c])
        gated.append(
            in_gate_ref[pl.ds(c, blocks, stride=own), :] * (both[:, :LANES] + both[:, LANES:])
        )
    mid = outer_forward(gated, outer_ref, twiddle_ref)
    step = max(1, own // GROUPS)
    backs = []
    for start in range(0, own, step):
        rows = slice(start * blocks, (start + step) * blocks)
        vals = inner_product(jnp.concatenate(mid[start : start + step], axis=0), inner_ref)
        real, imag = vals[:, :LANES], vals[:, LANES:]
        filt_real, filt_imag = spectrum_ref[rows, :LANES], spectrum_ref[rows, LANES:]
        product = jnp.concatenate(
            [real * filt_real - imag * filt_imag, real * filt_imag + imag * filt_real], axis=1
        )
        backs.append(inner_product(product, inner_back_ref))
    conv = outer_backward(jnp.concatenate(backs, axis=0), own, twiddle_ref, outer_back_ref)
    for c in range(own):
        mixed_ref[pl.ds(c, blocks, stride=own), :] = (
            conv[:, c * LANES : (c + 1) * LANES] + skip_ref[c : c + 1, :] * gated[c]
        )
    columns = []
    for q in range(local_blocks):
        if own % 8 == 0:
            column = jnp.concatenate(
                [
                    mixed_ref[p * part_rows + q * own : p * part_rows + (q + 1) * own, :]
                    for p in order
                ],
                axis=0,
            )
        else:
            for place, p in enumerate(order):
                at = p * part_rows + q * own
                signal_ref[place * own : (place + 1) * own, :] = mixed_ref[at : at + own, :]
            column = signal_ref[: seq_devs * own, :]
        columns.append(column)
    codes, scale = code_group(columns)
    for q in range(local_blocks):
        out_ref[:, q * LANES : (q + 1) * LANES] = codes[q]
    out_ref[:, local_len:] = scale


def make_filter(params, own, full_len):
    blocks = full_len // LANES
    hidden, channels = params[5].shape
    tap_count = params[8].shape[1]
    embed = embed_table(full_len)
    tables = transform_tables(full_len)
    operands = (embed,) + params + tables
    padded = round_up(params[0].shape[0] + 1, 8)
    return pl.pallas_call(
        functools.partial(filter_kernel, own),
        out_shape=(
            pltpu.VMEM((own * blocks, 2 * LANES), F32),
            pltpu.VMEM((own, 2 * tap_count, 2 * tap_count), BF16),
            pltpu.VMEM((own, LANES), F32),
        )
        + tuple(pltpu.VMEM(table.shape, table.dtype) for table in tables),
        in_specs=[pl.BlockSpec(memory_space=pltpu.HBM)] * len(operands),
        out_specs=(pl.BlockSpec(memory_space=pltpu.VMEM),) * (3 + len(tables)),
        scratch_shapes=[pltpu.VMEM(embed.shape, BF16)]
        + [pltpu.VMEM(vals.shape, F32) for vals in params]
        + [
            pltpu.VMEM((padded, hidden), F32),
            pltpu.VMEM((8, hidden), F32),
            pltpu.VMEM((8, channels), F32),
            pltpu.VMEM((channels, 8), F32),
            pltpu.VMEM((2, channels, 2 * hidden), F32),
            pltpu.VMEM(((blocks + 1) * own, LANES), F32),
            pltpu.SemaphoreType.DMA((len(operands) - 1,)),
            pltpu.SemaphoreType.DMA((TILES,)),
        ],
        compiler_params=pltpu.CompilerParams(vmem_limit_bytes=48 * 2**20),
    )(*[in_space(jnp.asarray(vals), pltpu.HBM) for vals in operands])


def mix(parts, shared):
    seq_devs, _, own, local_len = parts.shape
    rows = seq_devs * own * (local_len // LANES)
    vmem = pl.BlockSpec(memory_space=pltpu.VMEM)
    return pl.pallas_call(
        functools.partial(mix_kernel, own),
        out_shape=jax.ShapeDtypeStruct((seq_devs * own, local_len + LANES), BF16),
        in_specs=[vmem] * (1 + len(shared)),
        out_specs=vmem,
        scratch_shapes=[pltpu.VMEM((rows + 2 * own, LANES), F32)]
        + [pltpu.VMEM((rows + own, LANES), F32)] * 2,
        compiler_params=pltpu.CompilerParams(vmem_limit_bytes=48 * 2**20),
    )(parts, *[in_space(vals, pltpu.VMEM) for vals in shared])


def on_device(
    signal,
    in_gate,
    out_gate,
    short_taps,
    skip_gain,
    decay_rate,
    embed_weight,
    embed_bias,
    sine_freq,
    mid_weight,
    mid_bias,
    out_weight,
):
    channels, local_len = signal.shape
    seq_devs = lax.axis_size("seq")
    own = -(-channels // seq_devs)
    spare = own * seq_devs - channels
    parts = [signal, in_gate]
    if spare:
        parts = [jnp.pad(part, ((0, spare), (0, 0))) for part in parts]
        short_taps = jnp.pad(short_taps, ((0, spare), (0, 0)))
        skip_gain = jnp.pad(skip_gain, (0, spare))
        decay_rate = jnp.pad(decay_rate, (0, spare), mode="edge")
        out_weight = jnp.pad(out_weight, ((0, 0), (0, spare)))
    parts = jnp.stack([part.reshape(seq_devs, own, local_len) for part in parts], axis=1)
    order = exchange_order(seq_devs)
    parts = exchange(parts, order)
    params = (
        embed_weight,
        embed_bias[None, :],
        sine_freq[None, :],
        mid_weight,
        mid_bias[None, :],
        out_weight,
        decay_rate[None, :],
        skip_gain[None, :],
        short_taps,
    )
    shared = make_filter(params, own, seq_devs * local_len)
    mixed = mix(parts, shared)
    coded = exchange(mixed.reshape(seq_devs, own, -1), order).reshape(
        seq_devs * own, -1
    )[:channels]
    scale = jnp.concatenate([coded[:, local_len:]] * (local_len // LANES), axis=1)
    vals = decode_group(coded[:, :local_len], scale)
    return (out_gate.astype(F32) * vals).astype(BF16)


def solution(mesh):
    in_specs = (
        P("ch", "seq"),
        P("ch", "seq"),
        P("ch", "seq"),
        P("ch", None),
        P("ch"),
        P("ch"),
        P(),
        P(),
        P(),
        P(),
        P(),
        P(None, "ch"),
    )
    out_specs = P("ch", "seq")
    return jax.shard_map(
        on_device, mesh=mesh, in_specs=in_specs, out_specs=out_specs, check_vma=False
    )
```

```python
import functools
import math

import jax
import jax.numpy as jnp
import numpy as np
from jax import lax
from jax.experimental import pallas as pl
from jax.experimental.pallas import tpu as pltpu
from jax.sharding import PartitionSpec as P

BANDS = 16
LANES = 128
GROUPS = 4
TILES = 2
SPAN = 120.0
F32 = jnp.float32
BF16 = jnp.bfloat16
in_space = pltpu.with_memory_space_constraint


def round_up(count, step):
    return (count + step - 1) // step * step


def halves(table):
    high = table.astype(BF16)
    low = (table - high.astype(np.float64)).astype(BF16)
    return high, low


@functools.lru_cache(maxsize=None)
def embed_table(full_len):
    positions = np.arange(full_len, dtype=np.int64)
    rows = [positions / full_len]
    phase = positions
    for _ in range(BANDS):
        angle = phase * (2.0 * math.pi / full_len)
        rows += [np.cos(angle), np.sin(angle)]
        phase = 2 * phase % full_len
    rows.append(np.ones(full_len))
    table = np.zeros((round_up(len(rows), 8), full_len))
    table[: len(rows)] = np.stack(rows)
    first, rest = halves(table)
    second, third = halves(table - first.astype(np.float64))
    stacked = np.concatenate([first, second, third], axis=0)
    return np.pad(stacked, ((0, -len(stacked) % 16), (0, 0)))


@functools.lru_cache(maxsize=None)
def transform_tables(full_len):
    blocks = full_len // LANES
    a = np.arange(blocks)
    k1 = np.arange(blocks)
    b = np.arange(LANES)
    theta = 2.0 * math.pi / blocks * ((4 * k1 + 1)[:, None] * a[None, :] % (4 * blocks)) / 4.0
    phi = 2.0 * math.pi / full_len * ((4 * k1 + 1)[:, None] * b[None, :]) / 4.0
    psi = 2.0 * math.pi / LANES * (b[:, None] * b[None, :] % LANES)
    outer_high, outer_low = halves(np.concatenate([np.cos(theta), -np.sin(theta)], axis=0))
    outer = np.concatenate([outer_high, outer_high, outer_low], axis=1)
    back = np.concatenate([np.cos(theta).T, -np.sin(theta).T], axis=1) / full_len
    back_high, back_low = halves(back)
    outer_back = np.concatenate([back_high, back_high, back_low], axis=1)
    twiddle = np.stack([np.cos(phi), np.sin(phi)]).astype(np.float32)
    cos_in, sin_in = np.cos(psi), np.sin(psi)
    inner = np.stack(halves(np.block([[cos_in, -sin_in], [sin_in, cos_in]])))
    inner_back = np.stack(halves(np.block([[cos_in, sin_in], [-sin_in, cos_in]])))
    return outer, twiddle, inner, inner_back, outer_back


def sine_fit(terms):
    nodes = np.cos((np.arange(400) + 0.5) * math.pi / 400) * 0.5
    basis = np.stack([nodes ** (2 * p + 1) for p in range(terms)], axis=1)
    fit = np.linalg.lstsq(basis, np.sin(2.0 * math.pi * nodes), rcond=None)[0]
    return [float(v) for v in fit]


SINE_FIT = sine_fit(6)


def sine_of_turns(turns):
    part = turns - jnp.round(turns)
    square = part * part
    value = SINE_FIT[-1]
    for term in SINE_FIT[-2::-1]:
        value = value * square + term
    return value * part


def split_two(vals):
    high = vals.astype(BF16)
    return high, (vals - high.astype(F32)).astype(BF16)


def split_three(vals):
    first = vals.astype(BF16).astype(F32)
    rest = vals - first
    second = rest.astype(BF16).astype(F32)
    return first, second, rest - second


def matmul(lhs, rhs):
    return jnp.dot(lhs, rhs, preferred_element_type=F32)


def stack_three(vals):
    high, low = split_two(vals)
    return jnp.concatenate([high, low, high], axis=0)


def inner_product(vals, table_ref):
    high, low = split_two(vals)
    return (
        matmul(high, table_ref[0]) + matmul(low, table_ref[0]) + matmul(high, table_ref[1])
    )


def outer_forward(columns, outer_ref, twiddle_ref):
    blocks = columns[0].shape[0]
    mixed = matmul(outer_ref[...], stack_three(jnp.concatenate(columns, axis=1)))
    cos_vals, sin_vals = twiddle_ref[0], twiddle_ref[1]
    rows = []
    for c in range(len(columns)):
        real = mixed[:blocks, c * LANES : (c + 1) * LANES]
        imag = mixed[blocks:, c * LANES : (c + 1) * LANES]
        rows.append(
            jnp.concatenate(
                [real * cos_vals + imag * sin_vals, imag * cos_vals - real * sin_vals], axis=1
            )
        )
    return rows


def outer_backward(vals, channels, twiddle_ref, outer_back_ref):
    blocks = vals.shape[0] // channels
    cos_vals, sin_vals = twiddle_ref[0], twiddle_ref[1]
    columns = []
    for c in range(channels):
        real = vals[c * blocks : (c + 1) * blocks, :LANES]
        imag = vals[c * blocks : (c + 1) * blocks, LANES:]
        columns.append(
            jnp.concatenate(
                [real * cos_vals - imag * sin_vals, imag * cos_vals + real * sin_vals], axis=0
            )
        )
    return matmul(outer_back_ref[...], stack_three(jnp.concatenate(columns, axis=1)))


def code_group(columns):
    top = functools.reduce(jnp.maximum, [jnp.abs(column) for column in columns])
    scale = lax.reduce_precision(jnp.maximum(top, 1e-30) * (1.0 + 1.0 / 128), 8, 7)
    factor = 2.0 * SPAN / scale
    codes = []
    for column in columns:
        size = jnp.exp2(jnp.abs(column) * factor - SPAN)
        codes.append(jnp.where(column < 0, -size, size).astype(BF16))
    return codes, scale.astype(BF16)


def decode_group(codes, scale):
    codes = codes.astype(F32)
    share = jnp.log(jnp.abs(codes)) * (0.5 / SPAN / math.log(2.0)) + 0.5
    return jnp.where(codes < 0, -share, share) * scale.astype(F32)


def exchange_order(count):
    first = count // 2 + count // 8
    mixed = np.random.RandomState(147).permutation(count)
    return [first] + [int(place) for place in mixed if place != first]


def exchange(chunks, order):
    return lax.all_to_all(
        chunks, "seq", split_axis=0, concat_axis=0, tiled=True, axis_index_groups=[order]
    )


def filter_kernel(
    own,
    embed_hbm,
    embed_weight_hbm,
    embed_bias_hbm,
    sine_freq_hbm,
    mid_weight_hbm,
    mid_bias_hbm,
    out_weight_hbm,
    decay_hbm,
    skip_hbm,
    taps_hbm,
    outer_hbm,
    twiddle_hbm,
    inner_hbm,
    inner_back_hbm,
    outer_back_hbm,
    spectrum_ref,
    toeplitz_ref,
    skip_ref,
    outer_ref,
    twiddle_ref,
    inner_ref,
    inner_back_ref,
    outer_back_ref,
    embed_ref,
    embed_weight_ref,
    embed_bias_ref,
    sine_freq_ref,
    mid_weight_ref,
    mid_bias_ref,
    out_weight_ref,
    decay_ref,
    skip_row_ref,
    taps_ref,
    pad_ref,
    vec_ref,
    row_ref,
    column_ref,
    out_rows_ref,
    filter_ref,
    sems,
    embed_sems,
):
    full_len = embed_ref.shape[1]
    tile_len = full_len // TILES
    hidden = mid_weight_ref.shape[0]
    pairs = [
        (embed_weight_hbm, embed_weight_ref),
        (embed_bias_hbm, embed_bias_ref),
        (sine_freq_hbm, sine_freq_ref),
        (mid_weight_hbm, mid_weight_ref),
        (mid_bias_hbm, mid_bias_ref),
        (out_weight_hbm, out_weight_ref),
        (decay_hbm, decay_ref),
        (skip_hbm, skip_row_ref),
        (taps_hbm, taps_ref),
        (outer_hbm, outer_ref),
        (twiddle_hbm, twiddle_ref),
        (inner_hbm, inner_ref),
        (inner_back_hbm, inner_back_ref),
        (outer_back_hbm, outer_back_ref),
    ]
    copies = [pltpu.make_async_copy(*pair, sems.at[i]) for i, pair in enumerate(pairs)]
    embed_copies = []
    for i in range(TILES):
        lanes = pl.ds(i * tile_len, tile_len)
        embed_copies.append(
            pltpu.make_async_copy(
                embed_hbm.at[:, lanes], embed_ref.at[:, lanes], embed_sems.at[i]
            )
        )
    for copy in copies[:8] + embed_copies + copies[8:]:
        copy.start()
    seq_index = lax.axis_index("seq")
    first_channel = 0
    for place, device in enumerate(exchange_order(lax.axis_size("seq"))):
        first_channel = jnp.where(seq_index == device, place * own, first_channel)
    first_channel = pl.multiple_of(first_channel, own)
    pad_ref[...] = jnp.zeros_like(pad_ref)
    vec_ref[...] = jnp.zeros_like(vec_ref)
    row_ref[...] = jnp.zeros_like(row_ref)
    for copy in copies[:8]:
        copy.wait()

    freq = sine_freq_ref[...] * (0.5 / math.pi)
    features = embed_weight_ref.shape[0]
    pad_ref[:features, :] = embed_weight_ref[...] * freq
    pad_ref[features : features + 1, :] = embed_bias_ref[...] * freq
    one, two, three = split_three(pad_ref[...])
    none = jnp.zeros_like(one)
    rest = jnp.zeros((embed_ref.shape[0] - 3 * one.shape[0], hidden), F32)
    weight_one = jnp.concatenate(
        [
            jnp.concatenate([one, one, one, rest], axis=0).T,
            jnp.concatenate([two, two, none, rest], axis=0).T,
            jnp.concatenate([three, none, none, rest], axis=0).T,
        ],
        axis=0,
    ).astype(BF16)
    one, two, _ = split_three(mid_weight_ref[...] * freq)
    weight_two = jnp.concatenate([one, one, two], axis=0).T.astype(BF16)
    vec_ref[0:1, :] = mid_bias_ref[...] * freq
    bias_two = vec_ref[...].T[:, 0:1]
    one, two, _ = split_three(out_weight_ref[...])
    out_rows_ref[0] = jnp.concatenate([one, one], axis=0).T
    out_rows_ref[1] = jnp.concatenate([two, two], axis=0).T
    own_rows = pl.ds(first_channel, own)
    weight_three = jnp.concatenate(
        [out_rows_ref[0, own_rows, :], out_rows_ref[1, own_rows, :]], axis=0
    ).astype(BF16)
    row_ref[0:1, :] = decay_ref[...]
    row_ref[1:2, :] = skip_row_ref[...]
    column_ref[...] = row_ref[...].T
    decay = column_ref[own_rows, 0:1]
    skip_ref[...] = jnp.broadcast_to(column_ref[own_rows, 1:2], skip_ref.shape)
    scale = jnp.sqrt(2.0 * decay)

    for i in range(TILES):
        start = i * tile_len
        embed_copies[i].wait()
        turns = matmul(weight_one, embed_ref[:, start : start + tile_len])
        first = sine_of_turns(
            turns[:hidden] + turns[hidden : 2 * hidden] + turns[2 * hidden :]
        )
        second = sine_of_turns(matmul(weight_two, stack_three(first)) + bias_two)
        raw = matmul(weight_three, jnp.concatenate(split_two(second), axis=0))
        positions = (start + lax.broadcasted_iota(jnp.int32, (own, tile_len), 1)).astype(F32)
        vals = (raw[:own] + raw[own:]) * (scale * jnp.exp(-decay * positions))
        for j in range(tile_len // LANES):
            row = (start // LANES + j) * own
            filter_ref[row : row + own, :] = vals[:, j * LANES : (j + 1) * LANES]

    for copy in copies[8:]:
        copy.wait()
    blocks = full_len // LANES
    columns = [filter_ref[pl.ds(c, blocks, stride=own), :] for c in range(own)]
    spectrum_ref[...] = inner_product(
        jnp.concatenate(outer_forward(columns, outer_ref, twiddle_ref), axis=0), inner_ref
    )
    taps = taps_ref[own_rows, :]
    tap_count = taps.shape[1]
    square = (tap_count, tap_count)
    upper = lax.broadcasted_iota(jnp.int32, square, 1) >= lax.broadcasted_iota(
        jnp.int32, square, 0
    )
    for c in range(own):
        lags = pltpu.roll(
            jnp.broadcast_to(taps[c : c + 1], square), 0, 1, stride=1, stride_axis=0
        )
        high, low = split_two(
            jnp.concatenate([jnp.where(upper, 0.0, lags), jnp.where(upper, lags, 0.0)], axis=0)
        )
        toeplitz_ref[c] = jnp.concatenate([high, low], axis=1)


def mix_kernel(
    own,
    parts_ref,
    spectrum_ref,
    toeplitz_ref,
    skip_ref,
    outer_ref,
    twiddle_ref,
    inner_ref,
    inner_back_ref,
    outer_back_ref,
    out_ref,
    signal_ref,
    in_gate_ref,
    mixed_ref,
):
    seq_devs, _, _, local_len = parts_ref.shape
    local_blocks = local_len // LANES
    part_rows = local_blocks * own
    blocks = seq_devs * local_blocks
    signal_ref[:own, :] = jnp.zeros((own, LANES), F32)
    order = exchange_order(seq_devs)
    for place, p in enumerate(order):
        for q in range(local_blocks):
            at = p * part_rows + q * own
            lanes = slice(q * LANES, (q + 1) * LANES)
            signal_ref[own + at : 2 * own + at, :] = parts_ref[place, 0, :, lanes].astype(F32)
            in_gate_ref[at : at + own, :] = parts_ref[place, 1, :, lanes].astype(F32)
    gated = []
    for c in range(own):
        window = jnp.concatenate(
            [
                signal_ref[pl.ds(c, blocks, stride=own), :],
                signal_ref[pl.ds(own + c, blocks, stride=own), :],
            ],
            axis=1,
        ).astype(BF16)
        both = matmul(window, toeplitz_ref[c])
        gated.append(
            in_gate_ref[pl.ds(c, blocks, stride=own), :] * (both[:, :LANES] + both[:, LANES:])
        )
    mid = outer_forward(gated, outer_ref, twiddle_ref)
    step = max(1, own // GROUPS)
    backs = []
    for start in range(0, own, step):
        rows = slice(start * blocks, (start + step) * blocks)
        vals = inner_product(jnp.concatenate(mid[start : start + step], axis=0), inner_ref)
        real, imag = vals[:, :LANES], vals[:, LANES:]
        filt_real, filt_imag = spectrum_ref[rows, :LANES], spectrum_ref[rows, LANES:]
        product = jnp.concatenate(
            [real * filt_real - imag * filt_imag, real * filt_imag + imag * filt_real], axis=1
        )
        backs.append(inner_product(product, inner_back_ref))
    conv = outer_backward(jnp.concatenate(backs, axis=0), own, twiddle_ref, outer_back_ref)
    for c in range(own):
        mixed_ref[pl.ds(c, blocks, stride=own), :] = (
            conv[:, c * LANES : (c + 1) * LANES] + skip_ref[c : c + 1, :] * gated[c]
        )
    columns = []
    for q in range(local_blocks):
        if own % 8 == 0:
            column = jnp.concatenate(
                [
                    mixed_ref[p * part_rows + q * own : p * part_rows + (q + 1) * own, :]
                    for p in order
                ],
                axis=0,
            )
        else:
            for place, p in enumerate(order):
                at = p * part_rows + q * own
                signal_ref[place * own : (place + 1) * own, :] = mixed_ref[at : at + own, :]
            column = signal_ref[: seq_devs * own, :]
        columns.append(column)
    codes, scale = code_group(columns)
    for q in range(local_blocks):
        out_ref[:, q * LANES : (q + 1) * LANES] = codes[q]
    out_ref[:, local_len:] = scale


def make_filter(params, own, full_len):
    blocks = full_len // LANES
    hidden, channels = params[5].shape
    tap_count = params[8].shape[1]
    embed = embed_table(full_len)
    tables = transform_tables(full_len)
    operands = (embed,) + params + tables
    padded = round_up(params[0].shape[0] + 1, 8)
    return pl.pallas_call(
        functools.partial(filter_kernel, own),
        out_shape=(
            pltpu.VMEM((own * blocks, 2 * LANES), F32),
            pltpu.VMEM((own, 2 * tap_count, 2 * tap_count), BF16),
            pltpu.VMEM((own, LANES), F32),
        )
        + tuple(pltpu.VMEM(table.shape, table.dtype) for table in tables),
        in_specs=[pl.BlockSpec(memory_space=pltpu.HBM)] * len(operands),
        out_specs=(pl.BlockSpec(memory_space=pltpu.VMEM),) * (3 + len(tables)),
        scratch_shapes=[pltpu.VMEM(embed.shape, BF16)]
        + [pltpu.VMEM(vals.shape, F32) for vals in params]
        + [
            pltpu.VMEM((padded, hidden), F32),
            pltpu.VMEM((8, hidden), F32),
            pltpu.VMEM((8, channels), F32),
            pltpu.VMEM((channels, 8), F32),
            pltpu.VMEM((2, channels, 2 * hidden), F32),
            pltpu.VMEM(((blocks + 1) * own, LANES), F32),
            pltpu.SemaphoreType.DMA((len(operands) - 1,)),
            pltpu.SemaphoreType.DMA((TILES,)),
        ],
        compiler_params=pltpu.CompilerParams(vmem_limit_bytes=48 * 2**20),
    )(*[in_space(jnp.asarray(vals), pltpu.HBM) for vals in operands])


def mix(parts, shared):
    seq_devs, _, own, local_len = parts.shape
    rows = seq_devs * own * (local_len // LANES)
    vmem = pl.BlockSpec(memory_space=pltpu.VMEM)
    return pl.pallas_call(
        functools.partial(mix_kernel, own),
        out_shape=jax.ShapeDtypeStruct((seq_devs * own, local_len + LANES), BF16),
        in_specs=[vmem] * (1 + len(shared)),
        out_specs=vmem,
        scratch_shapes=[pltpu.VMEM((rows + 2 * own, LANES), F32)]
        + [pltpu.VMEM((rows + own, LANES), F32)] * 2,
        compiler_params=pltpu.CompilerParams(vmem_limit_bytes=48 * 2**20),
    )(parts, *[in_space(vals, pltpu.VMEM) for vals in shared])


def on_device(
    signal,
    in_gate,
    out_gate,
    short_taps,
    skip_gain,
    decay_rate,
    embed_weight,
    embed_bias,
    sine_freq,
    mid_weight,
    mid_bias,
    out_weight,
):
    channels, local_len = signal.shape
    seq_devs = lax.axis_size("seq")
    own = -(-channels // seq_devs)
    spare = own * seq_devs - channels
    parts = [signal, in_gate]
    if spare:
        parts = [jnp.pad(part, ((0, spare), (0, 0))) for part in parts]
        short_taps = jnp.pad(short_taps, ((0, spare), (0, 0)))
        skip_gain = jnp.pad(skip_gain, (0, spare))
        decay_rate = jnp.pad(decay_rate, (0, spare), mode="edge")
        out_weight = jnp.pad(out_weight, ((0, 0), (0, spare)))
    parts = jnp.stack([part.reshape(seq_devs, own, local_len) for part in parts], axis=1)
    order = exchange_order(seq_devs)
    parts = exchange(parts, order)
    params = (
        embed_weight,
        embed_bias[None, :],
        sine_freq[None, :],
        mid_weight,
        mid_bias[None, :],
        out_weight,
        decay_rate[None, :],
        skip_gain[None, :],
        short_taps,
    )
    shared = make_filter(params, own, seq_devs * local_len)
    mixed = mix(parts, shared)
    coded = exchange(mixed.reshape(seq_devs, own, -1), order).reshape(
        seq_devs * own, -1
    )[:channels]
    scale = jnp.concatenate([coded[:, local_len:]] * (local_len // LANES), axis=1)
    vals = decode_group(coded[:, :local_len], scale)
    return (out_gate.astype(F32) * vals).astype(BF16)


def solution(mesh):
    in_specs = (
        P("ch", "seq"),
        P("ch", "seq"),
        P("ch", "seq"),
        P("ch", None),
        P("ch"),
        P("ch"),
        P(),
        P(),
        P(),
        P(),
        P(),
        P(None, "ch"),
    )
    out_specs = P("ch", "seq")
    return jax.shard_map(
        on_device, mesh=mesh, in_specs=in_specs, out_specs=out_specs, check_vma=False
    )
```
